128 devices in a mesh: seq: 16 (over y_lo, x, core), tp: 8 (over z, y_hi).
Axes of the slice: x: 4, y: 4 (y_hi: 2, y_lo: 2; y = y_hi * 2 + y_lo), z: 4, core: 2. Of those that a mesh axis runs over, the one named last changes fastest.
Arguments:
- inputs: bfloat16 [16384, 4096], P('seq'), may hold values from -6 to 6
- w_query: bfloat16 [4096, 512], P(None, 'tp'), may hold values from -0.09375 to 0.09375
- w_key: bfloat16 [4096, 512], P(None, 'tp'), may hold values from -0.09375 to 0.09375
- w_value: bfloat16 [4096, 4096], P(None, 'tp'), may hold values from -0.09375 to 0.09375
- taps_query: float32 [3, 512], P(None, 'tp'), may hold values from -3 to 3
- taps_key: float32 [3, 512], P(None, 'tp'), may hold values from -3 to 3
- taps_value: float32 [3, 4096], P(None, 'tp'), may hold values from -3 to 3
- out_gain: float32 [4096], P('tp'), may hold values from 0.1 to 1.9
- out_grad: float32 [16384, 4096], P('seq', 'tp'), may hold values from -6 to 6
Outputs:
- outputs: float32 [16384, 4096], P('seq', 'tp')
- input_grad: bfloat16 [16384, 4096], P('seq', 'tp')
- grad_query: float32 [4096, 512], P('seq', 'tp')
- grad_key: float32 [4096, 512], P('seq', 'tp')
- grad_value: float32 [4096, 4096], P('seq', 'tp')
The draws below stay inside these ranges and needn't reach their ends.
All inputs are finite; a program needn't handle non-finite values.
Results may differ from the reference program's by a relative error of at most 0.0049.
Values may be sent and summed in bfloat16 or wider, within the bound.
No kernel may reach another device: no remote copies, remote signals or barrier semaphores. Data moves between devices by JAX's collectives and lax.ppermute only.
A program may use at most 192 MiB of HBM per device.

```python
import math
import jax
import jax.numpy as jnp
from jax import lax

D = 4096
HEADS = 32
FEAT = 16
HDIM = 128
TOK_DEV = 1024
TOKENS = 16384


def level_of(stream_key, dims, cuts, least, largest):
    def one(axis_at, parts):
        draws = jax.random.uniform(jax.random.fold_in(jax.random.fold_in(stream_key, 6), axis_at), (parts,), jnp.float32, least / len(cuts), largest / len(cuts))
        return jnp.repeat(jnp.exp(draws), dims[axis_at] // parts).reshape((-1,) + (1,) * (len(dims) - axis_at - 1))

    factor_of = one(*cuts[0])
    for cut in cuts[1:]:
        factor_of = factor_of * one(*cut)
    return factor_of


def normal_values(own_key, extent, width, most, cuts=(), kind=jnp.bfloat16):
    entries = jax.random.normal(own_key, extent, jnp.float32) * width
    if len(cuts) > 0:
        entries = level_of(own_key, extent, cuts, -0.22, 0.18) * entries
    return jnp.clip(entries, min=-most, max=most).astype(kind)


def setup_inputs(seed: int = 0) -> dict:
    key_list = jax.random.split(jax.random.key(seed), 10)
    inputs = normal_values(key_list[0], (TOKENS, D), 1.0, 6.0, ((0, 16),))
    w_query = normal_values(key_list[1], (D, HEADS * FEAT), D ** -0.5, 0.09375, ((1, 8),))
    w_key = normal_values(key_list[2], (D, HEADS * FEAT), D ** -0.5, 0.09375, ((1, 8),))
    w_value = normal_values(key_list[3], (D, HEADS * HDIM), D ** -0.5, 0.09375, ((1, 8),))
    taps_query = normal_values(key_list[4], (3, HEADS * FEAT), 1.0, 3.0, ((1, 8),), jnp.float32)
    taps_key = normal_values(key_list[5], (3, HEADS * FEAT), 1.0, 3.0, ((1, 8),), jnp.float32)
    taps_value = normal_values(key_list[6], (3, HEADS * HDIM), 1.0, 3.0, ((1, 8),), jnp.float32)
    out_gain = jnp.clip(1.0 + 0.18 * jax.random.normal(key_list[7], (HEADS * HDIM,), jnp.float32), 0.1, 1.9)
    out_grad = normal_values(key_list[8], (TOKENS, HEADS * HDIM), 1.0, 6.0, ((0, 16), (1, 8)), jnp.float32)
    return dict(inputs=inputs, w_query=w_query, w_key=w_key, w_value=w_value, taps_query=taps_query, taps_key=taps_key, taps_value=taps_value, out_gain=out_gain, out_grad=out_grad)


HIGHEST = lax.Precision.HIGHEST
ROOT_HALF = 1.0 / math.sqrt(2.0)
epsilon = 1e-05

def conv_taps(proj, tail, taps):
    length = proj.shape[0]
    extended = jnp.concatenate([tail, proj], axis=0)
    return taps[0] * extended[2:] + taps[1] * extended[1:length + 1] + taps[2] * extended[:length]

def features(conv_q, conv_k, conv_v, heads):
    length = conv_q.shape[0]
    query_one = conv_q.reshape(length, heads, FEAT) * 0.5
    key_one = conv_k.reshape(length, heads, FEAT) * 0.5
    query_two = (query_one[:, :, :, None] * query_one[:, :, None, :]).reshape(length, heads, FEAT * FEAT) * ROOT_HALF
    key_two = (key_one[:, :, :, None] * key_one[:, :, None, :]).reshape(length, heads, FEAT * FEAT) * ROOT_HALF
    values = conv_v.reshape(length, heads, HDIM)
    return (query_one, query_two, key_one, key_two, values)

def attend(query_one, query_two, key_one, key_two, values, state):
    state_zero, state_one, state_two = state
    length = query_one.shape[0]
    carried = state_zero[None] + jnp.einsum('thf,hfd->thd', query_one, state_one, precision=HIGHEST)
    carried = carried + jnp.einsum('the,hed->thd', query_two, state_two, precision=HIGHEST)
    score = jnp.einsum('thf,uhf->htu', query_one, key_one, precision=HIGHEST)
    kernel = 1.0 + score + 0.5 * score * score
    causal = jnp.tril(jnp.ones((length, length), dtype=bool))
    kernel = jnp.where(causal[None], kernel, 0.0)
    inner = jnp.einsum('htu,uhd->thd', kernel, values, precision=HIGHEST)
    return carried + inner

def contrib(key_one, key_two, values):
    return (lax.optimization_barrier(jnp.sum(values, axis=0)), jnp.einsum('uhf,uhd->hfd', key_one, values, precision=HIGHEST), jnp.einsum('uhe,uhd->hed', key_two, values, precision=HIGHEST))

def finish(numer, out_gain):
    heads = numer.shape[1]
    meansq = lax.optimization_barrier(jnp.mean(numer * numer, axis=-1, keepdims=True))
    scaled = numer * lax.rsqrt(meansq + epsilon) * out_gain.reshape(heads, HDIM)
    return scaled.reshape(numer.shape[0], heads * HDIM)

def reference(inputs, w_query, w_key, w_value, taps_query, taps_key, taps_value, out_gain, out_grad):
    proj_q = jnp.dot(inputs, w_query, preferred_element_type=jnp.float32)
    proj_k = jnp.dot(inputs, w_key, preferred_element_type=jnp.float32)
    proj_v = jnp.dot(inputs, w_value, preferred_element_type=jnp.float32)

    def heads_part(proj_q, proj_k, proj_v):
        conv_q = conv_taps(proj_q, jnp.zeros((2, proj_q.shape[1]), jnp.float32), taps_query)
        conv_k = conv_taps(proj_k, jnp.zeros((2, proj_k.shape[1]), jnp.float32), taps_key)
        conv_v = conv_taps(proj_v, jnp.zeros((2, proj_v.shape[1]), jnp.float32), taps_value)
        blocks = conv_q.shape[0] // TOK_DEV

        def split(array):
            return array.reshape(blocks, TOK_DEV, array.shape[1])

        @jax.checkpoint
        def advance(state, pieces):
            block_q, block_k, block_v = pieces
            query_one, query_two, key_one, key_two, values = features(block_q, block_k, block_v, HEADS)
            result = finish(attend(query_one, query_two, key_one, key_two, values, state), out_gain)
            own = contrib(key_one, key_two, values)
            return (tuple((a + b for a, b in zip(state, own))), result)
        start_state = (jnp.zeros((HEADS, HDIM), jnp.float32), jnp.zeros((HEADS, FEAT, HDIM), jnp.float32), jnp.zeros((HEADS, FEAT * FEAT, HDIM), jnp.float32))
        final_state, results = lax.scan(advance, start_state, (split(conv_q), split(conv_k), split(conv_v)))
        return results.reshape(blocks * TOK_DEV, HEADS * HDIM)
    outputs, pullback = jax.vjp(heads_part, proj_q, proj_k, proj_v)
    grad_pq, grad_pk, grad_pv = pullback(out_grad)
    round_q = grad_pq.astype(jnp.bfloat16)
    round_k = grad_pk.astype(jnp.bfloat16)
    round_v = grad_pv.astype(jnp.bfloat16)
    input_grad = (jnp.dot(round_q, w_query.T, preferred_element_type=jnp.float32) + jnp.dot(round_k, w_key.T, preferred_element_type=jnp.float32) + jnp.dot(round_v, w_value.T, preferred_element_type=jnp.float32)).astype(jnp.bfloat16)
    grad_query = jnp.dot(inputs.T, round_q, preferred_element_type=jnp.float32)
    grad_key = jnp.dot(inputs.T, round_k, preferred_element_type=jnp.float32)
    grad_value = jnp.dot(inputs.T, round_v, preferred_element_type=jnp.float32)
    return (outputs, input_grad, grad_query, grad_key, grad_value)
```

```python
import functools

import jax
import jax.numpy as jnp
import numpy as np
from jax import lax
from jax.experimental import pallas as pl
from jax.experimental.pallas import tpu as pltpu
from jax.sharding import PartitionSpec as P

FEAT = 16
HDIM = 128
HEADS = 4
CHUNK = 256
LEN = 1024
CHUNKS = LEN // CHUNK
NF = 160
WIDE = 256
EPS = 1e-05
F32, BF16 = jnp.float32, jnp.bfloat16


def feature_matrices():
    pairs = [(i, j) for i in range(FEAT) for j in range(i, FEAT)]
    pick = np.zeros((2, HEADS, 64, 2 * WIDE), np.float32)
    bias = np.zeros((1, 2 * WIDE), np.float32)
    for head in range(HEADS):
        base = head * FEAT
        for f, (i, j) in enumerate(pairs):
            pick[:, head, base + i, f] = 1.0
            pick[0, head, base + j, WIDE + f] = 0.5 if i == j else 1.0
            pick[1, head, base + j, WIDE + f] = 1.0
        for i in range(FEAT):
            pick[:, head, base + i, len(pairs) + i] = 1.0
    ones = len(pairs) + FEAT
    bias[0, ones] = 1.0
    bias[0, WIDE + len(pairs) : WIDE + ones + 1] = 1.0
    packed = np.zeros((2, HEADS, WIDE, 2 * WIDE), np.float32)
    packed[0, :, 0:64] = pick[0]
    packed[0, :, 64:128] = pick[0]
    packed[1, :, 0:64] = pick[1]
    packed[1, :, 128:192] = pick[1]
    back = np.zeros((2, HEADS, 2 * WIDE, 128), np.float32)
    back[:, :, :, 0:64] = pick.transpose(0, 1, 3, 2)
    return packed, bias, back


def nn(a, b):
    return lax.dot_general(a, b, (((1,), (0,)), ((), ())), preferred_element_type=F32)


def nt(a, b):
    return lax.dot_general(a, b, (((1,), (1,)), ((), ())), preferred_element_type=F32)


def halves(x):
    hi = x.astype(BF16)
    return hi, (x - hi.astype(F32)).astype(BF16)


def side(*parts):
    return jnp.concatenate(parts, axis=1)


def nn3(a_hi, a_lo, b_hi, b_lo):
    both = nn(a_hi, side(b_hi, b_lo))
    n = b_hi.shape[1]
    return both[:, :n] + both[:, n:] + nn(a_lo, b_hi)


def nt3(a_hi, a_lo, b_hi, b_lo):
    return nt(side(a_hi, a_lo), side(b_hi, b_hi)) + nt(a_hi, b_lo)


def factors(packed, pick, bias):
    both = nn(packed, pick) + bias
    return both[:, :WIDE], both[:, WIDE:]


def padded(state):
    return jnp.concatenate([state, jnp.zeros((WIDE - NF, HDIM), F32)], axis=0)


def head_mask(width, head):
    lane = lax.broadcasted_iota(jnp.int32, (1, width), 1)
    return (lane % 64) // FEAT == head


def cols(head):
    return slice(head * HDIM, (head + 1) * HDIM)


def call(body, grid, ins, outs, shapes, args, scratch=(), prefetch=0, flops=0, moved=0):
    return pl.pallas_call(
        body,
        grid_spec=pltpu.PrefetchScalarGridSpec(
            num_scalar_prefetch=prefetch, grid=grid, in_specs=ins, out_specs=outs, scratch_shapes=list(scratch)
        ),
        out_shape=shapes,
        compiler_params=pltpu.CompilerParams(vmem_limit_bytes=56 * 2**20),
        cost_estimate=pl.CostEstimate(flops=int(flops), bytes_accessed=int(moved), transcendentals=0),
    )(*args)


def full(*shape):
    return pl.BlockSpec(shape, lambda *_: (0,) * len(shape))


def arr(shape, dtype=F32):
    return jax.ShapeDtypeStruct(shape, dtype)


def project_kernel(x_ref, wq_ref, wk_ref, wv_ref, qk_ref, v_ref, wqk):
    @pl.when(pl.program_id(0) == 0)
    def _():
        wqk[0:64] = wq_ref[...]
        wqk[64:128] = wk_ref[...]

    x = x_ref[...]
    qk_ref[...] = nt(x, wqk[...])
    v_ref[...] = nn(x, wv_ref[...])


def project(x, wq_t, wk_t, wv):
    depth = x.shape[1]
    rows = lambda c: (c, 0)
    return call(
        project_kernel,
        (CHUNKS,),
        [pl.BlockSpec((CHUNK, depth), rows), full(64, depth), full(64, depth), full(depth, 512)],
        [pl.BlockSpec((CHUNK, 128), rows), pl.BlockSpec((CHUNK, 512), rows)],
        [arr((LEN, 128)), arr((LEN, 512))],
        (x, wq_t, wk_t, wv),
        [pltpu.VMEM((128, depth), BF16)],
        flops=2 * LEN * depth * 640,
        moved=14e6,
    )


def conv(x, tail, taps):
    row = lax.broadcasted_iota(jnp.int32, (8, 1), 0)
    once, twice = pltpu.roll(x, 1, 0), pltpu.roll(x, 2, 0)
    top1 = jnp.where(row == 0, tail[7:8], once[0:8])
    top2 = jnp.where(row == 0, tail[6:7], jnp.where(row == 1, tail[7:8], twice[0:8]))
    once = jnp.concatenate([top1, once[8:]], axis=0)
    twice = jnp.concatenate([top2, twice[8:]], axis=0)
    return taps[0:1] * x + taps[1:2] * once + taps[2:3] * twice


def state_kernel(
    qk_ref, v_ref, qkp_ref, vp_ref, t_ref, wq_ref, wk_ref, wv_ref, tqk_ref, tv_ref, pick_ref, biast_ref,
    ql_ref, kr_ref, vh_ref, vl_ref, sp_ref, st_ref, tail_qk, tail_v,
):
    c = pl.program_id(0)

    @pl.when(c == 0)
    def _():
        t = t_ref[...]
        tail_qk[...] = nt(t, jnp.concatenate([wq_ref[...], wk_ref[...]], axis=0))[8:16]
        tail_v[...] = nn(t, wv_ref[...])[8:16]
        st_ref[...] = jnp.zeros_like(st_ref)

    @pl.when(c > 0)
    def _():
        tail_qk[...] = qkp_ref[...]
        tail_v[...] = vp_ref[...]

    qk = conv(qk_ref[...], tail_qk[...], tqk_ref[...]) * 0.5
    v = conv(v_ref[...], tail_v[...], tv_ref[...])
    lane = lax.broadcasted_iota(jnp.int32, (1, 128), 1)
    low = lane < 64
    turned = pltpu.roll(qk, 64, 1)
    hi = qk.astype(BF16).astype(F32)
    lo = qk - hi
    turned_hi = turned.astype(BF16).astype(F32)
    turned_lo = turned - turned_hi
    zero = jnp.zeros_like(qk)
    ql = side(jnp.where(low, hi, turned_lo), jnp.where(low, hi, zero)).astype(BF16)
    kr = side(jnp.where(low, turned_hi, hi), jnp.where(low, turned_lo, zero)).astype(BF16)
    ql_ref[...] = ql
    kr_ref[...] = kr
    v_hi, v_lo = halves(v)
    vh_ref[...] = v_hi
    vl_ref[...] = v_lo
    for head in range(HEADS):
        ab = nt(pick_ref[head], kr) + biast_ref[...]
        p_hi, p_lo = halves(ab[:NF] * ab[WIDE : WIDE + NF])
        own = nn3(p_hi, p_lo, v_hi[:, cols(head)], v_lo[:, cols(head)])
        sp_ref[0, head] = st_ref[head]
        st_ref[head] += own


def shard_state(qk, v, tail, wq_t, wk_t, wv, taps_qk, taps_v, pick_kt, bias_t):
    depth = tail.shape[1]
    rows = lambda c: (c, 0)
    before = lambda c: (jnp.maximum(c * (CHUNK // 8) - 1, 0), 0)
    return call(
        state_kernel,
        (CHUNKS,),
        [
            pl.BlockSpec((CHUNK, 128), rows),
            pl.BlockSpec((CHUNK, 512), rows),
            pl.BlockSpec((8, 128), before),
            pl.BlockSpec((8, 512), before),
            full(16, depth),
            full(64, depth),
            full(64, depth),
            full(depth, 512),
            full(3, 128),
            full(3, 512),
            full(HEADS, 2 * WIDE, WIDE),
            full(2 * WIDE, 1),
        ],
        [
            pl.BlockSpec((CHUNK, WIDE), rows),
            pl.BlockSpec((CHUNK, WIDE), rows),
            pl.BlockSpec((CHUNK, 512), rows),
            pl.BlockSpec((CHUNK, 512), rows),
            pl.BlockSpec((1, HEADS, NF, HDIM), lambda c: (c, 0, 0, 0)),
            full(HEADS, NF, HDIM),
        ],
        [
            arr((LEN, WIDE), BF16),
            arr((LEN, WIDE), BF16),
            arr((LEN, 512), BF16),
            arr((LEN, 512), BF16),
            arr((CHUNKS, HEADS, NF, HDIM)),
            arr((HEADS, NF, HDIM)),
        ],
        (qk, v, qk, v, tail, wq_t, wk_t, wv, taps_qk, taps_v, pick_kt, bias_t),
        [pltpu.VMEM((8, 128), F32), pltpu.VMEM((8, 512), F32)],
        flops=4e9,
        moved=15e6,
    )


def running_kernel(backward, x_ref, o_ref):
    count = x_ref.shape[0]
    order = range(count - 1, -1, -1) if backward else range(count)
    total = jnp.zeros(x_ref.shape[1:], F32)
    for i in order:
        o_ref[i] = total
        total = total + x_ref[i]


def carried_in(state, backward):
    count = lax.axis_size("seq")
    rows = HEADS * NF // count
    pieces = lax.all_to_all(state.reshape(count, rows, HDIM), "seq", 0, 0)
    shape = (count, rows, HDIM)
    sums = call(
        functools.partial(running_kernel, backward), (1,), [full(*shape)], full(*shape), arr(shape), (pieces,), moved=6e5
    )
    return lax.all_to_all(sums, "seq", 0, 0).reshape(HEADS, NF, HDIM)


def lower():
    row = lax.broadcasted_iota(jnp.int32, (CHUNK, CHUNK), 0)
    col = lax.broadcasted_iota(jnp.int32, (CHUNK, CHUNK), 1)
    return row >= col


def inner_kernel(ql_ref, kr_ref, vh_ref, vl_ref, num_ref):
    ql, kr = ql_ref[...], kr_ref[...]
    causal = lower()
    for head in range(HEADS):
        mine = jnp.where(head_mask(WIDE, head), ql, jnp.zeros_like(ql))
        s = nt(mine, kr)
        w_hi, w_lo = halves(jnp.where(causal, 1.0 + s + 0.5 * s * s, 0.0))
        num_ref[:, cols(head)] = nn3(w_hi, w_lo, vh_ref[:, cols(head)], vl_ref[:, cols(head)])


def inner(ql, kr, vh, vl):
    rows = lambda c: (c, 0)
    narrow, wide = pl.BlockSpec((CHUNK, WIDE), rows), pl.BlockSpec((CHUNK, 512), rows)
    return call(
        inner_kernel, (CHUNKS,), [narrow, narrow, wide, wide], wide, arr((LEN, 512)), (ql, kr, vh, vl), flops=6e9, moved=6e6
    )


def forward_kernel(ql_ref, num_ref, sp_ref, se_ref, og_ref, gain_ref, pick_ref, pickt_ref, bias_ref, biast_ref,
                   out_ref, dh_ref, dl_ref, gs_ref, gt_ref):
    @pl.when(pl.program_id(0) == 0)
    def _():
        gt_ref[...] = jnp.zeros_like(gt_ref)

    ql = ql_ref[...]
    for head in range(HEADS):
        a, b = factors(ql, pick_ref[head], bias_ref[...])
        p_hi, p_lo = halves(a * b)
        s_hi, s_lo = halves(padded(sp_ref[0, head] + se_ref[head]))
        num = num_ref[:, cols(head)] + nn3(p_hi, p_lo, s_hi, s_lo)
        r = lax.rsqrt(jnp.mean(num * num, axis=-1, keepdims=True) + EPS)
        gain = gain_ref[:, cols(head)]
        unit = num * r
        out_ref[:, cols(head)] = unit * gain
        g = og_ref[:, cols(head)] * gain
        d = r * (g - unit * jnp.mean(g * unit, axis=-1, keepdims=True))
        d_hi, d_lo = halves(d)
        dh_ref[:, cols(head)] = d_hi
        dl_ref[:, cols(head)] = d_lo
        ab = nt(pickt_ref[head], ql) + biast_ref[...]
        pt_hi, pt_lo = halves(ab[:NF] * ab[WIDE : WIDE + NF])
        own = nn3(pt_hi, pt_lo, d_hi, d_lo)
        gs_ref[0, head] = own
        gt_ref[head] += own


def forward(ql, num, sp, se, og, gain, pick, pick_t, bias, bias_t):
    rows = lambda c: (c, 0)
    narrow, wide = pl.BlockSpec((CHUNK, WIDE), rows), pl.BlockSpec((CHUNK, 512), rows)
    states = pl.BlockSpec((1, HEADS, NF, HDIM), lambda c: (c, 0, 0, 0))
    return call(
        forward_kernel,
        (CHUNKS,),
        [
            narrow, wide, states, full(HEADS, NF, HDIM), wide, full(1, 512),
            full(HEADS, WIDE, 2 * WIDE), full(HEADS, 2 * WIDE, WIDE), full(1, 2 * WIDE), full(2 * WIDE, 1),
        ],
        [wide, wide, wide, states, full(HEADS, NF, HDIM)],
        [
            arr((LEN, 512)), arr((LEN, 512), BF16), arr((LEN, 512), BF16),
            arr((CHUNKS, HEADS, NF, HDIM)), arr((HEADS, NF, HDIM)),
        ],
        (ql, num, sp, se, og, gain, pick, pick_t, bias, bias_t),
        flops=8e9,
        moved=12e6,
    )


def backward_kernel(ql_ref, kr_ref, vh_ref, vl_ref, dh_ref, dl_ref, sp_ref, se_ref, pick_ref, bias_ref, back_ref,
                    gq_ref, gk_ref, gv_ref):
    ql, kr = ql_ref[...], kr_ref[...]
    row = lax.broadcasted_iota(jnp.int32, (CHUNK, CHUNK), 0)
    col = lax.broadcasted_iota(jnp.int32, (CHUNK, CHUNK), 1)
    gq = jnp.zeros((CHUNK, WIDE), F32)
    gk = jnp.zeros((CHUNK, WIDE), F32)
    du = jnp.zeros((CHUNK, 128), F32)
    for head in range(HEADS):
        mask = head_mask(WIDE, head)
        q = jnp.where(mask, ql, jnp.zeros_like(ql))
        k = jnp.where(mask, kr, jnp.zeros_like(kr))
        v_hi, v_lo = vh_ref[:, cols(head)], vl_ref[:, cols(head)]
        d_hi, d_lo = dh_ref[:, cols(head)], dl_ref[:, cols(head)]
        s = nt(q, kr)
        slope = jnp.where(row >= col, 1.0 + s, 0.0)
        ds_hi, ds_lo = halves(nt3(d_hi, d_lo, v_hi, v_lo) * slope)
        gq = gq + nn(ds_hi, k) + nn(ds_lo, k)
        st = nt(k, ql)
        slope = jnp.where(col >= row, 1.0 + st, 0.0)
        dst_hi, dst_lo = halves(nt3(v_hi, v_lo, d_hi, d_lo) * slope)
        gk = gk + nn(dst_hi, q) + nn(dst_lo, q)
        w_hi, w_lo = halves(jnp.where(col >= row, 1.0 + st + 0.5 * st * st, 0.0))
        gv_ref[:, cols(head)] = nn3(w_hi, w_lo, d_hi, d_lo)
        s_hi, s_lo = halves(padded(sp_ref[0, head] + se_ref[head]))
        dp = nt3(d_hi, d_lo, s_hi, s_lo)
        a, b = factors(ql, pick_ref[head], bias_ref[...])
        dab_hi, dab_lo = halves(side(dp * b, dp * a))
        du = du + nn(dab_hi, back_ref[head]) + nn(dab_lo, back_ref[head])
    gq_ref[...] = gq[:, :128] + gq[:, 128:] + du
    gk_ref[...] = gk[:, :128] + pltpu.roll(gk[:, :128], 64, 1)


def backward(ql, kr, vh, vl, dh, dl, sp, se, pick, bias, back):
    rows = lambda c: (c, 0)
    narrow, wide = pl.BlockSpec((CHUNK, WIDE), rows), pl.BlockSpec((CHUNK, 512), rows)
    half = pl.BlockSpec((CHUNK, 128), rows)
    states = pl.BlockSpec((1, HEADS, NF, HDIM), lambda c: (c, 0, 0, 0))
    return call(
        backward_kernel,
        (CHUNKS,),
        [
            narrow, narrow, wide, wide, wide, wide, states, full(HEADS, NF, HDIM),
            full(HEADS, WIDE, 2 * WIDE), full(1, 2 * WIDE), full(HEADS, 2 * WIDE, 128),
        ],
        [half, half, wide],
        [arr((LEN, 128)), arr((LEN, 128)), arr((LEN, 512))],
        (ql, kr, vh, vl, dh, dl, sp, se, pick, bias, back),
        flops=16e9,
        moved=12e6,
    )


def later_kernel(first, last, kr_ref, vh_ref, vl_ref, gs_ref, gl_ref, gq_ref, gk_ref, gv_ref, pick_ref, bias_ref,
                 back_ref, oqk_ref, ov_ref, total):
    @pl.when(pl.program_id(0) == 0)
    def _():
        begin = gl_ref[...]
        for c in range(CHUNKS - 1, last - 1, -1):
            begin = begin + gs_ref[c]
        total[...] = begin

    kr = kr_ref[...]
    du = jnp.zeros((CHUNK, 128), F32)
    for head in range(HEADS):
        a, b = factors(kr, pick_ref[head], bias_ref[...])
        p_hi, p_lo = halves(a * b)
        l_hi, l_lo = halves(padded(total[head]))
        v_hi, v_lo = vh_ref[:, cols(head)], vl_ref[:, cols(head)]
        ov_ref[:, cols(head)] = gv_ref[:, cols(head)] + nn3(p_hi, p_lo, l_hi, l_lo)
        dp = nt3(v_hi, v_lo, l_hi, l_lo)
        dab_hi, dab_lo = halves(side(dp * b, dp * a))
        du = du + nn(dab_hi, back_ref[head]) + nn(dab_lo, back_ref[head])
    low = lax.broadcasted_iota(jnp.int32, (1, 128), 1) < 64
    oqk_ref[...] = 0.5 * jnp.where(low, gq_ref[...], pltpu.roll(gk_ref[...] + du, 64, 1))
    total[...] += gs_ref[last - 1 - pl.program_id(0)]


def later(first, last, kr, vh, vl, gs, gl, gq, gk, gv, pick, bias, back):
    count = last - first
    rows = lambda c: (last - 1 - c, 0)
    to = lambda c: (count - 1 - c, 0)
    narrow, wide = pl.BlockSpec((CHUNK, WIDE), rows), pl.BlockSpec((CHUNK, 512), rows)
    half = pl.BlockSpec((CHUNK, 128), rows)
    return call(
        functools.partial(later_kernel, first, last),
        (count,),
        [
            narrow, wide, wide, full(CHUNKS, HEADS, NF, HDIM), full(HEADS, NF, HDIM), half, half, wide,
            full(HEADS, WIDE, 2 * WIDE), full(1, 2 * WIDE), full(HEADS, 2 * WIDE, 128),
        ],
        [pl.BlockSpec((CHUNK, 128), to), pl.BlockSpec((CHUNK, 512), to)],
        [arr((count * CHUNK, 128)), arr((count * CHUNK, 512))],
        (kr, vh, vl, gs, gl, gq, gk, gv, pick, bias, back),
        [pltpu.VMEM((HEADS, NF, HDIM), F32)],
        flops=2e9 * count,
        moved=3e6 * count,
    )


def conv_back(x, tail, taps):
    n = x.shape[0]
    row = lax.broadcasted_iota(jnp.int32, (8, 1), 0)
    once, twice = pltpu.roll(x, n - 1, 0), pltpu.roll(x, n - 2, 0)
    end1 = jnp.where(row == 7, tail[0:1], once[n - 8 :])
    end2 = jnp.where(row == 7, tail[1:2], jnp.where(row == 6, tail[0:1], twice[n - 8 :]))
    once = jnp.concatenate([once[: n - 8], end1], axis=0)
    twice = jnp.concatenate([twice[: n - 8], end2], axis=0)
    return (taps[0:1] * x + taps[1:2] * once + taps[2:3] * twice).astype(BF16)


def unconv_kernel(aqk_ref, av_ref, bqk_ref, bv_ref, hqk_ref, hv_ref, tqk_ref, tv_ref, dqk_ref, dv_ref, dt_ref):
    for a_ref, b_ref, h_ref, t_ref, d_ref, base in (
        (aqk_ref, bqk_ref, hqk_ref, tqk_ref, dqk_ref, 0),
        (av_ref, bv_ref, hv_ref, tv_ref, dv_ref, 128),
    ):
        n = a_ref.shape[0]
        for start in range(0, LEN, CHUNK):
            src = a_ref[start : start + CHUNK] if start < n else b_ref[start - n : start - n + CHUNK]
            end = start + CHUNK
            if end == LEN:
                tail = h_ref[...]
            else:
                tail = a_ref[end : end + 8] if end < n else b_ref[end - n : end - n + 8]
            got = conv_back(src, tail, t_ref[...])
            d_ref[start:end] = got
            dt_ref[base : base + got.shape[1], start:end] = got.T


def unconv(aqk, av, bqk, bv, hqk, hv, taps_qk, taps_v):
    n, m = aqk.shape[0], bqk.shape[0]
    return call(
        unconv_kernel,
        (1,),
        [full(n, 128), full(n, 512), full(m, 128), full(m, 512), full(8, 128), full(8, 512), full(3, 128), full(3, 512)],
        [full(LEN, 128), full(LEN, 512), full(640, LEN)],
        [arr((LEN, 128), BF16), arr((LEN, 512), BF16), arr((640, LEN), BF16)],
        (aqk, av, bqk, bv, hqk, hv, taps_qk, taps_v),
        moved=6e6,
    )


def input_kernel(dqk_ref, dv_ref, wq_ref, wk_ref, wv_ref, o_ref):
    w = jnp.concatenate([wq_ref[...], wk_ref[...]], axis=0)
    o_ref[0] = (nt(dv_ref[...], wv_ref[...]) + nn(dqk_ref[...], w)).astype(o_ref.dtype)


def input_blocks(dqk, dv, wq_t, wk_t, wv):
    parts = wv.shape[0] // 512
    at = lambda p: (0, p)
    return call(
        input_kernel,
        (parts,),
        [full(LEN, 128), full(LEN, 512), pl.BlockSpec((64, 512), at), pl.BlockSpec((64, 512), at),
         pl.BlockSpec((512, 512), lambda p: (p, 0))],
        pl.BlockSpec((1, LEN, 512), lambda p: (p, 0, 0)),
        arr((parts, LEN, 512), BF16),
        (dqk, dv, wq_t, wk_t, wv),
        flops=2 * LEN * 640 * 4096,
        moved=15e6,
    )


def weight_kernel(dt_ref, x_ref, o_ref):
    o_ref[0] = nn(dt_ref[...], x_ref[...]).astype(o_ref.dtype)


def weight_blocks(dt, x):
    parts = lax.axis_size("seq")
    width = x.shape[1] // parts
    return call(
        weight_kernel,
        (parts,),
        [full(640, LEN), pl.BlockSpec((LEN, width), lambda p: (0, p))],
        pl.BlockSpec((1, 640, width), lambda p: (p, 0, 0)),
        arr((parts, 640, width), BF16),
        (dt, x),
        flops=2 * LEN * 640 * 4096,
        moved=15e6,
    )


def along(x, by):
    n = lax.axis_size("seq")
    return lax.ppermute(x, "seq", [(i, i + by) for i in range(n) if 0 <= i + by < n])


def local(inputs, w_query, w_key, w_value, taps_query, taps_key, taps_value, out_gain, out_grad):
    packed, bias, back = feature_matrices()
    pick_q, pick_k = (jnp.asarray(packed[i], BF16) for i in range(2))
    pick_qt, pick_kt = (jnp.asarray(packed[i].transpose(0, 2, 1), BF16) for i in range(2))
    back_q, back_k = (jnp.asarray(back[i], BF16) for i in range(2))
    bias, bias_t = jnp.asarray(bias), jnp.asarray(bias.T)
    wq_t, wk_t = w_query.T, w_key.T
    taps_qk = jnp.concatenate([taps_query, taps_key], axis=1)

    tail = along(inputs[-16:], 1)
    proj_qk, proj_v = project(inputs, wq_t, wk_t, w_value)
    ql, kr, vh, vl, before, own = shard_state(
        proj_qk, proj_v, tail, wq_t, wk_t, w_value, taps_qk, taps_value, pick_kt, bias_t
    )
    earlier = carried_in(own, False)
    num = inner(ql, kr, vh, vl)
    outputs, dh, dl, grads, own_grad = forward(
        ql, num, before, earlier, out_grad, out_gain.reshape(1, 512), pick_q, pick_qt, bias, bias_t
    )
    after = carried_in(own_grad, True)
    gq, gk, gv = backward(ql, kr, vh, vl, dh, dl, before, earlier, pick_q, bias, back_q)
    rest = (kr, vh, vl, grads, after, gq, gk, gv, pick_k, bias, back_k)
    aqk, av = later(0, 1, *rest)
    hqk, hv = along(aqk[:8], -1), along(av[:8], -1)
    bqk, bv = later(1, CHUNKS, *rest)
    dqk, dv, dt = unconv(aqk, av, bqk, bv, hqk, hv, taps_qk, taps_value)
    blocks = lax.all_to_all(input_blocks(dqk, dv, wq_t, wk_t, w_value), "tp", 0, 0)
    input_grad = jnp.sum(blocks.astype(F32), axis=0).astype(BF16)
    pieces = lax.all_to_all(weight_blocks(dt, inputs), "seq", 0, 0)
    summed = jnp.sum(pieces.astype(F32), axis=0)
    return (outputs, input_grad, summed[0:64].T, summed[64:128].T, summed[128:].T)


def solution(mesh):
    return jax.shard_map(
        local,
        mesh=mesh,
        in_specs=(
            P("seq", None),
            P(None, "tp"),
            P(None, "tp"),
            P(None, "tp"),
            P(None, "tp"),
            P(None, "tp"),
            P(None, "tp"),
            P("tp"),
            P("seq", "tp"),
        ),
        out_specs=(P("seq", "tp"), P("seq", "tp"), P("seq", "tp"), P("seq", "tp"), P("seq", "tp")),
        check_vma=False,
    )
```

```python
import functools

import jax
import jax.numpy as jnp
import numpy as np
from jax import lax
from jax.experimental import pallas as pl
from jax.experimental.pallas import tpu as pltpu
from jax.sharding import PartitionSpec as P

FEAT = 16
HDIM = 128
HEADS = 4
CHUNK = 256
LEN = 1024
CHUNKS = LEN // CHUNK
NF = 160
WIDE = 256
EPS = 1e-05
STEP = 128
F32, BF16 = jnp.float32, jnp.bfloat16


def feature_matrices():
    pairs = [(i, j) for i in range(FEAT) for j in range(i, FEAT)]
    pick = np.zeros((2, HEADS, 64, 2 * WIDE), np.float32)
    bias = np.zeros((1, 2 * WIDE), np.float32)
    for head in range(HEADS):
        base = head * FEAT
        for f, (i, j) in enumerate(pairs):
            pick[:, head, base + i, f] = 1.0
            pick[0, head, base + j, WIDE + f] = 0.5 if i == j else 1.0
            pick[1, head, base + j, WIDE + f] = 1.0
        for i in range(FEAT):
            pick[:, head, base + i, len(pairs) + i] = 1.0
    ones = len(pairs) + FEAT
    bias[0, ones] = 1.0
    bias[0, WIDE + len(pairs) : WIDE + ones + 1] = 1.0
    packed = np.zeros((2, HEADS, WIDE, 2 * WIDE), np.float32)
    packed[0, :, 0:64] = pick[0]
    packed[0, :, 64:128] = pick[0]
    packed[1, :, 0:64] = pick[1]
    packed[1, :, 128:192] = pick[1]
    back = np.zeros((2, HEADS, 2 * WIDE, 128), np.float32)
    back[:, :, :, 0:64] = pick.transpose(0, 1, 3, 2)
    return packed, bias, back


def nn(a, b):
    return lax.dot_general(a, b, (((1,), (0,)), ((), ())), preferred_element_type=F32)


def nt(a, b):
    return lax.dot_general(a, b, (((1,), (1,)), ((), ())), preferred_element_type=F32)


def halves(x):
    hi = x.astype(BF16)
    return hi, (x - hi.astype(F32)).astype(BF16)


def side(*parts):
    return jnp.concatenate(parts, axis=1)


def nn3(a_hi, a_lo, b_hi, b_lo):
    both = nn(a_hi, side(b_hi, b_lo))
    n = b_hi.shape[1]
    return both[:, :n] + both[:, n:] + nn(a_lo, b_hi)


def nt3(a_hi, a_lo, b_hi, b_lo):
    return nt(side(a_hi, a_lo), side(b_hi, b_hi)) + nt(a_hi, b_lo)


def factors(packed, pick, bias):
    both = nn(packed, pick) + bias
    return both[:, :WIDE], both[:, WIDE:]


def padded(state):
    return jnp.concatenate([state, jnp.zeros((WIDE - NF, HDIM), F32)], axis=0)


def head_mask(width, head):
    lane = lax.broadcasted_iota(jnp.int32, (1, width), 1)
    return (lane % 64) // FEAT == head


def cols(head):
    return slice(head * HDIM, (head + 1) * HDIM)


def call(body, grid, ins, outs, shapes, args, scratch=(), prefetch=0, flops=0, moved=0, after=()):
    if after:
        kept, skip = body, len(after)
        at = prefetch + len(ins)
        body = lambda *refs: kept(*refs[:at], *refs[at + skip :])
        ins = [*ins] + [pl.BlockSpec(memory_space=pl.ANY)] * skip
        args = (*args, *after)
    return pl.pallas_call(
        body,
        grid_spec=pltpu.PrefetchScalarGridSpec(
            num_scalar_prefetch=prefetch, grid=grid, in_specs=ins, out_specs=outs, scratch_shapes=list(scratch)
        ),
        out_shape=shapes,
        compiler_params=pltpu.CompilerParams(vmem_limit_bytes=56 * 2**20),
        cost_estimate=pl.CostEstimate(flops=int(flops), bytes_accessed=int(moved), transcendentals=0),
    )(*args)


def full(*shape):
    return pl.BlockSpec(shape, lambda *_: (0,) * len(shape))


def arr(shape, dtype=F32):
    return jax.ShapeDtypeStruct(shape, dtype)


def project_kernel(x_ref, wq_ref, wk_ref, wv_ref, qk_ref, v_ref, wqk):
    @pl.when(pl.program_id(0) == 0)
    def _():
        wqk[0:64] = wq_ref[...]
        wqk[64:128] = wk_ref[...]

    x = x_ref[...]
    qk_ref[...] = nt(x, wqk[...])
    v_ref[...] = nn(x, wv_ref[...])


def project(x, wq_t, wk_t, wv):
    depth = x.shape[1]
    rows = lambda c: (c, 0)
    return call(
        project_kernel,
        (CHUNKS,),
        [pl.BlockSpec((CHUNK, depth), rows), full(64, depth), full(64, depth), full(depth, 512)],
        [pl.BlockSpec((CHUNK, 128), rows), pl.BlockSpec((CHUNK, 512), rows), full(128, depth)],
        [arr((LEN, 128)), arr((LEN, 512)), arr((128, depth), BF16)],
        (x, wq_t, wk_t, wv),
        flops=2 * LEN * depth * 640,
        moved=14e6,
    )


def conv(x, tail, taps):
    row = lax.broadcasted_iota(jnp.int32, (8, 1), 0)
    once, twice = pltpu.roll(x, 1, 0), pltpu.roll(x, 2, 0)
    top1 = jnp.where(row == 0, tail[7:8], once[0:8])
    top2 = jnp.where(row == 0, tail[6:7], jnp.where(row == 1, tail[7:8], twice[0:8]))
    once = jnp.concatenate([top1, once[8:]], axis=0)
    twice = jnp.concatenate([top2, twice[8:]], axis=0)
    return taps[0:1] * x + taps[1:2] * once + taps[2:3] * twice


def state_kernel(
    qk_ref, v_ref, qkp_ref, vp_ref, t_ref, wqk_ref, wv_ref, tqk_ref, tv_ref, pick_ref, biast_ref,
    ql_ref, kr_ref, vh_ref, vl_ref, sp_ref, st_ref, tail_qk, tail_v,
):
    c = pl.program_id(0)

    @pl.when(c == 0)
    def _():
        t = t_ref[...]
        tail_qk[...] = nt(t, wqk_ref[...])[8:16]
        tail_v[...] = nn(t, wv_ref[...])[8:16]
        st_ref[...] = jnp.zeros_like(st_ref)

    @pl.when(c > 0)
    def _():
        tail_qk[...] = qkp_ref[...]
        tail_v[...] = vp_ref[...]

    qk = conv(qk_ref[...], tail_qk[...], tqk_ref[...]) * 0.5
    v = conv(v_ref[...], tail_v[...], tv_ref[...])
    lane = lax.broadcasted_iota(jnp.int32, (1, 128), 1)
    low = lane < 64
    turned = pltpu.roll(qk, 64, 1)
    hi = qk.astype(BF16).astype(F32)
    lo = qk - hi
    turned_hi = turned.astype(BF16).astype(F32)
    turned_lo = turned - turned_hi
    zero = jnp.zeros_like(qk)
    ql = side(jnp.where(low, hi, turned_lo), jnp.where(low, hi, zero)).astype(BF16)
    kr = side(jnp.where(low, turned_hi, hi), jnp.where(low, turned_lo, zero)).astype(BF16)
    ql_ref[...] = ql
    kr_ref[...] = kr
    v_hi, v_lo = halves(v)
    vh_ref[...] = v_hi
    vl_ref[...] = v_lo
    for head in range(HEADS):
        ab = nt(pick_ref[head], kr) + biast_ref[...]
        p_hi, p_lo = halves(ab[:NF] * ab[WIDE : WIDE + NF])
        own = nn3(p_hi, p_lo, v_hi[:, cols(head)], v_lo[:, cols(head)])
        sp_ref[0, head] = st_ref[head]
        st_ref[head] += own


def shard_state(qk, v, tail, wqk_t, wv, taps_qk, taps_v, pick_kt, bias_t):
    depth = tail.shape[1]
    rows = lambda c: (c, 0)
    before = lambda c: (jnp.maximum(c * (CHUNK // 8) - 1, 0), 0)
    return call(
        state_kernel,
        (CHUNKS,),
        [
            pl.BlockSpec((CHUNK, 128), rows),
            pl.BlockSpec((CHUNK, 512), rows),
            pl.BlockSpec((8, 128), before),
            pl.BlockSpec((8, 512), before),
            full(16, depth),
            full(128, depth),
            full(depth, 512),
            full(3, 128),
            full(3, 512),
            full(HEADS, 2 * WIDE, WIDE),
            full(2 * WIDE, 1),
        ],
        [
            pl.BlockSpec((CHUNK, WIDE), rows),
            pl.BlockSpec((CHUNK, WIDE), rows),
            pl.BlockSpec((CHUNK, 512), rows),
            pl.BlockSpec((CHUNK, 512), rows),
            pl.BlockSpec((1, HEADS, NF, HDIM), lambda c: (c, 0, 0, 0)),
            full(HEADS, NF, HDIM),
        ],
        [
            arr((LEN, WIDE), BF16),
            arr((LEN, WIDE), BF16),
            arr((LEN, 512), BF16),
            arr((LEN, 512), BF16),
            arr((CHUNKS, HEADS, NF, HDIM)),
            arr((HEADS, NF, HDIM)),
        ],
        (qk, v, qk, v, tail, wqk_t, wv, taps_qk, taps_v, pick_kt, bias_t),
        [pltpu.VMEM((8, 128), F32), pltpu.VMEM((8, 512), F32)],
        flops=4e9,
        moved=15e6,
    )


def running_kernel(backward, x_ref, o_ref):
    count = x_ref.shape[0]
    order = range(count - 1, -1, -1) if backward else range(count)
    total = jnp.zeros(x_ref.shape[1:], F32)
    for i in order:
        o_ref[i] = total
        total = total + x_ref[i]


def carried_in(state, backward):
    count = lax.axis_size("seq")
    rows = HEADS * NF // count
    pieces = lax.all_to_all(state.reshape(count, rows, HDIM), "seq", 0, 0)
    shape = (count, rows, HDIM)
    sums = call(
        functools.partial(running_kernel, backward), (1,), [full(*shape)], full(*shape), arr(shape), (pieces,), moved=6e5
    )
    return lax.all_to_all(sums, "seq", 0, 0).reshape(HEADS, NF, HDIM)


def lower():
    row = lax.broadcasted_iota(jnp.int32, (CHUNK, CHUNK), 0)
    col = lax.broadcasted_iota(jnp.int32, (CHUNK, CHUNK), 1)
    return row >= col


def inner_kernel(ql_ref, kr_ref, vh_ref, vl_ref, num_ref):
    ql, kr = ql_ref[...], kr_ref[...]
    causal = lower()
    for head in range(HEADS):
        mine = jnp.where(head_mask(WIDE, head), ql, jnp.zeros_like(ql))
        s = nt(mine, kr)
        w_hi, w_lo = halves(jnp.where(causal, 1.0 + s + 0.5 * s * s, 0.0))
        num_ref[:, cols(head)] = nn3(w_hi, w_lo, vh_ref[:, cols(head)], vl_ref[:, cols(head)])


def inner(ql, kr, vh, vl):
    rows = lambda c: (c, 0)
    narrow, wide = pl.BlockSpec((CHUNK, WIDE), rows), pl.BlockSpec((CHUNK, 512), rows)
    return call(
        inner_kernel, (CHUNKS,), [narrow, narrow, wide, wide], wide, arr((LEN, 512)), (ql, kr, vh, vl), flops=6e9, moved=6e6
    )


def forward_kernel(ql_ref, num_ref, sp_ref, se_ref, og_ref, gain_ref, pick_ref, pickt_ref, bias_ref, biast_ref,
                   out_ref, dh_ref, dl_ref, gs_ref, gt_ref):
    @pl.when(pl.program_id(0) == 0)
    def _():
        gt_ref[...] = jnp.zeros_like(gt_ref)

    ql = ql_ref[...]
    for head in range(HEADS):
        a, b = factors(ql, pick_ref[head], bias_ref[...])
        p_hi, p_lo = halves(a * b)
        s_hi, s_lo = halves(padded(sp_ref[0, head] + se_ref[head]))
        num = num_ref[:, cols(head)] + nn3(p_hi, p_lo, s_hi, s_lo)
        r = lax.rsqrt(jnp.mean(num * num, axis=-1, keepdims=True) + EPS)
        gain = gain_ref[:, cols(head)]
        unit = num * r
        out_ref[:, cols(head)] = unit * gain
        g = og_ref[:, cols(head)] * gain
        d = r * (g - unit * jnp.mean(g * unit, axis=-1, keepdims=True))
        d_hi, d_lo = halves(d)
        dh_ref[:, cols(head)] = d_hi
        dl_ref[:, cols(head)] = d_lo
        ab = nt(pickt_ref[head], ql) + biast_ref[...]
        pt_hi, pt_lo = halves(ab[:NF] * ab[WIDE : WIDE + NF])
        own = nn3(pt_hi, pt_lo, d_hi, d_lo)
        gs_ref[0, head] = own
        gt_ref[head] += own


def forward(ql, num, sp, se, og, gain, pick, pick_t, bias, bias_t):
    rows = lambda c: (c, 0)
    narrow, wide = pl.BlockSpec((CHUNK, WIDE), rows), pl.BlockSpec((CHUNK, 512), rows)
    states = pl.BlockSpec((1, HEADS, NF, HDIM), lambda c: (c, 0, 0, 0))
    return call(
        forward_kernel,
        (CHUNKS,),
        [
            narrow, wide, states, full(HEADS, NF, HDIM), wide, full(1, 512),
            full(HEADS, WIDE, 2 * WIDE), full(HEADS, 2 * WIDE, WIDE), full(1, 2 * WIDE), full(2 * WIDE, 1),
        ],
        [wide, wide, wide, states, full(HEADS, NF, HDIM)],
        [
            arr((LEN, 512)), arr((LEN, 512), BF16), arr((LEN, 512), BF16),
            arr((CHUNKS, HEADS, NF, HDIM)), arr((HEADS, NF, HDIM)),
        ],
        (ql, num, sp, se, og, gain, pick, pick_t, bias, bias_t),
        flops=8e9,
        moved=12e6,
    )


def query_kernel(ql_ref, kr_ref, vh_ref, vl_ref, dh_ref, dl_ref, sp_ref, se_ref, pick_ref, bias_ref, back_ref, gq_ref):
    ql, kr = ql_ref[...], kr_ref[...]
    causal = lower()
    gq = jnp.zeros((CHUNK, WIDE), F32)
    du = jnp.zeros((CHUNK, 128), F32)
    for head in range(HEADS):
        mask = head_mask(WIDE, head)
        q = jnp.where(mask, ql, jnp.zeros_like(ql))
        k = jnp.where(mask, kr, jnp.zeros_like(kr))
        v_hi, v_lo = vh_ref[:, cols(head)], vl_ref[:, cols(head)]
        d_hi, d_lo = dh_ref[:, cols(head)], dl_ref[:, cols(head)]
        slope = jnp.where(causal, 1.0 + nt(q, kr), 0.0)
        ds_hi, ds_lo = halves(nt3(d_hi, d_lo, v_hi, v_lo) * slope)
        gq = gq + nn(ds_hi, k) + nn(ds_lo, k)
        s_hi, s_lo = halves(padded(sp_ref[0, head] + se_ref[head]))
        dp = nt3(d_hi, d_lo, s_hi, s_lo)
        a, b = factors(ql, pick_ref[head], bias_ref[...])
        dab_hi, dab_lo = halves(side(dp * b, dp * a))
        du = du + nn(dab_hi, back_ref[head]) + nn(dab_lo, back_ref[head])
    gq_ref[...] = gq[:, :128] + gq[:, 128:] + du


def key_kernel(ql_ref, kr_ref, vh_ref, vl_ref, dh_ref, dl_ref, gk_ref, gv_ref):
    ql, kr = ql_ref[...], kr_ref[...]
    row = lax.broadcasted_iota(jnp.int32, (CHUNK, CHUNK), 0)
    col = lax.broadcasted_iota(jnp.int32, (CHUNK, CHUNK), 1)
    causal = col >= row
    gk = jnp.zeros((CHUNK, WIDE), F32)
    for head in range(HEADS):
        mask = head_mask(WIDE, head)
        q = jnp.where(mask, ql, jnp.zeros_like(ql))
        k = jnp.where(mask, kr, jnp.zeros_like(kr))
        v_hi, v_lo = vh_ref[:, cols(head)], vl_ref[:, cols(head)]
        d_hi, d_lo = dh_ref[:, cols(head)], dl_ref[:, cols(head)]
        s = nt(k, ql)
        ds_hi, ds_lo = halves(nt3(v_hi, v_lo, d_hi, d_lo) * jnp.where(causal, 1.0 + s, 0.0))
        gk = gk + nn(ds_hi, q) + nn(ds_lo, q)
        w_hi, w_lo = halves(jnp.where(causal, 1.0 + s + 0.5 * s * s, 0.0))
        gv_ref[:, cols(head)] = nn3(w_hi, w_lo, d_hi, d_lo)
    gk_ref[...] = gk[:, :128] + pltpu.roll(gk[:, :128], 64, 1)


def backward(ql, kr, vh, vl, dh, dl, sp, se, pick, bias, back):
    rows = lambda c: (c, 0)
    narrow, wide = pl.BlockSpec((CHUNK, WIDE), rows), pl.BlockSpec((CHUNK, 512), rows)
    half = pl.BlockSpec((CHUNK, 128), rows)
    states = pl.BlockSpec((1, HEADS, NF, HDIM), lambda c: (c, 0, 0, 0))
    gk, gv = call(
        key_kernel,
        (CHUNKS,),
        [narrow, narrow, wide, wide, wide, wide],
        [half, wide],
        [arr((LEN, 128)), arr((LEN, 512))],
        (ql, kr, vh, vl, dh, dl),
        flops=8e9,
        moved=8e6,
    )
    gq = call(
        query_kernel,
        (CHUNKS,),
        [
            narrow, narrow, wide, wide, wide, wide, states, full(HEADS, NF, HDIM),
            full(HEADS, WIDE, 2 * WIDE), full(1, 2 * WIDE), full(HEADS, 2 * WIDE, 128),
        ],
        half,
        arr((LEN, 128)),
        (ql, kr, vh, vl, dh, dl, sp, se, pick, bias, back),
        flops=8e9,
        moved=8e6,
    )
    return gq, gk, gv


def later_kernel(first, last, kr_ref, vh_ref, vl_ref, gs_ref, gl_ref, gq_ref, gk_ref, gv_ref, pick_ref, bias_ref,
                 back_ref, o_ref, total):
    @pl.when(pl.program_id(0) == 0)
    def _():
        begin = gl_ref[...]
        for c in range(CHUNKS - 1, last - 1, -1):
            begin = begin + gs_ref[c]
        total[...] = begin

    kr = kr_ref[...]
    du = jnp.zeros((CHUNK, 128), F32)
    for head in range(HEADS):
        a, b = factors(kr, pick_ref[head], bias_ref[...])
        p_hi, p_lo = halves(a * b)
        l_hi, l_lo = halves(padded(total[head]))
        v_hi, v_lo = vh_ref[:, cols(head)], vl_ref[:, cols(head)]
        o_ref[:, 128 + head * HDIM : 256 + head * HDIM] = gv_ref[:, cols(head)] + nn3(p_hi, p_lo, l_hi, l_lo)
        dp = nt3(v_hi, v_lo, l_hi, l_lo)
        dab_hi, dab_lo = halves(side(dp * b, dp * a))
        du = du + nn(dab_hi, back_ref[head]) + nn(dab_lo, back_ref[head])
    low = lax.broadcasted_iota(jnp.int32, (1, 128), 1) < 64
    o_ref[:, :128] = 0.5 * jnp.where(low, gq_ref[...], pltpu.roll(gk_ref[...] + du, 64, 1))
    total[...] += gs_ref[last - 1 - pl.program_id(0)]


def later(first, last, kr, vh, vl, gs, gl, gq, gk, gv, pick, bias, back):
    count = last - first
    rows = lambda c: (last - 1 - c, 0)
    to = lambda c: (count - 1 - c, 0)
    narrow, wide = pl.BlockSpec((CHUNK, WIDE), rows), pl.BlockSpec((CHUNK, 512), rows)
    half = pl.BlockSpec((CHUNK, 128), rows)
    return call(
        functools.partial(later_kernel, first, last),
        (count,),
        [
            narrow, wide, wide, full(CHUNKS, HEADS, NF, HDIM), full(HEADS, NF, HDIM), half, half, wide,
            full(HEADS, WIDE, 2 * WIDE), full(1, 2 * WIDE), full(HEADS, 2 * WIDE, 128),
        ],
        pl.BlockSpec((CHUNK, 640), to),
        arr((count * CHUNK, 640)),
        (kr, vh, vl, gs, gl, gq, gk, gv, pick, bias, back),
        [pltpu.VMEM((HEADS, NF, HDIM), F32)],
        flops=2e9 * count,
        moved=3e6 * count,
    )


def conv_back(x, tail, taps):
    n = x.shape[0]
    row = lax.broadcasted_iota(jnp.int32, (8, 1), 0)
    once, twice = pltpu.roll(x, n - 1, 0), pltpu.roll(x, n - 2, 0)
    end1 = jnp.where(row == 7, tail[0:1], once[n - 8 :])
    end2 = jnp.where(row == 7, tail[1:2], jnp.where(row == 6, tail[0:1], twice[n - 8 :]))
    once = jnp.concatenate([once[: n - 8], end1], axis=0)
    twice = jnp.concatenate([twice[: n - 8], end2], axis=0)
    return (taps[0:1] * x + taps[1:2] * once + taps[2:3] * twice).astype(BF16)


def unconv_kernel(a_ref, b_ref, h_ref, t_ref, d_ref, dt_ref):
    n = a_ref.shape[0]
    for start in range(0, LEN, STEP):
        end = start + STEP
        src = a_ref[start:end] if start < n else b_ref[start - n : end - n]
        if end == LEN:
            tail = h_ref[...]
        else:
            tail = a_ref[end : end + 8] if end < n else b_ref[end - n : end - n + 8]
        got = conv_back(src, tail, t_ref[...])
        d_ref[start:end] = got
        dt_ref[:, start:end] = got.T


def unconv(a, b, halo, taps):
    n, m = a.shape[0], b.shape[0]
    return call(
        unconv_kernel,
        (1,),
        [full(n, 640), full(m, 640), full(8, 640), full(3, 640)],
        [full(LEN, 640), full(640, LEN)],
        [arr((LEN, 640), BF16), arr((640, LEN), BF16)],
        (a, b, halo, taps),
        moved=6e6,
    )


def f32(x):
    return x.astype(F32)


def flip(x, axis, bit):
    return lax.ppermute(x, axis, [(i, i ^ bit) for i in range(lax.axis_size(axis))])


def input_kernel(d_ref, wv_ref, wqk_ref, o_ref):
    d = d_ref[...]
    o_ref[0] = (nt(d[:, 128:], wv_ref[...]) + nn(d[:, :128], wqk_ref[...])).astype(BF16)


def input_products(d, wv, wqk):
    parts = wv.shape[0] // 512
    return call(
        input_kernel,
        (parts,),
        [full(LEN, 640), pl.BlockSpec((512, 512), lambda i: (i, 0)), pl.BlockSpec((128, 512), lambda i: (0, i))],
        pl.BlockSpec((1, LEN, 512), lambda i: (i, 0, 0)),
        arr((parts, LEN, 512), BF16),
        (d, wv, wqk),
        flops=2 * LEN * 640 * 4096,
        moved=15e6,
    )


def sum_kernel(p_ref, o_ref):
    total = f32(p_ref[0])
    for i in range(1, p_ref.shape[0]):
        total = total + f32(p_ref[i])
    o_ref[...] = total.astype(BF16)


def summed(parts, after):
    count, rows, width = parts.shape
    return call(
        sum_kernel,
        (8,),
        [pl.BlockSpec((count, rows // 8, width), lambda i: (0, i, 0))],
        pl.BlockSpec((rows // 8, width), lambda i: (i, 0)),
        arr((rows, width), BF16),
        (parts,),
        moved=9e6,
        after=after,
    )


def weight_kernel(dest_ref, d_ref, x_ref, theirs_ref, ours_ref):
    got = nn(d_ref[...], x_ref[...]).astype(BF16)

    @pl.when(pl.program_id(0) < 8)
    def _():
        theirs_ref[0] = got

    @pl.when(pl.program_id(0) >= 8)
    def _():
        ours_ref[0] = got


def split_kernel(mine_ref, came_ref, *outs):
    step = pl.program_id(0)
    got = f32(mine_ref[0]) + f32(came_ref[0])
    for j in range(4):

        @pl.when(step // 2 == j)
        def _(j=j):
            outs[j][0] = got.astype(BF16)


def row_sum_kernel(mine_ref, a_ref, b_ref, c_ref, keep_ref, send_ref):
    for r, out in enumerate((keep_ref, send_ref)):
        out[...] = (f32(mine_ref[r]) + f32(a_ref[r]) + f32(b_ref[r]) + f32(c_ref[r])).astype(out.dtype)


def finish_kernel(keep_ref, came_ref, q_ref, k_ref, v_ref):
    step = pl.program_id(0)
    total = keep_ref[...] + f32(came_ref[...])

    @pl.when(step == 0)
    def _():
        q_ref[...] = total[:64]
        k_ref[...] = total[64:]

    @pl.when(step > 0)
    def _():
        v_ref[...] = total.T


def to_x(x, by):
    return lax.ppermute(x, "seq", [(s, s // 8 * 8 + (s % 8 + 2 * by) % 8) for s in range(16)])


def reduce_weight_grad(dt, x, before):
    me = lax.axis_index("seq")
    y, px, core = me // 8, me // 2 % 4, me % 2
    width = x.shape[1] // 16
    chips = jnp.stack([((y ^ r) * 4 + (px + dx) % 4) * 2 for dx in range(4) for r in range(2)])
    dest = jnp.concatenate([chips + 1 - core, chips + core]).astype(jnp.int32)
    theirs, ours = call(
        weight_kernel,
        (16,),
        [pl.BlockSpec((640, LEN), lambda i, dest: (0, 0)), pl.BlockSpec((LEN, width), lambda i, dest: (0, dest[i]))],
        [
            pl.BlockSpec((1, 640, width), lambda i, dest: (jnp.minimum(i, 7), 0, 0)),
            pl.BlockSpec((1, 640, width), lambda i, dest: (jnp.maximum(i - 8, 0), 0, 0)),
        ],
        [arr((8, 640, width), BF16)] * 2,
        (dest, dt, x),
        prefetch=1,
        after=(before,),
        flops=2 * LEN * 640 * 4096,
        moved=15e6,
    )
    came = flip(theirs, "seq", 1)
    block = pl.BlockSpec((1, 640, width), lambda i: (i, 0, 0))
    parts = call(
        split_kernel,
        (8,),
        [block, block],
        [pl.BlockSpec((1, 640, width), lambda i, j=j: (jnp.clip(i - 2 * j, 0, 1), 0, 0)) for j in range(4)],
        [arr((2, 640, width), BF16)] * 4,
        (ours, came),
        moved=8e6,
    )
    mine, *rest = parts
    rest = [to_x(part, dx) for dx, part in enumerate(rest, 1)]
    pair = pl.BlockSpec((2, 128, width), lambda i: (0, i, 0))
    one = pl.BlockSpec((128, width), lambda i: (i, 0))
    keep, send = call(
        row_sum_kernel,
        (5,),
        [pair] * 4,
        [one] * 2,
        [arr((640, width)), arr((640, width), BF16)],
        (mine, *rest),
        moved=4e6,
    )
    return keep, flip(send, "seq", 8)


def finish_weight_grad(keep, came):
    width = keep.shape[1]
    one = pl.BlockSpec((128, width), lambda i: (i, 0))
    return call(
        finish_kernel,
        (5,),
        [one, one],
        [full(64, width), full(64, width), pl.BlockSpec((width, 128), lambda i: (0, jnp.maximum(i - 1, 0)))],
        [arr((64, width)), arr((64, width)), arr((width, 512))],
        (keep, came),
        moved=2e6,
    )


def along(x, by):
    n = lax.axis_size("seq")
    return lax.ppermute(x, "seq", [(i, i + by) for i in range(n) if 0 <= i + by < n])


def local(inputs, w_query, w_key, w_value, taps_query, taps_key, taps_value, out_gain, out_grad):
    packed, bias, back = feature_matrices()
    pick_q, pick_k = (jnp.asarray(packed[i], BF16) for i in range(2))
    pick_qt, pick_kt = (jnp.asarray(packed[i].transpose(0, 2, 1), BF16) for i in range(2))
    back_q, back_k = (jnp.asarray(back[i], BF16) for i in range(2))
    bias, bias_t = jnp.asarray(bias), jnp.asarray(bias.T)
    wq_t, wk_t = w_query.T, w_key.T
    taps_qk = jnp.concatenate([taps_query, taps_key], axis=1)
    taps = jnp.concatenate([taps_qk, taps_value], axis=1)

    tail = along(inputs[-16:], 1)
    proj_qk, proj_v, wqk_t = project(inputs, wq_t, wk_t, w_value)
    ql, kr, vh, vl, before, own = shard_state(
        proj_qk, proj_v, tail, wqk_t, w_value, taps_qk, taps_value, pick_kt, bias_t
    )
    earlier = carried_in(own, False)
    num = inner(ql, kr, vh, vl)
    outputs, dh, dl, grads, own_grad = forward(
        ql, num, before, earlier, out_grad, out_gain.reshape(1, 512), pick_q, pick_qt, bias, bias_t
    )
    after = carried_in(own_grad, True)
    gq, gk, gv = backward(ql, kr, vh, vl, dh, dl, before, earlier, pick_q, bias, back_q)
    rest = (kr, vh, vl, grads, after, gq, gk, gv, pick_k, bias, back_k)
    ga = later(0, 1, *rest)
    halo = along(ga[:8], -1)
    gb = later(1, CHUNKS, *rest)
    d, dt = unconv(ga, gb, halo, taps)
    blocks = input_products(d, w_value, wqk_t)
    parts = lax.all_to_all(blocks, "tp", 0, 0)
    grad_query, grad_key, grad_value = finish_weight_grad(*reduce_weight_grad(dt, inputs, blocks))
    input_grad = summed(parts, (grad_query,))
    return (outputs, input_grad, grad_query.T, grad_key.T, grad_value)


def solution(mesh):
    return jax.shard_map(
        local,
        mesh=mesh,
        in_specs=(
            P("seq", None),
            P(None, "tp"),
            P(None, "tp"),
            P(None, "tp"),
            P(None, "tp"),
            P(None, "tp"),
            P(None, "tp"),
            P("tp"),
            P("seq", "tp"),
        ),
        out_specs=(P("seq", "tp"), P("seq", "tp"), P("seq", "tp"), P("seq", "tp"), P("seq", "tp")),
        check_vma=False,
    )
```

```python
import functools

import jax
import jax.numpy as jnp
import numpy as np
from jax import lax
from jax.experimental import pallas as pl
from jax.experimental.pallas import tpu as pltpu
from jax.sharding import PartitionSpec as P

FEAT = 16
HDIM = 128
HEADS = 4
CHUNK = 256
LEN = 1024
CHUNKS = LEN // CHUNK
NF = 160
WIDE = 256
EPS = 1e-05
STEP = 128
F32, BF16 = jnp.float32, jnp.bfloat16


def feature_matrices():
    pairs = [(i, j) for i in range(FEAT) for j in range(i, FEAT)]
    pick = np.zeros((2, HEADS, 64, 2 * WIDE), np.float32)
    bias = np.zeros((1, 2 * WIDE), np.float32)
    for head in range(HEADS):
        base = head * FEAT
        for f, (i, j) in enumerate(pairs):
            pick[:, head, base + i, f] = 1.0
            pick[0, head, base + j, WIDE + f] = 0.5 if i == j else 1.0
            pick[1, head, base + j, WIDE + f] = 1.0
        for i in range(FEAT):
            pick[:, head, base + i, len(pairs) + i] = 1.0
    ones = len(pairs) + FEAT
    bias[0, ones] = 1.0
    bias[0, WIDE + len(pairs) : WIDE + ones + 1] = 1.0
    packed = np.zeros((2, HEADS, WIDE, 2 * WIDE), np.float32)
    packed[0, :, 0:64] = pick[0]
    packed[0, :, 64:128] = pick[0]
    packed[1, :, 0:64] = pick[1]
    packed[1, :, 128:192] = pick[1]
    back = np.zeros((2, HEADS, 2 * WIDE, 128), np.float32)
    back[:, :, :, 0:64] = pick.transpose(0, 1, 3, 2)
    return packed, bias, back


def nn(a, b):
    return lax.dot_general(a, b, (((1,), (0,)), ((), ())), preferred_element_type=F32)


def nt(a, b):
    return lax.dot_general(a, b, (((1,), (1,)), ((), ())), preferred_element_type=F32)


def halves(x):
    hi = x.astype(BF16)
    return hi, (x - hi.astype(F32)).astype(BF16)


def side(*parts):
    return jnp.concatenate(parts, axis=1)


def nn3(a_hi, a_lo, b_hi, b_lo):
    both = nn(a_hi, side(b_hi, b_lo))
    n = b_hi.shape[1]
    return both[:, :n] + both[:, n:] + nn(a_lo, b_hi)


def nt3(a_hi, a_lo, b_hi, b_lo):
    return nt(side(a_hi, a_lo), side(b_hi, b_hi)) + nt(a_hi, b_lo)


def factors(packed, pick, bias):
    both = nn(packed, pick) + bias
    return both[:, :WIDE], both[:, WIDE:]


def padded(state):
    return jnp.concatenate([state, jnp.zeros((WIDE - NF, HDIM), F32)], axis=0)


def head_mask(width, head):
    lane = lax.broadcasted_iota(jnp.int32, (1, width), 1)
    return (lane % 64) // FEAT == head


def cols(head):
    return slice(head * HDIM, (head + 1) * HDIM)


def call(body, grid, ins, outs, shapes, args, scratch=(), prefetch=0, flops=0, moved=0, after=()):
    if after:
        kept, skip = body, len(after)
        at = prefetch + len(ins)
        body = lambda *refs: kept(*refs[:at], *refs[at + skip :])
        ins = [*ins] + [pl.BlockSpec(memory_space=pl.ANY)] * skip
        args = (*args, *after)
    return pl.pallas_call(
        body,
        grid_spec=pltpu.PrefetchScalarGridSpec(
            num_scalar_prefetch=prefetch, grid=grid, in_specs=ins, out_specs=outs, scratch_shapes=list(scratch)
        ),
        out_shape=shapes,
        compiler_params=pltpu.CompilerParams(vmem_limit_bytes=56 * 2**20),
        cost_estimate=pl.CostEstimate(flops=int(flops), bytes_accessed=int(moved), transcendentals=0),
    )(*args)


def full(*shape):
    return pl.BlockSpec(shape, lambda *_: (0,) * len(shape))


def arr(shape, dtype=F32):
    return jax.ShapeDtypeStruct(shape, dtype)


def end_kernel(x_ref, wq_ref, wk_ref, wv_ref, o_ref, wqk_ref):
    wqk_ref[0:64] = wq_ref[...]
    wqk_ref[64:128] = wk_ref[...]
    x = x_ref[...]
    o_ref[:, :128] = nt(x, wqk_ref[...])
    o_ref[:, 128:] = nn(x, wv_ref[...])


def project_end(x, wq_t, wk_t, wv):
    depth = x.shape[1]
    return call(
        end_kernel,
        (1,),
        [pl.BlockSpec((CHUNK, depth), lambda c: (CHUNKS - 1, 0)), full(64, depth), full(64, depth), full(depth, 512)],
        [full(CHUNK, 640), full(128, depth)],
        [arr((CHUNK, 640)), arr((128, depth), BF16)],
        (x, wq_t, wk_t, wv),
        flops=2 * CHUNK * depth * 640,
        moved=8e6,
    )


def project_kernel(x_ref, wqk_ref, wv_ref, o_ref):
    x = x_ref[...]
    o_ref[:, :128] = nt(x, wqk_ref[...])
    o_ref[:, 128:] = nn(x, wv_ref[...])


def project(x, wqk_t, wv):
    depth = x.shape[1]
    rows = lambda c: (c, 0)
    return call(
        project_kernel,
        (CHUNKS - 1,),
        [pl.BlockSpec((CHUNK, depth), rows), full(128, depth), full(depth, 512)],
        pl.BlockSpec((CHUNK, 640), rows),
        arr((LEN - CHUNK, 640)),
        (x, wqk_t, wv),
        flops=2 * (LEN - CHUNK) * depth * 640,
        moved=12e6,
    )


def conv(x, tail, taps):
    row = lax.broadcasted_iota(jnp.int32, (8, 1), 0)
    once, twice = pltpu.roll(x, 1, 0), pltpu.roll(x, 2, 0)
    top1 = jnp.where(row == 0, tail[7:8], once[0:8])
    top2 = jnp.where(row == 0, tail[6:7], jnp.where(row == 1, tail[7:8], twice[0:8]))
    once = jnp.concatenate([top1, once[8:]], axis=0)
    twice = jnp.concatenate([top2, twice[8:]], axis=0)
    return taps[0:1] * x + taps[1:2] * once + taps[2:3] * twice


def state_kernel(
    a_ref, b_ref, before_ref, tail_ref, taps_ref, pick_ref, biast_ref,
    ql_ref, kr_ref, vh_ref, vl_ref, sp_ref, st_ref,
):
    c = pl.program_id(0)

    @pl.when(c == 0)
    def _():
        st_ref[...] = jnp.zeros_like(st_ref)

    x = jnp.where(c < CHUNKS - 1, a_ref[...], b_ref[...])
    both = conv(x, jnp.where(c > 0, before_ref[...], tail_ref[...]), taps_ref[...])
    qk, v = both[:, :128] * 0.5, both[:, 128:]
    lane = lax.broadcasted_iota(jnp.int32, (1, 128), 1)
    low = lane < 64
    turned = pltpu.roll(qk, 64, 1)
    hi = qk.astype(BF16).astype(F32)
    lo = qk - hi
    turned_hi = turned.astype(BF16).astype(F32)
    turned_lo = turned - turned_hi
    zero = jnp.zeros_like(qk)
    ql = side(jnp.where(low, hi, turned_lo), jnp.where(low, hi, zero)).astype(BF16)
    kr = side(jnp.where(low, turned_hi, hi), jnp.where(low, turned_lo, zero)).astype(BF16)
    ql_ref[...] = ql
    kr_ref[...] = kr
    v_hi, v_lo = halves(v)
    vh_ref[...] = v_hi
    vl_ref[...] = v_lo
    for head in range(HEADS):
        ab = nt(pick_ref[head], kr) + biast_ref[...]
        p_hi, p_lo = halves(ab[:NF] * ab[WIDE : WIDE + NF])
        own = nn3(p_hi, p_lo, v_hi[:, cols(head)], v_lo[:, cols(head)])
        sp_ref[0, head] = st_ref[head]
        st_ref[head] += own


def shard_state(proj, end, tail, taps, pick_kt, bias_t):
    rows = lambda c: (c, 0)
    before = lambda c: (jnp.maximum(c * (CHUNK // 8) - 1, 0), 0)
    return call(
        state_kernel,
        (CHUNKS,),
        [
            pl.BlockSpec((CHUNK, 640), lambda c: (jnp.minimum(c, CHUNKS - 2), 0)),
            full(CHUNK, 640),
            pl.BlockSpec((8, 640), before),
            full(8, 640),
            full(3, 640),
            full(HEADS, 2 * WIDE, WIDE),
            full(2 * WIDE, 1),
        ],
        [
            pl.BlockSpec((CHUNK, WIDE), rows),
            pl.BlockSpec((CHUNK, WIDE), rows),
            pl.BlockSpec((CHUNK, 512), rows),
            pl.BlockSpec((CHUNK, 512), rows),
            pl.BlockSpec((1, HEADS, NF, HDIM), lambda c: (c, 0, 0, 0)),
            full(HEADS, NF, HDIM),
        ],
        [
            arr((LEN, WIDE), BF16),
            arr((LEN, WIDE), BF16),
            arr((LEN, 512), BF16),
            arr((LEN, 512), BF16),
            arr((CHUNKS, HEADS, NF, HDIM)),
            arr((HEADS, NF, HDIM)),
        ],
        (proj, end, proj, tail, taps, pick_kt, bias_t),
        flops=4e9,
        moved=15e6,
    )


def running_kernel(backward, x_ref, o_ref):
    count = x_ref.shape[0]
    order = range(count - 1, -1, -1) if backward else range(count)
    total = jnp.zeros(x_ref.shape[1:], F32)
    for i in order:
        o_ref[i] = total
        total = total + x_ref[i]


def carried_in(state, backward):
    count = lax.axis_size("seq")
    rows = HEADS * NF // count
    pieces = lax.all_to_all(state.reshape(count, rows, HDIM), "seq", 0, 0)
    shape = (count, rows, HDIM)
    sums = call(
        functools.partial(running_kernel, backward), (1,), [full(*shape)], full(*shape), arr(shape), (pieces,), moved=6e5
    )
    return lax.all_to_all(sums, "seq", 0, 0).reshape(HEADS, NF, HDIM)


def lower():
    row = lax.broadcasted_iota(jnp.int32, (CHUNK, CHUNK), 0)
    col = lax.broadcasted_iota(jnp.int32, (CHUNK, CHUNK), 1)
    return row >= col


def inner_kernel(ql_ref, kr_ref, vh_ref, vl_ref, num_ref):
    ql, kr = ql_ref[...], kr_ref[...]
    causal = lower()
    for head in range(HEADS):
        mine = jnp.where(head_mask(WIDE, head), ql, jnp.zeros_like(ql))
        s = nt(mine, kr)
        w_hi, w_lo = halves(jnp.where(causal, 1.0 + s + 0.5 * s * s, 0.0))
        num_ref[:, cols(head)] = nn3(w_hi, w_lo, vh_ref[:, cols(head)], vl_ref[:, cols(head)])


def inner(ql, kr, vh, vl):
    rows = lambda c: (c, 0)
    narrow, wide = pl.BlockSpec((CHUNK, WIDE), rows), pl.BlockSpec((CHUNK, 512), rows)
    return call(
        inner_kernel, (CHUNKS,), [narrow, narrow, wide, wide], wide, arr((LEN, 512)), (ql, kr, vh, vl), flops=6e9, moved=6e6
    )


def forward_kernel(ql_ref, num_ref, sp_ref, se_ref, og_ref, gain_ref, pick_ref, pickt_ref, bias_ref, biast_ref,
                   out_ref, dh_ref, dl_ref, gs_ref, gt_ref):
    @pl.when(pl.program_id(0) == 0)
    def _():
        gt_ref[...] = jnp.zeros_like(gt_ref)

    ql = ql_ref[...]
    for head in range(HEADS):
        a, b = factors(ql, pick_ref[head], bias_ref[...])
        p_hi, p_lo = halves(a * b)
        s_hi, s_lo = halves(padded(sp_ref[0, head] + se_ref[head]))
        num = num_ref[:, cols(head)] + nn3(p_hi, p_lo, s_hi, s_lo)
        r = lax.rsqrt(jnp.mean(num * num, axis=-1, keepdims=True) + EPS)
        gain = gain_ref[:, cols(head)]
        unit = num * r
        out_ref[:, cols(head)] = unit * gain
        g = og_ref[:, cols(head)] * gain
        d = r * (g - unit * jnp.mean(g * unit, axis=-1, keepdims=True))
        d_hi, d_lo = halves(d)
        dh_ref[:, cols(head)] = d_hi
        dl_ref[:, cols(head)] = d_lo
        ab = nt(pickt_ref[head], ql) + biast_ref[...]
        pt_hi, pt_lo = halves(ab[:NF] * ab[WIDE : WIDE + NF])
        own = nn3(pt_hi, pt_lo, d_hi, d_lo)
        gs_ref[0, head] = own
        gt_ref[head] += own


def forward(ql, num, sp, se, og, gain, pick, pick_t, bias, bias_t):
    rows = lambda c: (c, 0)
    narrow, wide = pl.BlockSpec((CHUNK, WIDE), rows), pl.BlockSpec((CHUNK, 512), rows)
    states = pl.BlockSpec((1, HEADS, NF, HDIM), lambda c: (c, 0, 0, 0))
    return call(
        forward_kernel,
        (CHUNKS,),
        [
            narrow, wide, states, full(HEADS, NF, HDIM), wide, full(1, 512),
            full(HEADS, WIDE, 2 * WIDE), full(HEADS, 2 * WIDE, WIDE), full(1, 2 * WIDE), full(2 * WIDE, 1),
        ],
        [wide, wide, wide, states, full(HEADS, NF, HDIM)],
        [
            arr((LEN, 512)), arr((LEN, 512), BF16), arr((LEN, 512), BF16),
            arr((CHUNKS, HEADS, NF, HDIM)), arr((HEADS, NF, HDIM)),
        ],
        (ql, num, sp, se, og, gain, pick, pick_t, bias, bias_t),
        flops=8e9,
        moved=12e6,
    )


def query_kernel(ql_ref, kr_ref, vh_ref, vl_ref, dh_ref, dl_ref, sp_ref, se_ref, pick_ref, bias_ref, back_ref, gq_ref):
    ql, kr = ql_ref[...], kr_ref[...]
    causal = lower()
    gq = jnp.zeros((CHUNK, WIDE), F32)
    du = jnp.zeros((CHUNK, 128), F32)
    for head in range(HEADS):
        mask = head_mask(WIDE, head)
        q = jnp.where(mask, ql, jnp.zeros_like(ql))
        k = jnp.where(mask, kr, jnp.zeros_like(kr))
        v_hi, v_lo = vh_ref[:, cols(head)], vl_ref[:, cols(head)]
        d_hi, d_lo = dh_ref[:, cols(head)], dl_ref[:, cols(head)]
        slope = jnp.where(causal, 1.0 + nt(q, kr), 0.0)
        gq = gq + nn((nt3(d_hi, d_lo, v_hi, v_lo) * slope).astype(BF16), k)
        s_hi, s_lo = halves(padded(sp_ref[0, head] + se_ref[head]))
        dp = nt3(d_hi, d_lo, s_hi, s_lo)
        a, b = factors(ql, pick_ref[head], bias_ref[...])
        du = du + nn(side(dp * b, dp * a).astype(BF16), back_ref[head])
    gq_ref[...] = gq[:, :128] + gq[:, 128:] + du


def key_kernel(ql_ref, kr_ref, vh_ref, vl_ref, dh_ref, dl_ref, gk_ref, gv_ref):
    ql, kr = ql_ref[...], kr_ref[...]
    row = lax.broadcasted_iota(jnp.int32, (CHUNK, CHUNK), 0)
    col = lax.broadcasted_iota(jnp.int32, (CHUNK, CHUNK), 1)
    causal = col >= row
    gk = jnp.zeros((CHUNK, WIDE), F32)
    for head in range(HEADS):
        mask = head_mask(WIDE, head)
        q = jnp.where(mask, ql, jnp.zeros_like(ql))
        k = jnp.where(mask, kr, jnp.zeros_like(kr))
        v_hi, v_lo = vh_ref[:, cols(head)], vl_ref[:, cols(head)]
        d_hi, d_lo = dh_ref[:, cols(head)], dl_ref[:, cols(head)]
        s = nt(k, ql)
        ds_hi, ds_lo = halves(nt3(v_hi, v_lo, d_hi, d_lo) * jnp.where(causal, 1.0 + s, 0.0))
        gk = gk + nn(ds_hi, q) + nn(ds_lo, q)
        w_hi, w_lo = halves(jnp.where(causal, 1.0 + s + 0.5 * s * s, 0.0))
        gv_ref[:, cols(head)] = nn3(w_hi, w_lo, d_hi, d_lo)
    gk_ref[...] = gk[:, :128] + pltpu.roll(gk[:, :128], 64, 1)


def backward(ql, kr, vh, vl, dh, dl, sp, se, pick, bias, back):
    rows = lambda c: (c, 0)
    narrow, wide = pl.BlockSpec((CHUNK, WIDE), rows), pl.BlockSpec((CHUNK, 512), rows)
    half = pl.BlockSpec((CHUNK, 128), rows)
    states = pl.BlockSpec((1, HEADS, NF, HDIM), lambda c: (c, 0, 0, 0))
    gk, gv = call(
        key_kernel,
        (CHUNKS,),
        [narrow, narrow, wide, wide, wide, wide],
        [half, wide],
        [arr((LEN, 128)), arr((LEN, 512))],
        (ql, kr, vh, vl, dh, dl),
        flops=8e9,
        moved=8e6,
    )
    gq = call(
        query_kernel,
        (CHUNKS,),
        [
            narrow, narrow, wide, wide, wide, wide, states, full(HEADS, NF, HDIM),
            full(HEADS, WIDE, 2 * WIDE), full(1, 2 * WIDE), full(HEADS, 2 * WIDE, 128),
        ],
        half,
        arr((LEN, 128)),
        (ql, kr, vh, vl, dh, dl, sp, se, pick, bias, back),
        flops=8e9,
        moved=8e6,
    )
    return gq, gk, gv


def later_kernel(first, last, kr_ref, vh_ref, vl_ref, gs_ref, gl_ref, gq_ref, gk_ref, gv_ref, pick_ref, bias_ref,
                 back_ref, o_ref, total):
    @pl.when(pl.program_id(0) == 0)
    def _():
        begin = gl_ref[...]
        for c in range(CHUNKS - 1, last - 1, -1):
            begin = begin + gs_ref[c]
        total[...] = begin

    kr = kr_ref[...]
    du = jnp.zeros((CHUNK, 128), F32)
    for head in range(HEADS):
        a, b = factors(kr, pick_ref[head], bias_ref[...])
        l_hi, l_lo = halves(padded(total[head]))
        gained = nn((a * b).astype(BF16), side(l_hi, l_lo))
        v_hi, v_lo = vh_ref[:, cols(head)], vl_ref[:, cols(head)]
        o_ref[:, 128 + head * HDIM : 256 + head * HDIM] = gv_ref[:, cols(head)] + gained[:, :HDIM] + gained[:, HDIM:]
        dp = nt(side(v_hi, v_lo), side(l_hi, l_hi))
        du = du + nn(side(dp * b, dp * a).astype(BF16), back_ref[head])
    low = lax.broadcasted_iota(jnp.int32, (1, 128), 1) < 64
    o_ref[:, :128] = 0.5 * jnp.where(low, gq_ref[...], pltpu.roll(gk_ref[...] + du, 64, 1))
    total[...] += gs_ref[last - 1 - pl.program_id(0)]


def later(first, last, kr, vh, vl, gs, gl, gq, gk, gv, pick, bias, back):
    count = last - first
    rows = lambda c: (last - 1 - c, 0)
    to = lambda c: (count - 1 - c, 0)
    narrow, wide = pl.BlockSpec((CHUNK, WIDE), rows), pl.BlockSpec((CHUNK, 512), rows)
    half = pl.BlockSpec((CHUNK, 128), rows)
    return call(
        functools.partial(later_kernel, first, last),
        (count,),
        [
            narrow, wide, wide, full(CHUNKS, HEADS, NF, HDIM), full(HEADS, NF, HDIM), half, half, wide,
            full(HEADS, WIDE, 2 * WIDE), full(1, 2 * WIDE), full(HEADS, 2 * WIDE, 128),
        ],
        pl.BlockSpec((CHUNK, 640), to),
        arr((count * CHUNK, 640)),
        (kr, vh, vl, gs, gl, gq, gk, gv, pick, bias, back),
        [pltpu.VMEM((HEADS, NF, HDIM), F32)],
        flops=2e9 * count,
        moved=3e6 * count,
    )


def conv_back(x, tail, taps):
    n = x.shape[0]
    row = lax.broadcasted_iota(jnp.int32, (8, 1), 0)
    once, twice = pltpu.roll(x, n - 1, 0), pltpu.roll(x, n - 2, 0)
    end1 = jnp.where(row == 7, tail[0:1], once[n - 8 :])
    end2 = jnp.where(row == 7, tail[1:2], jnp.where(row == 6, tail[0:1], twice[n - 8 :]))
    once = jnp.concatenate([once[: n - 8], end1], axis=0)
    twice = jnp.concatenate([twice[: n - 8], end2], axis=0)
    return (taps[0:1] * x + taps[1:2] * once + taps[2:3] * twice).astype(BF16)


def f32(x):
    return x.astype(F32)


def flip(x, axis, bit):
    return lax.ppermute(x, axis, [(i, i ^ bit) for i in range(lax.axis_size(axis))])


def input_kernel(a_ref, b_ref, h_ref, t_ref, wv_ref, wqk_ref, o_ref, dt_ref, d_ref):
    @pl.when(pl.program_id(0) == 0)
    def _():
        n = a_ref.shape[0]
        for start in range(0, LEN, STEP):
            end = start + STEP
            src = a_ref[start:end] if start < n else b_ref[start - n : end - n]
            if end == LEN:
                tail = h_ref[...]
            else:
                tail = a_ref[end : end + 8] if end < n else b_ref[end - n : end - n + 8]
            got = conv_back(src, tail, t_ref[...])
            d_ref[start:end] = got
            dt_ref[:, start:end] = got.T

    d = d_ref[...]
    for i in range(o_ref.shape[0]):
        part = slice(512 * i, 512 * (i + 1))
        o_ref[i] = (nt(d[:, 128:], wv_ref[part]) + nn(d[:, :128], wqk_ref[:, part])).astype(BF16)


def input_products(a, b, halo, taps, wv, wqk):
    parts, wide = wv.shape[0] // 512, 2
    n, m = a.shape[0], b.shape[0]
    return call(
        input_kernel,
        (parts // wide,),
        [
            full(n, 640), full(m, 640), full(8, 640), full(3, 640),
            pl.BlockSpec((512 * wide, 512), lambda i: (i, 0)), pl.BlockSpec((128, 512 * wide), lambda i: (0, i)),
        ],
        [pl.BlockSpec((wide, LEN, 512), lambda i: (i, 0, 0)), full(640, LEN)],
        [arr((parts, LEN, 512), BF16), arr((640, LEN), BF16)],
        (a, b, halo, taps, wv, wqk),
        [pltpu.VMEM((LEN, 640), BF16)],
        flops=2 * LEN * 640 * 4096,
        moved=18e6,
    )


def weight_kernel(dest_ref, d_ref, x_ref, theirs_ref, ours_ref):
    got = nn(d_ref[...], x_ref[...]).astype(BF16)
    half = got.shape[1] // 2
    low, high = got[:, :half], got[:, half:]
    first = dest_ref[8] == 0
    theirs_ref[0] = jnp.where(first, high, low)
    ours_ref[0] = jnp.where(first, low, high)


def split_kernel(mine_ref, came_ref, *outs):
    step = pl.program_id(0)
    got = f32(mine_ref[0]) + f32(came_ref[0])
    for j in range(4):

        @pl.when(step // 2 == j)
        def _(j=j):
            outs[j][0] = got.astype(BF16)


def row_sum_kernel(mine_ref, a_ref, b_ref, c_ref, keep_ref, send_ref):
    for r, out in enumerate((keep_ref, send_ref)):
        out[...] = (f32(mine_ref[r]) + f32(a_ref[r]) + f32(b_ref[r]) + f32(c_ref[r])).astype(out.dtype)


def finish_kernel(keep_ref, came_ref, q_ref, k_ref, v_ref):
    step = pl.program_id(0)
    total = keep_ref[...] + f32(came_ref[...])

    @pl.when(step == 0)
    def _():
        q_ref[...] = total[:64]
        k_ref[...] = total[64:]

    @pl.when(step > 0)
    def _():
        v_ref[...] = total.T


def to_x(x, by):
    return lax.ppermute(x, "seq", [(s, s // 8 * 8 + (s % 8 + 2 * by) % 8) for s in range(16)])


def reduce_weight_grad(dt, x, before):
    me = lax.axis_index("seq")
    y, px, core = me // 8, me // 2 % 4, me % 2
    width = x.shape[1] // 16
    chips = [(y ^ r) * 4 + (px + dx) % 4 for dx in range(4) for r in range(2)]
    dest = jnp.stack([*chips, core]).astype(jnp.int32)
    theirs, ours = call(
        weight_kernel,
        (8,),
        [pl.BlockSpec((640, LEN), lambda i, dest: (0, 0)), pl.BlockSpec((LEN, 2 * width), lambda i, dest: (0, dest[i]))],
        [pl.BlockSpec((1, 640, width), lambda i, dest: (i, 0, 0))] * 2,
        [arr((8, 640, width), BF16)] * 2,
        (dest, dt, x),
        prefetch=1,
        after=(before,),
        flops=2 * LEN * 640 * 4096,
        moved=15e6,
    )
    came = flip(theirs, "seq", 1)
    block = pl.BlockSpec((1, 640, width), lambda i: (i, 0, 0))
    parts = call(
        split_kernel,
        (8,),
        [block, block],
        [pl.BlockSpec((1, 640, width), lambda i, j=j: (jnp.clip(i - 2 * j, 0, 1), 0, 0)) for j in range(4)],
        [arr((2, 640, width), BF16)] * 4,
        (ours, came),
        moved=8e6,
    )
    mine, *rest = parts
    rest = [to_x(part, dx) for dx, part in enumerate(rest, 1)]
    pair = pl.BlockSpec((2, 128, width), lambda i: (0, i, 0))
    one = pl.BlockSpec((128, width), lambda i: (i, 0))
    keep, send = call(
        row_sum_kernel,
        (5,),
        [pair] * 4,
        [one] * 2,
        [arr((640, width)), arr((640, width), BF16)],
        (mine, *rest),
        moved=4e6,
    )
    return keep, flip(send, "seq", 8)


def finish_weight_grad(keep, came):
    width = keep.shape[1]
    one = pl.BlockSpec((128, width), lambda i: (i, 0))
    return call(
        finish_kernel,
        (5,),
        [one, one],
        [full(64, width), full(64, width), pl.BlockSpec((width, 128), lambda i: (0, jnp.maximum(i - 1, 0)))],
        [arr((64, width)), arr((64, width)), arr((width, 512))],
        (keep, came),
        moved=2e6,
    )


def along(x, by):
    n = lax.axis_size("seq")
    return lax.ppermute(x, "seq", [(i, i + by) for i in range(n) if 0 <= i + by < n])


def local(inputs, w_query, w_key, w_value, taps_query, taps_key, taps_value, out_gain, out_grad):
    packed, bias, back = feature_matrices()
    pick_q, pick_k = (jnp.asarray(packed[i], BF16) for i in range(2))
    pick_qt, pick_kt = (jnp.asarray(packed[i].transpose(0, 2, 1), BF16) for i in range(2))
    back_q, back_k = (jnp.asarray(back[i], BF16) for i in range(2))
    bias, bias_t = jnp.asarray(bias), jnp.asarray(bias.T)
    wq_t, wk_t = w_query.T, w_key.T
    taps = jnp.concatenate([taps_query, taps_key, taps_value], axis=1)

    end, wqk_t = project_end(inputs, wq_t, wk_t, w_value)
    tail = along(end[-8:], 1)
    proj = project(inputs, wqk_t, w_value)
    ql, kr, vh, vl, before, own = shard_state(proj, end, tail, taps, pick_kt, bias_t)
    earlier = carried_in(own, False)
    num = inner(ql, kr, vh, vl)
    outputs, dh, dl, grads, own_grad = forward(
        ql, num, before, earlier, out_grad, out_gain.reshape(1, 512), pick_q, pick_qt, bias, bias_t
    )
    after = carried_in(own_grad, True)
    gq, gk, gv = backward(ql, kr, vh, vl, dh, dl, before, earlier, pick_q, bias, back_q)
    rest = (kr, vh, vl, grads, after, gq, gk, gv, pick_k, bias, back_k)
    ga = later(0, 1, *rest)
    halo = along(ga[:8], -1)
    gb = later(1, CHUNKS, *rest)
    blocks, dt = input_products(ga, gb, halo, taps, w_value, wqk_t)
    parts = lax.all_to_all(blocks, "tp", 0, 0)
    grad_query, grad_key, grad_value = finish_weight_grad(*reduce_weight_grad(dt, inputs, blocks))
    input_grad = jnp.sum(parts.astype(F32), axis=0).astype(BF16)
    return (outputs, input_grad, grad_query.T, grad_key.T, grad_value)


def solution(mesh):
    return jax.shard_map(
        local,
        mesh=mesh,
        in_specs=(
            P("seq", None),
            P(None, "tp"),
            P(None, "tp"),
            P(None, "tp"),
            P(None, "tp"),
            P(None, "tp"),
            P(None, "tp"),
            P("tp"),
            P("seq", "tp"),
        ),
        out_specs=(P("seq", "tp"), P("seq", "tp"), P("seq", "tp"), P("seq", "tp"), P("seq", "tp")),
        check_vma=False,
    )
```

```python
import functools

import jax
import jax.numpy as jnp
import numpy as np
from jax import lax
from jax.experimental import pallas as pl
from jax.experimental.pallas import tpu as pltpu
from jax.sharding import PartitionSpec as P

FEAT = 16
HDIM = 128
HEADS = 4
CHUNK = 256
LEN = 1024
CHUNKS = LEN // CHUNK
NF = 160
WIDE = 256
EPS = 1e-05
STEP = 128
F32, BF16 = jnp.float32, jnp.bfloat16


def feature_matrices():
    pairs = [(i, j) for i in range(FEAT) for j in range(i, FEAT)]
    pick = np.zeros((2, HEADS, 64, 2 * WIDE), np.float32)
    bias = np.zeros((1, 2 * WIDE), np.float32)
    for head in range(HEADS):
        base = head * FEAT
        for f, (i, j) in enumerate(pairs):
            pick[:, head, base + i, f] = 1.0
            pick[0, head, base + j, WIDE + f] = 0.5 if i == j else 1.0
            pick[1, head, base + j, WIDE + f] = 1.0
        for i in range(FEAT):
            pick[:, head, base + i, len(pairs) + i] = 1.0
    ones = len(pairs) + FEAT
    bias[0, ones] = 1.0
    bias[0, WIDE + len(pairs) : WIDE + ones + 1] = 1.0
    packed = np.zeros((2, HEADS, WIDE, 2 * WIDE), np.float32)
    packed[0, :, 0:64] = pick[0]
    packed[0, :, 64:128] = pick[0]
    packed[1, :, 0:64] = pick[1]
    packed[1, :, 128:192] = pick[1]
    back = np.zeros((2, HEADS, 2 * WIDE, 128), np.float32)
    back[:, :, :, 0:64] = pick.transpose(0, 1, 3, 2)
    return packed, bias, back


def nn(a, b):
    return lax.dot_general(a, b, (((1,), (0,)), ((), ())), preferred_element_type=F32)


def nt(a, b):
    return lax.dot_general(a, b, (((1,), (1,)), ((), ())), preferred_element_type=F32)


def halves(x):
    hi = x.astype(BF16)
    return hi, (x - hi.astype(F32)).astype(BF16)


def side(*parts):
    return jnp.concatenate(parts, axis=1)


def nn3(a_hi, a_lo, b_hi, b_lo):
    both = nn(a_hi, side(b_hi, b_lo))
    n = b_hi.shape[1]
    return both[:, :n] + both[:, n:] + nn(a_lo, b_hi)


def nt3(a_hi, a_lo, b_hi, b_lo):
    return nt(side(a_hi, a_lo), side(b_hi, b_hi)) + nt(a_hi, b_lo)


def factors(packed, pick, bias):
    both = nn(packed, pick) + bias
    return both[:, :WIDE], both[:, WIDE:]


def padded(state):
    return jnp.concatenate([state, jnp.zeros((WIDE - NF, HDIM), F32)], axis=0)


def head_mask(width, head):
    lane = lax.broadcasted_iota(jnp.int32, (1, width), 1)
    return (lane % 64) // FEAT == head


def cols(head):
    return slice(head * HDIM, (head + 1) * HDIM)


def call(body, grid, ins, outs, shapes, args, scratch=(), prefetch=0, flops=0, moved=0, after=()):
    if after:
        kept, skip = body, len(after)
        at = prefetch + len(ins)
        body = lambda *refs: kept(*refs[:at], *refs[at + skip :])
        ins = [*ins] + [pl.BlockSpec(memory_space=pl.ANY)] * skip
        args = (*args, *after)
    return pl.pallas_call(
        body,
        grid_spec=pltpu.PrefetchScalarGridSpec(
            num_scalar_prefetch=prefetch, grid=grid, in_specs=ins, out_specs=outs, scratch_shapes=list(scratch)
        ),
        out_shape=shapes,
        compiler_params=pltpu.CompilerParams(vmem_limit_bytes=56 * 2**20),
        cost_estimate=pl.CostEstimate(flops=int(flops), bytes_accessed=int(moved), transcendentals=0),
    )(*args)


def full(*shape):
    return pl.BlockSpec(shape, lambda *_: (0,) * len(shape))


def arr(shape, dtype=F32):
    return jax.ShapeDtypeStruct(shape, dtype)


def end_kernel(x_ref, wq_ref, wk_ref, wv_ref, o_ref, tail_ref, wqk_ref):
    wqk_ref[0:64] = wq_ref[...]
    wqk_ref[64:128] = wk_ref[...]
    x = x_ref[...]
    o_ref[:, :128] = nt(x, wqk_ref[...])
    o_ref[:, 128:] = nn(x, wv_ref[...])
    tail_ref[...] = o_ref[CHUNK - 8 :]


def project_end(x, wq_t, wk_t, wv):
    depth = x.shape[1]
    return call(
        end_kernel,
        (1,),
        [pl.BlockSpec((CHUNK, depth), lambda c: (CHUNKS - 1, 0)), full(64, depth), full(64, depth), full(depth, 512)],
        [full(CHUNK, 640), full(8, 640), full(128, depth)],
        [arr((CHUNK, 640)), arr((8, 640)), arr((128, depth), BF16)],
        (x, wq_t, wk_t, wv),
        flops=2 * CHUNK * depth * 640,
        moved=8e6,
    )


def project_kernel(x_ref, wqk_ref, wv_ref, o_ref):
    x = x_ref[...]
    o_ref[:, :128] = nt(x, wqk_ref[...])
    o_ref[:, 128:] = nn(x, wv_ref[...])


def project(x, wqk_t, wv):
    depth = x.shape[1]
    rows = lambda c: (c, 0)
    return call(
        project_kernel,
        (CHUNKS - 1,),
        [pl.BlockSpec((CHUNK, depth), rows), full(128, depth), full(depth, 512)],
        pl.BlockSpec((CHUNK, 640), rows),
        arr((LEN - CHUNK, 640)),
        (x, wqk_t, wv),
        flops=2 * (LEN - CHUNK) * depth * 640,
        moved=12e6,
    )


def conv(x, tail, taps):
    row = lax.broadcasted_iota(jnp.int32, (8, 1), 0)
    once, twice = pltpu.roll(x, 1, 0), pltpu.roll(x, 2, 0)
    top1 = jnp.where(row == 0, tail[7:8], once[0:8])
    top2 = jnp.where(row == 0, tail[6:7], jnp.where(row == 1, tail[7:8], twice[0:8]))
    once = jnp.concatenate([top1, once[8:]], axis=0)
    twice = jnp.concatenate([top2, twice[8:]], axis=0)
    return taps[0:1] * x + taps[1:2] * once + taps[2:3] * twice


def state_kernel(
    a_ref, b_ref, before_ref, tail_ref, taps_ref, pick_ref, biast_ref,
    ql_ref, kr_ref, vh_ref, vl_ref, sp_ref, st_ref,
):
    c = pl.program_id(0)

    @pl.when(c == 0)
    def _():
        st_ref[...] = jnp.zeros_like(st_ref)

    x = jnp.where(c < CHUNKS - 1, a_ref[...], b_ref[...])
    both = conv(x, jnp.where(c > 0, before_ref[...], tail_ref[...]), taps_ref[...])
    qk, v = both[:, :128] * 0.5, both[:, 128:]
    lane = lax.broadcasted_iota(jnp.int32, (1, 128), 1)
    low = lane < 64
    turned = pltpu.roll(qk, 64, 1)
    hi = qk.astype(BF16).astype(F32)
    lo = qk - hi
    turned_hi = turned.astype(BF16).astype(F32)
    turned_lo = turned - turned_hi
    zero = jnp.zeros_like(qk)
    ql = side(jnp.where(low, hi, turned_lo), jnp.where(low, hi, zero)).astype(BF16)
    kr = side(jnp.where(low, turned_hi, hi), jnp.where(low, turned_lo, zero)).astype(BF16)
    ql_ref[...] = ql
    kr_ref[...] = kr
    v_hi, v_lo = halves(v)
    vh_ref[...] = v_hi
    vl_ref[...] = v_lo
    for head in range(HEADS):
        ab = nt(pick_ref[head], kr) + biast_ref[...]
        p_hi, p_lo = halves(ab[:NF] * ab[WIDE : WIDE + NF])
        own = nn3(p_hi, p_lo, v_hi[:, cols(head)], v_lo[:, cols(head)])
        sp_ref[0, head] = st_ref[head]
        st_ref[head] += own


def shard_state(proj, end, tail, taps, pick_kt, bias_t):
    rows = lambda c: (c, 0)
    before = lambda c: (jnp.maximum(c * (CHUNK // 8) - 1, 0), 0)
    return call(
        state_kernel,
        (CHUNKS,),
        [
            pl.BlockSpec((CHUNK, 640), lambda c: (jnp.minimum(c, CHUNKS - 2), 0)),
            full(CHUNK, 640),
            pl.BlockSpec((8, 640), before),
            full(8, 640),
            full(3, 640),
            full(HEADS, 2 * WIDE, WIDE),
            full(2 * WIDE, 1),
        ],
        [
            pl.BlockSpec((CHUNK, WIDE), rows),
            pl.BlockSpec((CHUNK, WIDE), rows),
            pl.BlockSpec((CHUNK, 512), rows),
            pl.BlockSpec((CHUNK, 512), rows),
            pl.BlockSpec((1, HEADS, NF, HDIM), lambda c: (c, 0, 0, 0)),
            full(HEADS, NF, HDIM),
        ],
        [
            arr((LEN, WIDE), BF16),
            arr((LEN, WIDE), BF16),
            arr((LEN, 512), BF16),
            arr((LEN, 512), BF16),
            arr((CHUNKS, HEADS, NF, HDIM)),
            arr((HEADS, NF, HDIM)),
        ],
        (proj, end, proj, tail, taps, pick_kt, bias_t),
        flops=4e9,
        moved=15e6,
    )


def running_kernel(backward, x_ref, o_ref):
    count = x_ref.shape[0]
    order = range(count - 1, -1, -1) if backward else range(count)
    total = jnp.zeros(x_ref.shape[1:], F32)
    for i in order:
        o_ref[i] = total
        total = total + x_ref[i]


def carried_in(state, backward):
    count = lax.axis_size("seq")
    rows = HEADS * NF // count
    pieces = lax.all_to_all(state.reshape(count, rows, HDIM), "seq", 0, 0)
    shape = (count, rows, HDIM)
    sums = call(
        functools.partial(running_kernel, backward), (1,), [full(*shape)], full(*shape), arr(shape), (pieces,), moved=6e5
    )
    return lax.all_to_all(sums, "seq", 0, 0).reshape(HEADS, NF, HDIM)


def lower():
    row = lax.broadcasted_iota(jnp.int32, (CHUNK, CHUNK), 0)
    col = lax.broadcasted_iota(jnp.int32, (CHUNK, CHUNK), 1)
    return row >= col


def inner_kernel(ql_ref, kr_ref, vh_ref, vl_ref, num_ref):
    ql, kr = ql_ref[...], kr_ref[...]
    causal = lower()
    for head in range(HEADS):
        mine = jnp.where(head_mask(WIDE, head), ql, jnp.zeros_like(ql))
        s = nt(mine, kr)
        w_hi, w_lo = halves(jnp.where(causal, 1.0 + s + 0.5 * s * s, 0.0))
        num_ref[:, cols(head)] = nn3(w_hi, w_lo, vh_ref[:, cols(head)], vl_ref[:, cols(head)])


def inner(ql, kr, vh, vl):
    rows = lambda c: (c, 0)
    narrow, wide = pl.BlockSpec((CHUNK, WIDE), rows), pl.BlockSpec((CHUNK, 512), rows)
    return call(
        inner_kernel, (CHUNKS,), [narrow, narrow, wide, wide], wide, arr((LEN, 512)), (ql, kr, vh, vl), flops=6e9, moved=6e6
    )


def feature_kernel(ql_ref, pick_ref, pickt_ref, bias_ref, biast_ref, ph_ref, pl_ref, th_ref, tl_ref):
    ql = ql_ref[...]
    for head in range(HEADS):
        part = slice(head * WIDE, (head + 1) * WIDE)
        a, b = factors(ql, pick_ref[head], bias_ref[...])
        ph_ref[:, part], pl_ref[:, part] = halves(a * b)
        ab = nt(pickt_ref[head], ql) + biast_ref[...]
        th_ref[head], tl_ref[head] = halves(ab[:NF] * ab[WIDE : WIDE + NF])


def query_features(ql, pick, pick_t, bias, bias_t):
    rows = lambda c: (c, 0)
    wide, turned = pl.BlockSpec((CHUNK, HEADS * WIDE), rows), pl.BlockSpec((HEADS, NF, CHUNK), lambda c: (0, 0, c))
    return call(
        feature_kernel,
        (CHUNKS,),
        [
            pl.BlockSpec((CHUNK, WIDE), rows),
            full(HEADS, WIDE, 2 * WIDE), full(HEADS, 2 * WIDE, WIDE), full(1, 2 * WIDE), full(2 * WIDE, 1),
        ],
        [wide, wide, turned, turned],
        [arr((LEN, HEADS * WIDE), BF16)] * 2 + [arr((HEADS, NF, LEN), BF16)] * 2,
        (ql, pick, pick_t, bias, bias_t),
        flops=4e9,
        moved=10e6,
    )


def forward_kernel(ph_ref, pl_ref, th_ref, tl_ref, num_ref, sp_ref, se_ref, og_ref, gain_ref,
                   out_ref, dh_ref, dl_ref, gs_ref, gt_ref):
    @pl.when(pl.program_id(0) == 0)
    def _():
        gt_ref[...] = jnp.zeros_like(gt_ref)

    for head in range(HEADS):
        part = slice(head * WIDE, (head + 1) * WIDE)
        s_hi, s_lo = halves(padded(sp_ref[0, head] + se_ref[head]))
        num = num_ref[:, cols(head)] + nn3(ph_ref[:, part], pl_ref[:, part], s_hi, s_lo)
        r = lax.rsqrt(jnp.mean(num * num, axis=-1, keepdims=True) + EPS)
        gain = gain_ref[:, cols(head)]
        unit = num * r
        out_ref[:, cols(head)] = unit * gain
        g = og_ref[:, cols(head)] * gain
        d = r * (g - unit * jnp.mean(g * unit, axis=-1, keepdims=True))
        d_hi, d_lo = halves(d)
        dh_ref[:, cols(head)] = d_hi
        dl_ref[:, cols(head)] = d_lo
        own = nn3(th_ref[head], tl_ref[head], d_hi, d_lo)
        gs_ref[0, head] = own
        gt_ref[head] += own


def forward(features, num, sp, se, og, gain):
    rows = lambda c: (c, 0)
    packed, turned = pl.BlockSpec((CHUNK, HEADS * WIDE), rows), pl.BlockSpec((HEADS, NF, CHUNK), lambda c: (0, 0, c))
    wide = pl.BlockSpec((CHUNK, 512), rows)
    states = pl.BlockSpec((1, HEADS, NF, HDIM), lambda c: (c, 0, 0, 0))
    return call(
        forward_kernel,
        (CHUNKS,),
        [packed, packed, turned, turned, wide, states, full(HEADS, NF, HDIM), wide, full(1, 512)],
        [wide, wide, wide, states, full(HEADS, NF, HDIM)],
        [
            arr((LEN, 512)), arr((LEN, 512), BF16), arr((LEN, 512), BF16),
            arr((CHUNKS, HEADS, NF, HDIM)), arr((HEADS, NF, HDIM)),
        ],
        (*features, num, sp, se, og, gain),
        flops=5e9,
        moved=18e6,
    )


def query_kernel(ql_ref, kr_ref, vh_ref, vl_ref, dh_ref, dl_ref, sp_ref, se_ref, pick_ref, bias_ref, back_ref, gq_ref):
    ql, kr = ql_ref[...], kr_ref[...]
    causal = lower()
    gq = jnp.zeros((CHUNK, WIDE), F32)
    du = jnp.zeros((CHUNK, 128), F32)
    for head in range(HEADS):
        mask = head_mask(WIDE, head)
        q = jnp.where(mask, ql, jnp.zeros_like(ql))
        k = jnp.where(mask, kr, jnp.zeros_like(kr))
        v_hi, v_lo = vh_ref[:, cols(head)], vl_ref[:, cols(head)]
        d_hi, d_lo = dh_ref[:, cols(head)], dl_ref[:, cols(head)]
        slope = jnp.where(causal, 1.0 + nt(q, kr), 0.0)
        gq = gq + nn((nt3(d_hi, d_lo, v_hi, v_lo) * slope).astype(BF16), k)
        s_hi, s_lo = halves(padded(sp_ref[0, head] + se_ref[head]))
        dp = nt3(d_hi, d_lo, s_hi, s_lo)
        a, b = factors(ql, pick_ref[head], bias_ref[...])
        dab_hi, dab_lo = halves(side(dp * b, dp * a))
        du = du + nn(dab_hi, back_ref[head]) + nn(dab_lo, back_ref[head])
    gq_ref[...] = gq[:, :128] + gq[:, 128:] + du


def key_kernel(ql_ref, kr_ref, vh_ref, vl_ref, dh_ref, dl_ref, gk_ref, gv_ref):
    ql, kr = ql_ref[...], kr_ref[...]
    row = lax.broadcasted_iota(jnp.int32, (CHUNK, CHUNK), 0)
    col = lax.broadcasted_iota(jnp.int32, (CHUNK, CHUNK), 1)
    causal = col >= row
    gk = jnp.zeros((CHUNK, WIDE), F32)
    for head in range(HEADS):
        mask = head_mask(WIDE, head)
        q = jnp.where(mask, ql, jnp.zeros_like(ql))
        k = jnp.where(mask, kr, jnp.zeros_like(kr))
        v_hi, v_lo = vh_ref[:, cols(head)], vl_ref[:, cols(head)]
        d_hi, d_lo = dh_ref[:, cols(head)], dl_ref[:, cols(head)]
        s = nt(k, ql)
        ds_hi, ds_lo = halves(nt3(v_hi, v_lo, d_hi, d_lo) * jnp.where(causal, 1.0 + s, 0.0))
        gk = gk + nn(ds_hi, q) + nn(ds_lo, q)
        w_hi, w_lo = halves(jnp.where(causal, 1.0 + s + 0.5 * s * s, 0.0))
        gv_ref[:, cols(head)] = nn3(w_hi, w_lo, d_hi, d_lo)
    gk_ref[...] = gk[:, :128] + pltpu.roll(gk[:, :128], 64, 1)


def backward(ql, kr, vh, vl, dh, dl, sp, se, pick, bias, back):
    rows = lambda c: (c, 0)
    narrow, wide = pl.BlockSpec((CHUNK, WIDE), rows), pl.BlockSpec((CHUNK, 512), rows)
    half = pl.BlockSpec((CHUNK, 128), rows)
    states = pl.BlockSpec((1, HEADS, NF, HDIM), lambda c: (c, 0, 0, 0))
    gk, gv = call(
        key_kernel,
        (CHUNKS,),
        [narrow, narrow, wide, wide, wide, wide],
        [half, wide],
        [arr((LEN, 128)), arr((LEN, 512))],
        (ql, kr, vh, vl, dh, dl),
        flops=8e9,
        moved=8e6,
    )
    gq = call(
        query_kernel,
        (CHUNKS,),
        [
            narrow, narrow, wide, wide, wide, wide, states, full(HEADS, NF, HDIM),
            full(HEADS, WIDE, 2 * WIDE), full(1, 2 * WIDE), full(HEADS, 2 * WIDE, 128),
        ],
        half,
        arr((LEN, 128)),
        (ql, kr, vh, vl, dh, dl, sp, se, pick, bias, back),
        flops=8e9,
        moved=8e6,
    )
    return gq, gk, gv


def later_kernel(first, last, kr_ref, vh_ref, vl_ref, gs_ref, gl_ref, gq_ref, gk_ref, gv_ref, pick_ref, bias_ref,
                 back_ref, o_ref, head_ref, total):
    @pl.when(pl.program_id(0) == 0)
    def _():
        begin = gl_ref[...]
        for c in range(CHUNKS - 1, last - 1, -1):
            begin = begin + gs_ref[c]
        total[...] = begin

    kr = kr_ref[...]
    du = jnp.zeros((CHUNK, 128), F32)
    for head in range(HEADS):
        a, b = factors(kr, pick_ref[head], bias_ref[...])
        l_hi, l_lo = halves(padded(total[head]))
        gained = nn((a * b).astype(BF16), side(l_hi, l_lo))
        v_hi, v_lo = vh_ref[:, cols(head)], vl_ref[:, cols(head)]
        o_ref[:, 128 + head * HDIM : 256 + head * HDIM] = gv_ref[:, cols(head)] + gained[:, :HDIM] + gained[:, HDIM:]
        dp = nt(side(v_hi, v_lo), side(l_hi, l_hi))
        dab_hi, dab_lo = halves(side(dp * b, dp * a))
        du = du + nn(dab_hi, back_ref[head]) + nn(dab_lo, back_ref[head])
    low = lax.broadcasted_iota(jnp.int32, (1, 128), 1) < 64
    o_ref[:, :128] = 0.5 * jnp.where(low, gq_ref[...], pltpu.roll(gk_ref[...] + du, 64, 1))
    head_ref[...] = o_ref[:8]
    total[...] += gs_ref[last - 1 - pl.program_id(0)]


def later(first, last, kr, vh, vl, gs, gl, gq, gk, gv, pick, bias, back):
    count = last - first
    rows = lambda c: (last - 1 - c, 0)
    to = lambda c: (count - 1 - c, 0)
    narrow, wide = pl.BlockSpec((CHUNK, WIDE), rows), pl.BlockSpec((CHUNK, 512), rows)
    half = pl.BlockSpec((CHUNK, 128), rows)
    return call(
        functools.partial(later_kernel, first, last),
        (count,),
        [
            narrow, wide, wide, full(CHUNKS, HEADS, NF, HDIM), full(HEADS, NF, HDIM), half, half, wide,
            full(HEADS, WIDE, 2 * WIDE), full(1, 2 * WIDE), full(HEADS, 2 * WIDE, 128),
        ],
        [pl.BlockSpec((CHUNK, 640), to), full(8, 640)],
        [arr((count * CHUNK, 640)), arr((8, 640))],
        (kr, vh, vl, gs, gl, gq, gk, gv, pick, bias, back),
        [pltpu.VMEM((HEADS, NF, HDIM), F32)],
        flops=2e9 * count,
        moved=3e6 * count,
    )


def conv_back(x, tail, taps):
    n = x.shape[0]
    row = lax.broadcasted_iota(jnp.int32, (8, 1), 0)
    once, twice = pltpu.roll(x, n - 1, 0), pltpu.roll(x, n - 2, 0)
    end1 = jnp.where(row == 7, tail[0:1], once[n - 8 :])
    end2 = jnp.where(row == 7, tail[1:2], jnp.where(row == 6, tail[0:1], twice[n - 8 :]))
    once = jnp.concatenate([once[: n - 8], end1], axis=0)
    twice = jnp.concatenate([twice[: n - 8], end2], axis=0)
    return (taps[0:1] * x + taps[1:2] * once + taps[2:3] * twice).astype(BF16)


def f32(x):
    return x.astype(F32)


def flip(x, axis, bit):
    return lax.ppermute(x, axis, [(i, i ^ bit) for i in range(lax.axis_size(axis))])


def input_kernel(a_ref, b_ref, h_ref, t_ref, wv_ref, wqk_ref, o_ref, dt_ref, d_ref):
    @pl.when(pl.program_id(0) == 0)
    def _():
        n = a_ref.shape[0]
        for start in range(0, LEN, STEP):
            end = start + STEP
            src = a_ref[start:end] if start < n else b_ref[start - n : end - n]
            if end == LEN:
                tail = h_ref[...]
            else:
                tail = a_ref[end : end + 8] if end < n else b_ref[end - n : end - n + 8]
            got = conv_back(src, tail, t_ref[...])
            d_ref[start:end] = got
            dt_ref[:, start:end] = got.T

    d = d_ref[...]
    for i in range(o_ref.shape[0]):
        part = slice(512 * i, 512 * (i + 1))
        o_ref[i] = (nt(d[:, 128:], wv_ref[part]) + nn(d[:, :128], wqk_ref[:, part])).astype(BF16)


def input_products(a, b, halo, taps, wv, wqk):
    parts, wide = wv.shape[0] // 512, 2
    n, m = a.shape[0], b.shape[0]
    return call(
        input_kernel,
        (parts // wide,),
        [
            full(n, 640), full(m, 640), full(8, 640), full(3, 640),
            pl.BlockSpec((512 * wide, 512), lambda i: (i, 0)), pl.BlockSpec((128, 512 * wide), lambda i: (0, i)),
        ],
        [pl.BlockSpec((wide, LEN, 512), lambda i: (i, 0, 0)), full(640, LEN)],
        [arr((parts, LEN, 512), BF16), arr((640, LEN), BF16)],
        (a, b, halo, taps, wv, wqk),
        [pltpu.VMEM((LEN, 640), BF16)],
        flops=2 * LEN * 640 * 4096,
        moved=18e6,
    )


def weight_kernel(dest_ref, d_ref, x_ref, theirs_ref, ours_ref):
    got = nn(d_ref[...], x_ref[...]).astype(BF16)
    half = got.shape[1] // 2
    low, high = got[:, :half], got[:, half:]
    first = dest_ref[8] == 0
    theirs_ref[0] = jnp.where(first, high, low)
    ours_ref[0] = jnp.where(first, low, high)


def split_kernel(mine_ref, came_ref, *outs):
    step = pl.program_id(0)
    got = f32(mine_ref[0]) + f32(came_ref[0])
    for j in range(4):

        @pl.when(step // 2 == j)
        def _(j=j):
            outs[j][0] = got.astype(BF16)


def row_sum_kernel(mine_ref, a_ref, b_ref, c_ref, keep_ref, send_ref):
    for r, out in enumerate((keep_ref, send_ref)):
        out[...] = (f32(mine_ref[r]) + f32(a_ref[r]) + f32(b_ref[r]) + f32(c_ref[r])).astype(out.dtype)


def finish_kernel(keep_ref, came_ref, q_ref, k_ref, v_ref):
    step = pl.program_id(0)
    total = keep_ref[...] + f32(came_ref[...])

    @pl.when(step == 0)
    def _():
        q_ref[...] = total[:64]
        k_ref[...] = total[64:]

    @pl.when(step > 0)
    def _():
        v_ref[...] = total.T


def to_x(x, by):
    return lax.ppermute(x, "seq", [(s, s // 8 * 8 + (s % 8 + 2 * by) % 8) for s in range(16)])


def reduce_weight_grad(dt, x, before):
    me = lax.axis_index("seq")
    y, px, core = me // 8, me // 2 % 4, me % 2
    width = x.shape[1] // 16
    chips = [(y ^ r) * 4 + (px + dx) % 4 for dx in range(4) for r in range(2)]
    dest = jnp.stack([*chips, core]).astype(jnp.int32)
    theirs, ours = call(
        weight_kernel,
        (8,),
        [pl.BlockSpec((640, LEN), lambda i, dest: (0, 0)), pl.BlockSpec((LEN, 2 * width), lambda i, dest: (0, dest[i]))],
        [pl.BlockSpec((1, 640, width), lambda i, dest: (i, 0, 0))] * 2,
        [arr((8, 640, width), BF16)] * 2,
        (dest, dt, x),
        prefetch=1,
        after=(before,),
        flops=2 * LEN * 640 * 4096,
        moved=15e6,
    )
    came = flip(theirs, "seq", 1)
    block = pl.BlockSpec((1, 640, width), lambda i: (i, 0, 0))
    parts = call(
        split_kernel,
        (8,),
        [block, block],
        [pl.BlockSpec((1, 640, width), lambda i, j=j: (jnp.clip(i - 2 * j, 0, 1), 0, 0)) for j in range(4)],
        [arr((2, 640, width), BF16)] * 4,
        (ours, came),
        moved=8e6,
    )
    mine, *rest = parts
    rest = [to_x(part, dx) for dx, part in enumerate(rest, 1)]
    pair = pl.BlockSpec((2, 128, width), lambda i: (0, i, 0))
    one = pl.BlockSpec((128, width), lambda i: (i, 0))
    keep, send = call(
        row_sum_kernel,
        (5,),
        [pair] * 4,
        [one] * 2,
        [arr((640, width)), arr((640, width), BF16)],
        (mine, *rest),
        moved=4e6,
    )
    return keep, flip(send, "seq", 8)


def finish_weight_grad(keep, came, before):
    width = keep.shape[1]
    one = pl.BlockSpec((128, width), lambda i: (i, 0))
    return call(
        finish_kernel,
        (5,),
        [one, one],
        [full(64, width), full(64, width), pl.BlockSpec((width, 128), lambda i: (0, jnp.maximum(i - 1, 0)))],
        [arr((64, width)), arr((64, width)), arr((width, 512))],
        (keep, came),
        moved=2e6,
        after=(before,),
    )


def along(x, by):
    n = lax.axis_size("seq")
    return lax.ppermute(x, "seq", [(i, i + by) for i in range(n) if 0 <= i + by < n])


def local(inputs, w_query, w_key, w_value, taps_query, taps_key, taps_value, out_gain, out_grad):
    packed, bias, back = feature_matrices()
    pick_q, pick_k = (jnp.asarray(packed[i], BF16) for i in range(2))
    pick_qt, pick_kt = (jnp.asarray(packed[i].transpose(0, 2, 1), BF16) for i in range(2))
    back_q, back_k = (jnp.asarray(back[i], BF16) for i in range(2))
    bias, bias_t = jnp.asarray(bias), jnp.asarray(bias.T)
    wq_t, wk_t = w_query.T, w_key.T
    taps = jnp.concatenate([taps_query, taps_key, taps_value], axis=1)

    end, tail, wqk_t = project_end(inputs, wq_t, wk_t, w_value)
    tail = along(tail, 1)
    proj = project(inputs, wqk_t, w_value)
    ql, kr, vh, vl, before, own = shard_state(proj, end, tail, taps, pick_kt, bias_t)
    earlier = carried_in(own, False)
    num = inner(ql, kr, vh, vl)
    features = query_features(ql, pick_q, pick_qt, bias, bias_t)
    outputs, dh, dl, grads, own_grad = forward(features, num, before, earlier, out_grad, out_gain.reshape(1, 512))
    after = carried_in(own_grad, True)
    gq, gk, gv = backward(ql, kr, vh, vl, dh, dl, before, earlier, pick_q, bias, back_q)
    rest = (kr, vh, vl, grads, after, gq, gk, gv, pick_k, bias, back_k)
    ga, halo = later(0, 1, *rest)
    halo = along(halo, -1)
    gb, _ = later(1, CHUNKS, *rest)
    blocks, dt = input_products(ga, gb, halo, taps, w_value, wqk_t)
    parts = lax.all_to_all(blocks, "tp", 0, 0)
    input_grad = jnp.sum(parts.astype(F32), axis=0).astype(BF16)
    grad_query, grad_key, grad_value = finish_weight_grad(*reduce_weight_grad(dt, inputs, blocks), input_grad)
    return (outputs, input_grad, grad_query.T, grad_key.T, grad_value)


def solution(mesh):
    return jax.shard_map(
        local,
        mesh=mesh,
        in_specs=(
            P("seq", None),
            P(None, "tp"),
            P(None, "tp"),
            P(None, "tp"),
            P(None, "tp"),
            P(None, "tp"),
            P(None, "tp"),
            P("tp"),
            P("seq", "tp"),
        ),
        out_specs=(P("seq", "tp"), P("seq", "tp"), P("seq", "tp"), P("seq", "tp"), P("seq", "tp")),
        check_vma=False,
    )
```

```python
import functools

import jax
import jax.numpy as jnp
import numpy as np
from jax import lax
from jax.experimental import pallas as pl
from jax.experimental.pallas import tpu as pltpu
from jax.sharding import PartitionSpec as P

FEAT = 16
HDIM = 128
HEADS = 4
CHUNK = 256
LEN = 1024
CHUNKS = LEN // CHUNK
NF = 160
WIDE = 256
EPS = 1e-05
STEP = 128
F32, BF16 = jnp.float32, jnp.bfloat16


def feature_matrices():
    pairs = [(i, j) for i in range(FEAT) for j in range(i, FEAT)]
    pick = np.zeros((2, HEADS, 64, 2 * WIDE), np.float32)
    bias = np.zeros((1, 2 * WIDE), np.float32)
    for head in range(HEADS):
        base = head * FEAT
        for f, (i, j) in enumerate(pairs):
            pick[:, head, base + i, f] = 1.0
            pick[0, head, base + j, WIDE + f] = 0.5 if i == j else 1.0
            pick[1, head, base + j, WIDE + f] = 1.0
        for i in range(FEAT):
            pick[:, head, base + i, len(pairs) + i] = 1.0
    ones = len(pairs) + FEAT
    bias[0, ones] = 1.0
    bias[0, WIDE + len(pairs) : WIDE + ones + 1] = 1.0
    packed = np.zeros((2, HEADS, WIDE, 2 * WIDE), np.float32)
    packed[0, :, 0:64] = pick[0]
    packed[0, :, 64:128] = pick[0]
    packed[1, :, 0:64] = pick[1]
    packed[1, :, 128:192] = pick[1]
    back = np.zeros((2, HEADS, 2 * WIDE, 128), np.float32)
    back[:, :, :, 0:64] = pick.transpose(0, 1, 3, 2)
    return packed, bias, back


def nn(a, b):
    return lax.dot_general(a, b, (((1,), (0,)), ((), ())), preferred_element_type=F32)


def nt(a, b):
    return lax.dot_general(a, b, (((1,), (1,)), ((), ())), preferred_element_type=F32)


def halves(x):
    hi = x.astype(BF16)
    return hi, (x - hi.astype(F32)).astype(BF16)


def side(*parts):
    return jnp.concatenate(parts, axis=1)


def nn3(a_hi, a_lo, b_hi, b_lo):
    both = nn(a_hi, side(b_hi, b_lo))
    n = b_hi.shape[1]
    return both[:, :n] + both[:, n:] + nn(a_lo, b_hi)


def nt3(a_hi, a_lo, b_hi, b_lo):
    return nt(side(a_hi, a_lo), side(b_hi, b_hi)) + nt(a_hi, b_lo)


def factors(packed, pick, bias):
    both = nn(packed, pick) + bias
    return both[:, :WIDE], both[:, WIDE:]


def padded(state):
    return jnp.concatenate([state, jnp.zeros((WIDE - NF, HDIM), F32)], axis=0)


def head_mask(width, head):
    lane = lax.broadcasted_iota(jnp.int32, (1, width), 1)
    return (lane % 64) // FEAT == head


def cols(head):
    return slice(head * HDIM, (head + 1) * HDIM)


def call(body, grid, ins, outs, shapes, args, scratch=(), prefetch=0, flops=0, moved=0, after=()):
    if after:
        kept, skip = body, len(after)
        at = prefetch + len(ins)
        body = lambda *refs: kept(*refs[:at], *refs[at + skip :])
        ins = [*ins] + [pl.BlockSpec(memory_space=pl.ANY)] * skip
        args = (*args, *after)
    return pl.pallas_call(
        body,
        grid_spec=pltpu.PrefetchScalarGridSpec(
            num_scalar_prefetch=prefetch, grid=grid, in_specs=ins, out_specs=outs, scratch_shapes=list(scratch)
        ),
        out_shape=shapes,
        compiler_params=pltpu.CompilerParams(vmem_limit_bytes=56 * 2**20),
        cost_estimate=pl.CostEstimate(flops=int(flops), bytes_accessed=int(moved), transcendentals=0),
    )(*args)


def full(*shape):
    return pl.BlockSpec(shape, lambda *_: (0,) * len(shape))


def arr(shape, dtype=F32):
    return jax.ShapeDtypeStruct(shape, dtype)


def end_kernel(x_ref, wq_ref, wk_ref, wv_ref, o_ref, tail_ref, wqk_ref):
    wqk_ref[0:64] = wq_ref[...]
    wqk_ref[64:128] = wk_ref[...]
    x = x_ref[...]
    o_ref[:, :128] = nt(x, wqk_ref[...])
    o_ref[:, 128:] = nn(x, wv_ref[...])
    tail_ref[...] = o_ref[CHUNK - 8 :]


def project_end(x, wq_t, wk_t, wv):
    depth = x.shape[1]
    return call(
        end_kernel,
        (1,),
        [pl.BlockSpec((CHUNK, depth), lambda c: (CHUNKS - 1, 0)), full(64, depth), full(64, depth), full(depth, 512)],
        [full(CHUNK, 640), full(8, 640), full(128, depth)],
        [arr((CHUNK, 640)), arr((8, 640)), arr((128, depth), BF16)],
        (x, wq_t, wk_t, wv),
        flops=2 * CHUNK * depth * 640,
        moved=8e6,
    )


def project_kernel(x_ref, wqk_ref, wv_ref, o_ref):
    x = x_ref[...]
    o_ref[:, :128] = nt(x, wqk_ref[...])
    o_ref[:, 128:] = nn(x, wv_ref[...])


def project(x, wqk_t, wv):
    depth = x.shape[1]
    rows = lambda c: (c, 0)
    return call(
        project_kernel,
        (CHUNKS - 1,),
        [pl.BlockSpec((CHUNK, depth), rows), full(128, depth), full(depth, 512)],
        pl.BlockSpec((CHUNK, 640), rows),
        arr((LEN - CHUNK, 640)),
        (x, wqk_t, wv),
        flops=2 * (LEN - CHUNK) * depth * 640,
        moved=12e6,
    )


def conv(x, tail, taps):
    row = lax.broadcasted_iota(jnp.int32, (8, 1), 0)
    once, twice = pltpu.roll(x, 1, 0), pltpu.roll(x, 2, 0)
    top1 = jnp.where(row == 0, tail[7:8], once[0:8])
    top2 = jnp.where(row == 0, tail[6:7], jnp.where(row == 1, tail[7:8], twice[0:8]))
    once = jnp.concatenate([top1, once[8:]], axis=0)
    twice = jnp.concatenate([top2, twice[8:]], axis=0)
    return taps[0:1] * x + taps[1:2] * once + taps[2:3] * twice


def state_kernel(
    a_ref, b_ref, before_ref, tail_ref, taps_ref, pick_ref, biast_ref,
    ql_ref, kr_ref, vh_ref, vl_ref, sp_ref, st_ref,
):
    c = pl.program_id(0)

    @pl.when(c == 0)
    def _():
        st_ref[...] = jnp.zeros_like(st_ref)

    x = jnp.where(c < CHUNKS - 1, a_ref[...], b_ref[...])
    both = conv(x, jnp.where(c > 0, before_ref[...], tail_ref[...]), taps_ref[...])
    qk, v = both[:, :128] * 0.5, both[:, 128:]
    lane = lax.broadcasted_iota(jnp.int32, (1, 128), 1)
    low = lane < 64
    turned = pltpu.roll(qk, 64, 1)
    hi = qk.astype(BF16).astype(F32)
    lo = qk - hi
    turned_hi = turned.astype(BF16).astype(F32)
    turned_lo = turned - turned_hi
    zero = jnp.zeros_like(qk)
    ql = side(jnp.where(low, hi, turned_lo), jnp.where(low, hi, zero)).astype(BF16)
    kr = side(jnp.where(low, turned_hi, hi), jnp.where(low, turned_lo, zero)).astype(BF16)
    ql_ref[...] = ql
    kr_ref[...] = kr
    v_hi, v_lo = halves(v)
    vh_ref[...] = v_hi
    vl_ref[...] = v_lo
    for head in range(HEADS):
        ab = nt(pick_ref[head], kr) + biast_ref[...]
        p_hi, p_lo = halves(ab[:NF] * ab[WIDE : WIDE + NF])
        own = nn3(p_hi, p_lo, v_hi[:, cols(head)], v_lo[:, cols(head)])
        sp_ref[0, head] = st_ref[head]
        st_ref[head] += own


def shard_state(proj, end, tail, taps, pick_kt, bias_t):
    rows = lambda c: (c, 0)
    before = lambda c: (jnp.maximum(c * (CHUNK // 8) - 1, 0), 0)
    return call(
        state_kernel,
        (CHUNKS,),
        [
            pl.BlockSpec((CHUNK, 640), lambda c: (jnp.minimum(c, CHUNKS - 2), 0)),
            full(CHUNK, 640),
            pl.BlockSpec((8, 640), before),
            full(8, 640),
            full(3, 640),
            full(HEADS, 2 * WIDE, WIDE),
            full(2 * WIDE, 1),
        ],
        [
            pl.BlockSpec((CHUNK, WIDE), rows),
            pl.BlockSpec((CHUNK, WIDE), rows),
            pl.BlockSpec((CHUNK, 512), rows),
            pl.BlockSpec((CHUNK, 512), rows),
            pl.BlockSpec((1, HEADS, NF, HDIM), lambda c: (c, 0, 0, 0)),
            full(HEADS, NF, HDIM),
        ],
        [
            arr((LEN, WIDE), BF16),
            arr((LEN, WIDE), BF16),
            arr((LEN, 512), BF16),
            arr((LEN, 512), BF16),
            arr((CHUNKS, HEADS, NF, HDIM)),
            arr((HEADS, NF, HDIM)),
        ],
        (proj, end, proj, tail, taps, pick_kt, bias_t),
        flops=4e9,
        moved=15e6,
    )


def running_kernel(backward, x_ref, o_ref):
    count = x_ref.shape[0]
    order = range(count - 1, -1, -1) if backward else range(count)
    total = jnp.zeros(x_ref.shape[1:], F32)
    for i in order:
        o_ref[i] = total
        total = total + x_ref[i]


def carried_in(state, backward):
    count = lax.axis_size("seq")
    rows = HEADS * NF // count
    pieces = lax.all_to_all(state.reshape(count, rows, HDIM), "seq", 0, 0)
    shape = (count, rows, HDIM)
    sums = call(
        functools.partial(running_kernel, backward), (1,), [full(*shape)], full(*shape), arr(shape), (pieces,), moved=6e5
    )
    return lax.all_to_all(sums, "seq", 0, 0).reshape(HEADS, NF, HDIM)


def lower():
    row = lax.broadcasted_iota(jnp.int32, (CHUNK, CHUNK), 0)
    col = lax.broadcasted_iota(jnp.int32, (CHUNK, CHUNK), 1)
    return row >= col


def inner_kernel(ql_ref, kr_ref, vh_ref, vl_ref, num_ref):
    ql, kr = ql_ref[...], kr_ref[...]
    causal = lower()
    for head in range(HEADS):
        mine = jnp.where(head_mask(WIDE, head), ql, jnp.zeros_like(ql))
        s = nt(mine, kr)
        w_hi, w_lo = halves(jnp.where(causal, 1.0 + s + 0.5 * s * s, 0.0))
        num_ref[:, cols(head)] = nn3(w_hi, w_lo, vh_ref[:, cols(head)], vl_ref[:, cols(head)])


def inner(ql, kr, vh, vl):
    rows = lambda c: (c, 0)
    narrow, wide = pl.BlockSpec((CHUNK, WIDE), rows), pl.BlockSpec((CHUNK, 512), rows)
    return call(
        inner_kernel, (CHUNKS,), [narrow, narrow, wide, wide], wide, arr((LEN, 512)), (ql, kr, vh, vl), flops=6e9, moved=6e6
    )


def feature_kernel(ql_ref, pick_ref, pickt_ref, bias_ref, biast_ref, ph_ref, pl_ref, th_ref, tl_ref):
    ql = ql_ref[...]
    for head in range(HEADS):
        part = slice(head * WIDE, (head + 1) * WIDE)
        a, b = factors(ql, pick_ref[head], bias_ref[...])
        ph_ref[:, part], pl_ref[:, part] = halves(a * b)
        ab = nt(pickt_ref[head], ql) + biast_ref[...]
        th_ref[head], tl_ref[head] = halves(ab[:NF] * ab[WIDE : WIDE + NF])


def query_features(ql, pick, pick_t, bias, bias_t):
    rows = lambda c: (c, 0)
    wide, turned = pl.BlockSpec((CHUNK, HEADS * WIDE), rows), pl.BlockSpec((HEADS, NF, CHUNK), lambda c: (0, 0, c))
    return call(
        feature_kernel,
        (CHUNKS,),
        [
            pl.BlockSpec((CHUNK, WIDE), rows),
            full(HEADS, WIDE, 2 * WIDE), full(HEADS, 2 * WIDE, WIDE), full(1, 2 * WIDE), full(2 * WIDE, 1),
        ],
        [wide, wide, turned, turned],
        [arr((LEN, HEADS * WIDE), BF16)] * 2 + [arr((HEADS, NF, LEN), BF16)] * 2,
        (ql, pick, pick_t, bias, bias_t),
        flops=4e9,
        moved=10e6,
    )


def forward_kernel(ph_ref, pl_ref, th_ref, tl_ref, num_ref, sp_ref, se_ref, og_ref, gain_ref,
                   out_ref, dh_ref, dl_ref, gs_ref, gt_ref):
    @pl.when(pl.program_id(0) == 0)
    def _():
        gt_ref[...] = jnp.zeros_like(gt_ref)

    for head in range(HEADS):
        part = slice(head * WIDE, (head + 1) * WIDE)
        s_hi, s_lo = halves(padded(sp_ref[0, head] + se_ref[head]))
        num = num_ref[:, cols(head)] + nn3(ph_ref[:, part], pl_ref[:, part], s_hi, s_lo)
        r = lax.rsqrt(jnp.mean(num * num, axis=-1, keepdims=True) + EPS)
        gain = gain_ref[:, cols(head)]
        unit = num * r
        out_ref[:, cols(head)] = unit * gain
        g = og_ref[:, cols(head)] * gain
        d = r * (g - unit * jnp.mean(g * unit, axis=-1, keepdims=True))
        d_hi, d_lo = halves(d)
        dh_ref[:, cols(head)] = d_hi
        dl_ref[:, cols(head)] = d_lo
        own = nn3(th_ref[head], tl_ref[head], d_hi, d_lo)
        gs_ref[0, head] = own
        gt_ref[head] += own


def forward(features, num, sp, se, og, gain):
    rows = lambda c: (c, 0)
    packed, turned = pl.BlockSpec((CHUNK, HEADS * WIDE), rows), pl.BlockSpec((HEADS, NF, CHUNK), lambda c: (0, 0, c))
    wide = pl.BlockSpec((CHUNK, 512), rows)
    states = pl.BlockSpec((1, HEADS, NF, HDIM), lambda c: (c, 0, 0, 0))
    return call(
        forward_kernel,
        (CHUNKS,),
        [packed, packed, turned, turned, wide, states, full(HEADS, NF, HDIM), wide, full(1, 512)],
        [wide, wide, wide, states, full(HEADS, NF, HDIM)],
        [
            arr((LEN, 512)), arr((LEN, 512), BF16), arr((LEN, 512), BF16),
            arr((CHUNKS, HEADS, NF, HDIM)), arr((HEADS, NF, HDIM)),
        ],
        (*features, num, sp, se, og, gain),
        flops=5e9,
        moved=18e6,
    )


def query_kernel(ql_ref, kr_ref, vh_ref, vl_ref, dh_ref, dl_ref, sp_ref, se_ref, pick_ref, bias_ref, back_ref, gq_ref):
    ql, kr = ql_ref[...], kr_ref[...]
    causal = lower()
    gq = jnp.zeros((CHUNK, WIDE), F32)
    du = jnp.zeros((CHUNK, 128), F32)
    for head in range(HEADS):
        mask = head_mask(WIDE, head)
        q = jnp.where(mask, ql, jnp.zeros_like(ql))
        k = jnp.where(mask, kr, jnp.zeros_like(kr))
        v_hi, v_lo = vh_ref[:, cols(head)], vl_ref[:, cols(head)]
        d_hi, d_lo = dh_ref[:, cols(head)], dl_ref[:, cols(head)]
        slope = jnp.where(causal, 1.0 + nt(q, kr), 0.0)
        gq = gq + nn((nt3(d_hi, d_lo, v_hi, v_lo) * slope).astype(BF16), k)
        s_hi, s_lo = halves(padded(sp_ref[0, head] + se_ref[head]))
        dp = nt3(d_hi, d_lo, s_hi, s_lo)
        a, b = factors(ql, pick_ref[head], bias_ref[...])
        dab_hi, dab_lo = halves(side(dp * b, dp * a))
        du = du + nn(dab_hi, back_ref[head]) + nn(dab_lo, back_ref[head])
    gq_ref[...] = gq[:, :128] + gq[:, 128:] + du


def key_kernel(ql_ref, kr_ref, vh_ref, vl_ref, dh_ref, dl_ref, gk_ref, gv_ref):
    ql, kr = ql_ref[...], kr_ref[...]
    row = lax.broadcasted_iota(jnp.int32, (CHUNK, CHUNK), 0)
    col = lax.broadcasted_iota(jnp.int32, (CHUNK, CHUNK), 1)
    causal = col >= row
    gk = jnp.zeros((CHUNK, WIDE), F32)
    for head in range(HEADS):
        mask = head_mask(WIDE, head)
        q = jnp.where(mask, ql, jnp.zeros_like(ql))
        k = jnp.where(mask, kr, jnp.zeros_like(kr))
        v_hi, v_lo = vh_ref[:, cols(head)], vl_ref[:, cols(head)]
        d_hi, d_lo = dh_ref[:, cols(head)], dl_ref[:, cols(head)]
        s = nt(k, ql)
        ds_hi, ds_lo = halves(nt3(v_hi, v_lo, d_hi, d_lo) * jnp.where(causal, 1.0 + s, 0.0))
        gk = gk + nn(ds_hi, q) + nn(ds_lo, q)
        w_hi, w_lo = halves(jnp.where(causal, 1.0 + s + 0.5 * s * s, 0.0))
        gv_ref[:, cols(head)] = nn3(w_hi, w_lo, d_hi, d_lo)
    gk_ref[...] = gk[:, :128] + pltpu.roll(gk[:, :128], 64, 1)


def backward(ql, kr, vh, vl, dh, dl, sp, se, pick, bias, back):
    rows = lambda c: (c, 0)
    narrow, wide = pl.BlockSpec((CHUNK, WIDE), rows), pl.BlockSpec((CHUNK, 512), rows)
    half = pl.BlockSpec((CHUNK, 128), rows)
    states = pl.BlockSpec((1, HEADS, NF, HDIM), lambda c: (c, 0, 0, 0))
    gk, gv = call(
        key_kernel,
        (CHUNKS,),
        [narrow, narrow, wide, wide, wide, wide],
        [half, wide],
        [arr((LEN, 128)), arr((LEN, 512))],
        (ql, kr, vh, vl, dh, dl),
        flops=8e9,
        moved=8e6,
    )
    gq = call(
        query_kernel,
        (CHUNKS,),
        [
            narrow, narrow, wide, wide, wide, wide, states, full(HEADS, NF, HDIM),
            full(HEADS, WIDE, 2 * WIDE), full(1, 2 * WIDE), full(HEADS, 2 * WIDE, 128),
        ],
        half,
        arr((LEN, 128)),
        (ql, kr, vh, vl, dh, dl, sp, se, pick, bias, back),
        flops=8e9,
        moved=8e6,
    )
    return gq, gk, gv


def later_kernel(first, last, kr_ref, vh_ref, vl_ref, gs_ref, gl_ref, gq_ref, gk_ref, gv_ref, pick_ref, bias_ref,
                 back_ref, o_ref, head_ref, total):
    @pl.when(pl.program_id(0) == 0)
    def _():
        begin = gl_ref[...]
        for c in range(CHUNKS - 1, last - 1, -1):
            begin = begin + gs_ref[c]
        total[...] = begin

    kr = kr_ref[...]
    du = jnp.zeros((CHUNK, 128), F32)
    for head in range(HEADS):
        a, b = factors(kr, pick_ref[head], bias_ref[...])
        l_hi, l_lo = halves(padded(total[head]))
        gained = nn((a * b).astype(BF16), side(l_hi, l_lo))
        v_hi, v_lo = vh_ref[:, cols(head)], vl_ref[:, cols(head)]
        o_ref[:, 128 + head * HDIM : 256 + head * HDIM] = gv_ref[:, cols(head)] + gained[:, :HDIM] + gained[:, HDIM:]
        dp = nt(side(v_hi, v_lo), side(l_hi, l_hi))
        dab_hi, dab_lo = halves(side(dp * b, dp * a))
        du = du + nn(dab_hi, back_ref[head]) + nn(dab_lo, back_ref[head])
    low = lax.broadcasted_iota(jnp.int32, (1, 128), 1) < 64
    o_ref[:, :128] = 0.5 * jnp.where(low, gq_ref[...], pltpu.roll(gk_ref[...] + du, 64, 1))
    head_ref[...] = o_ref[:8]
    total[...] += gs_ref[last - 1 - pl.program_id(0)]


def later(first, last, kr, vh, vl, gs, gl, gq, gk, gv, pick, bias, back):
    count = last - first
    rows = lambda c: (last - 1 - c, 0)
    to = lambda c: (count - 1 - c, 0)
    narrow, wide = pl.BlockSpec((CHUNK, WIDE), rows), pl.BlockSpec((CHUNK, 512), rows)
    half = pl.BlockSpec((CHUNK, 128), rows)
    return call(
        functools.partial(later_kernel, first, last),
        (count,),
        [
            narrow, wide, wide, full(CHUNKS, HEADS, NF, HDIM), full(HEADS, NF, HDIM), half, half, wide,
            full(HEADS, WIDE, 2 * WIDE), full(1, 2 * WIDE), full(HEADS, 2 * WIDE, 128),
        ],
        [pl.BlockSpec((CHUNK, 640), to), full(8, 640)],
        [arr((count * CHUNK, 640)), arr((8, 640))],
        (kr, vh, vl, gs, gl, gq, gk, gv, pick, bias, back),
        [pltpu.VMEM((HEADS, NF, HDIM), F32)],
        flops=2e9 * count,
        moved=3e6 * count,
    )


def conv_back(x, tail, taps):
    n = x.shape[0]
    row = lax.broadcasted_iota(jnp.int32, (8, 1), 0)
    once, twice = pltpu.roll(x, n - 1, 0), pltpu.roll(x, n - 2, 0)
    end1 = jnp.where(row == 7, tail[0:1], once[n - 8 :])
    end2 = jnp.where(row == 7, tail[1:2], jnp.where(row == 6, tail[0:1], twice[n - 8 :]))
    once = jnp.concatenate([once[: n - 8], end1], axis=0)
    twice = jnp.concatenate([twice[: n - 8], end2], axis=0)
    return (taps[0:1] * x + taps[1:2] * once + taps[2:3] * twice).astype(BF16)


def f32(x):
    return x.astype(F32)


def flip(x, axis, bit):
    return lax.ppermute(x, axis, [(i, i ^ bit) for i in range(lax.axis_size(axis))])


def input_kernel(me_ref, a_ref, b_ref, h_ref, t_ref, wv_ref, wqk_ref, z_ref, keep_ref, send_ref, dt_ref, d_ref):
    @pl.when(pl.program_id(0) == 0)
    def _():
        n = a_ref.shape[0]
        for start in range(0, LEN, STEP):
            end = start + STEP
            src = a_ref[start:end] if start < n else b_ref[start - n : end - n]
            if end == LEN:
                tail = h_ref[...]
            else:
                tail = a_ref[end : end + 8] if end < n else b_ref[end - n : end - n + 8]
            got = conv_back(src, tail, t_ref[...])
            d_ref[start:end] = got
            dt_ref[:, start:end] = got.T

    d = d_ref[...]
    half = LEN // 2
    bottom = []
    for i in range(2):
        part = slice(512 * i, 512 * (i + 1))
        got = nt(d[:, 128:], wv_ref[part]) + nn(d[:, :128], wqk_ref[:, part])
        z_ref[0, i] = got[:half].astype(BF16)
        bottom.append(got[half:])
    first = me_ref[0] == 0
    keep_ref[0] = jnp.where(first, bottom[0], bottom[1])
    send_ref[0] = jnp.where(first, bottom[1], bottom[0]).astype(BF16)


def input_products(side_y, a, b, halo, taps, wv, wqk):
    n, m, half = a.shape[0], b.shape[0], LEN // 2
    const = lambda *shape: pl.BlockSpec(shape, lambda i, me: (0,) * len(shape))
    block = pl.BlockSpec((1, half, 512), lambda i, me: (i, 0, 0))
    return call(
        input_kernel,
        (4,),
        [
            const(n, 640), const(m, 640), const(8, 640), const(3, 640),
            pl.BlockSpec((1024, 512), lambda i, me: (i, 0)), pl.BlockSpec((128, 1024), lambda i, me: (0, i)),
        ],
        [pl.BlockSpec((1, 2, half, 512), lambda i, me: (i, 0, 0, 0)), block, block, const(640, LEN)],
        [arr((4, 2, half, 512), BF16), arr((4, half, 512)), arr((4, half, 512), BF16), arr((640, LEN), BF16)],
        (side_y, a, b, halo, taps, wv, wqk),
        [pltpu.VMEM((LEN, 640), BF16)],
        prefetch=1,
        flops=2 * LEN * 640 * 4096,
        moved=20e6,
    )


def pair_kernel(keep_ref, came_ref, o_ref):
    o_ref[...] = (keep_ref[...] + f32(came_ref[...])).astype(BF16)


def top_kernel(me_ref, p_ref, keep_ref, send_ref):
    total = f32(p_ref[0])
    for i in range(1, 4):
        total = total + f32(p_ref[i])
    first = me_ref[0] == 0
    keep_ref[...] = jnp.where(first, total[0], total[1])
    send_ref[...] = jnp.where(first, total[1], total[0]).astype(BF16)


def last_kernel(keep_ref, came_ref, p_ref, o_ref):
    @pl.when(pl.program_id(0) < 2)
    def _():
        o_ref[...] = (keep_ref[...] + f32(came_ref[...])).astype(BF16)

    @pl.when(pl.program_id(0) >= 2)
    def _():
        total = f32(p_ref[0])
        for i in range(1, 4):
            total = total + f32(p_ref[i])
        o_ref[...] = total.astype(BF16)


def along_z(x):
    return lax.all_to_all(x, "tp", 0, 0, axis_index_groups=[[0, 2, 4, 6], [1, 3, 5, 7]])


def reduce_input_grad(side_y, by_z, keep, send, before):
    half, tile = LEN // 2, LEN // 4
    came = flip(send, "tp", 1)
    tops = along_z(by_z)
    block = pl.BlockSpec((1, half, 512), lambda i: (i, 0, 0))
    pairs = call(pair_kernel, (4,), [block, block], block, arr((4, half, 512), BF16), (keep, came), moved=8e6, after=(before,))
    rows = pl.BlockSpec((tile // 2, 512), lambda i, me: (i, 0))
    keep, send = call(
        top_kernel,
        (4,),
        [pl.BlockSpec((4, 2, tile // 2, 512), lambda i, me: (0, 0, i, 0))],
        [rows, rows],
        [arr((half, 512)), arr((half, 512), BF16)],
        (side_y, tops),
        prefetch=1,
        moved=6e6,
    )
    pairs = along_z(pairs)
    came = flip(send, "tp", 1)
    top = pl.BlockSpec((tile, 512), lambda i: (jnp.minimum(i, 1), 0))
    return call(
        last_kernel,
        (4,),
        [top, top, pl.BlockSpec((4, tile, 512), lambda i: (0, jnp.maximum(i - 2, 0), 0))],
        pl.BlockSpec((tile, 512), lambda i: (i, 0)),
        arr((LEN, 512), BF16),
        (keep, came, pairs),
        moved=5e6,
    )


def weight_kernel(dest_ref, d_ref, x_ref, y_ref, theirs_ref, ours_ref):
    first = dest_ref[8] == 0
    for r, ref in enumerate((x_ref, y_ref)):
        got = nn(d_ref[...], ref[...]).astype(BF16)
        half = got.shape[1] // 2
        low, high = got[:, :half], got[:, half:]
        theirs_ref[r] = jnp.where(first, high, low)
        ours_ref[r] = jnp.where(first, low, high)


def split_kernel(mine_ref, came_ref, *outs):
    step = pl.program_id(0)
    got = (f32(mine_ref[...]) + f32(came_ref[...])).astype(BF16)
    for j in range(4):

        @pl.when(step == j)
        def _(j=j):
            outs[j][...] = got


def row_sum_kernel(mine_ref, a_ref, b_ref, c_ref, keep_ref, send_ref):
    for r, out in enumerate((keep_ref, send_ref)):
        out[...] = (f32(mine_ref[r]) + f32(a_ref[r]) + f32(b_ref[r]) + f32(c_ref[r])).astype(out.dtype)


def finish_kernel(keep_ref, came_ref, q_ref, k_ref, v_ref):
    step = pl.program_id(0)
    total = keep_ref[...] + f32(came_ref[...])

    @pl.when(step == 0)
    def _():
        q_ref[...] = total[:64]
        k_ref[...] = total[64:]

    @pl.when(step > 0)
    def _():
        v_ref[...] = total.T


def to_x(x, by):
    return lax.ppermute(x, "seq", [(s, s // 8 * 8 + (s % 8 + 2 * by) % 8) for s in range(16)])


def weight_parts(dt, x):
    me = lax.axis_index("seq")
    y, px, core = me // 8, me // 2 % 4, me % 2
    width = x.shape[1] // 16
    chips = [(y ^ r) * 4 + (px + dx) % 4 for dx in range(4) for r in range(2)]
    dest = jnp.stack([*chips, core]).astype(jnp.int32)
    theirs, ours = call(
        weight_kernel,
        (4,),
        [pl.BlockSpec((640, LEN), lambda i, dest: (0, 0))]
        + [pl.BlockSpec((LEN, 2 * width), lambda i, dest, r=r: (0, dest[2 * i + r])) for r in range(2)],
        [pl.BlockSpec((2, 640, width), lambda i, dest: (i, 0, 0))] * 2,
        [arr((8, 640, width), BF16)] * 2,
        (dest, dt, x, x),
        prefetch=1,
        flops=2 * LEN * 640 * 4096,
        moved=15e6,
    )
    came = flip(theirs, "seq", 1)
    block = pl.BlockSpec((2, 640, width), lambda i: (i, 0, 0))
    return call(
        split_kernel,
        (4,),
        [block, block],
        [full(2, 640, width)] * 4,
        [arr((2, 640, width), BF16)] * 4,
        (ours, came),
        moved=8e6,
    )


def reduce_weight_grad(parts):
    mine, *rest = parts
    width = mine.shape[2]
    pair = pl.BlockSpec((2, 128, width), lambda i: (0, i, 0))
    one = pl.BlockSpec((128, width), lambda i: (i, 0))
    keep, send = call(
        row_sum_kernel,
        (5,),
        [pair] * 4,
        [one] * 2,
        [arr((640, width)), arr((640, width), BF16)],
        (mine, *rest),
        moved=4e6,
    )
    return keep, flip(send, "seq", 8)


def finish_weight_grad(keep, came):
    width = keep.shape[1]
    one = pl.BlockSpec((128, width), lambda i: (i, 0))
    return call(
        finish_kernel,
        (5,),
        [one, one],
        [full(64, width), full(64, width), pl.BlockSpec((width, 128), lambda i: (0, jnp.maximum(i - 1, 0)))],
        [arr((64, width)), arr((64, width)), arr((width, 512))],
        (keep, came),
        moved=2e6,
    )


def along(x, by):
    n = lax.axis_size("seq")
    return lax.ppermute(x, "seq", [(i, i + by) for i in range(n) if 0 <= i + by < n])


def local(inputs, w_query, w_key, w_value, taps_query, taps_key, taps_value, out_gain, out_grad):
    packed, bias, back = feature_matrices()
    pick_q, pick_k = (jnp.asarray(packed[i], BF16) for i in range(2))
    pick_qt, pick_kt = (jnp.asarray(packed[i].transpose(0, 2, 1), BF16) for i in range(2))
    back_q, back_k = (jnp.asarray(back[i], BF16) for i in range(2))
    bias, bias_t = jnp.asarray(bias), jnp.asarray(bias.T)
    wq_t, wk_t = w_query.T, w_key.T
    taps = jnp.concatenate([taps_query, taps_key, taps_value], axis=1)

    end, tail, wqk_t = project_end(inputs, wq_t, wk_t, w_value)
    tail = along(tail, 1)
    proj = project(inputs, wqk_t, w_value)
    ql, kr, vh, vl, before, own = shard_state(proj, end, tail, taps, pick_kt, bias_t)
    earlier = carried_in(own, False)
    num = inner(ql, kr, vh, vl)
    features = query_features(ql, pick_q, pick_qt, bias, bias_t)
    outputs, dh, dl, grads, own_grad = forward(features, num, before, earlier, out_grad, out_gain.reshape(1, 512))
    after = carried_in(own_grad, True)
    gq, gk, gv = backward(ql, kr, vh, vl, dh, dl, before, earlier, pick_q, bias, back_q)
    rest = (kr, vh, vl, grads, after, gq, gk, gv, pick_k, bias, back_k)
    ga, halo = later(0, 1, *rest)
    halo = along(halo, -1)
    gb, _ = later(1, CHUNKS, *rest)
    side_y = (lax.axis_index("tp") % 2).astype(jnp.int32).reshape(1)
    by_z, keep, send, dt = input_products(side_y, ga, gb, halo, taps, w_value, wqk_t)
    mine, *rest = weight_parts(dt, inputs)
    parts = [mine, *(to_x(part, dx) for dx, part in enumerate(rest, 1))]
    own, came = reduce_weight_grad(parts)
    input_grad = reduce_input_grad(side_y, by_z, keep, send, own)
    grad_query, grad_key, grad_value = finish_weight_grad(own, came)
    return (outputs, input_grad, grad_query.T, grad_key.T, grad_value)


def solution(mesh):
    return jax.shard_map(
        local,
        mesh=mesh,
        in_specs=(
            P("seq", None),
            P(None, "tp"),
            P(None, "tp"),
            P(None, "tp"),
            P(None, "tp"),
            P(None, "tp"),
            P(None, "tp"),
            P("tp"),
            P("seq", "tp"),
        ),
        out_specs=(P("seq", "tp"), P("seq", "tp"), P("seq", "tp"), P("seq", "tp"), P("seq", "tp")),
        check_vma=False,
    )
```

```python
import functools

import jax
import jax.numpy as jnp
import numpy as np
from jax import lax
from jax.experimental import pallas as pl
from jax.experimental.pallas import tpu as pltpu
from jax.sharding import PartitionSpec as P

FEAT = 16
HDIM = 128
HEADS = 4
CHUNK = 256
LEN = 1024
CHUNKS = LEN // CHUNK
NF = 160
WIDE = 256
EPS = 1e-05
STEP = 128
F32, BF16 = jnp.float32, jnp.bfloat16


def feature_matrices():
    pairs = [(i, j) for i in range(FEAT) for j in range(i, FEAT)]
    pick = np.zeros((2, HEADS, 64, 2 * WIDE), np.float32)
    bias = np.zeros((1, 2 * WIDE), np.float32)
    for head in range(HEADS):
        base = head * FEAT
        for f, (i, j) in enumerate(pairs):
            pick[:, head, base + i, f] = 1.0
            pick[0, head, base + j, WIDE + f] = 0.5 if i == j else 1.0
            pick[1, head, base + j, WIDE + f] = 1.0
        for i in range(FEAT):
            pick[:, head, base + i, len(pairs) + i] = 1.0
    ones = len(pairs) + FEAT
    bias[0, ones] = 1.0
    bias[0, WIDE + len(pairs) : WIDE + ones + 1] = 1.0
    packed = np.zeros((2, HEADS, WIDE, 2 * WIDE), np.float32)
    packed[0, :, 0:64] = pick[0]
    packed[0, :, 64:128] = pick[0]
    packed[1, :, 0:64] = pick[1]
    packed[1, :, 128:192] = pick[1]
    back = np.zeros((2, HEADS, 2 * WIDE, 128), np.float32)
    back[:, :, :, 0:64] = pick.transpose(0, 1, 3, 2)
    return packed, bias, back


def nn(a, b):
    return lax.dot_general(a, b, (((1,), (0,)), ((), ())), preferred_element_type=F32)


def nt(a, b):
    return lax.dot_general(a, b, (((1,), (1,)), ((), ())), preferred_element_type=F32)


def halves(x):
    hi = x.astype(BF16)
    return hi, (x - hi.astype(F32)).astype(BF16)


def side(*parts):
    return jnp.concatenate(parts, axis=1)


def nn3(a_hi, a_lo, b_hi, b_lo):
    both = nn(a_hi, side(b_hi, b_lo))
    n = b_hi.shape[1]
    return both[:, :n] + both[:, n:] + nn(a_lo, b_hi)


def nt3(a_hi, a_lo, b_hi, b_lo):
    return nt(side(a_hi, a_lo), side(b_hi, b_hi)) + nt(a_hi, b_lo)


def factors(packed, pick, bias):
    both = nn(packed, pick) + bias
    return both[:, :WIDE], both[:, WIDE:]


def padded(state):
    return jnp.concatenate([state, jnp.zeros((WIDE - NF, HDIM), F32)], axis=0)


def head_mask(width, head):
    lane = lax.broadcasted_iota(jnp.int32, (1, width), 1)
    return (lane % 64) // FEAT == head


def cols(head):
    return slice(head * HDIM, (head + 1) * HDIM)


def call(body, grid, ins, outs, shapes, args, scratch=(), prefetch=0, flops=0, moved=0, after=()):
    if after:
        kept, skip = body, len(after)
        at = prefetch + len(ins)
        body = lambda *refs: kept(*refs[:at], *refs[at + skip :])
        ins = [*ins] + [pl.BlockSpec(memory_space=pl.ANY)] * skip
        args = (*args, *after)
    return pl.pallas_call(
        body,
        grid_spec=pltpu.PrefetchScalarGridSpec(
            num_scalar_prefetch=prefetch, grid=grid, in_specs=ins, out_specs=outs, scratch_shapes=list(scratch)
        ),
        out_shape=shapes,
        compiler_params=pltpu.CompilerParams(vmem_limit_bytes=56 * 2**20),
        cost_estimate=pl.CostEstimate(flops=int(flops), bytes_accessed=int(moved), transcendentals=0),
    )(*args)


def full(*shape):
    return pl.BlockSpec(shape, lambda *_: (0,) * len(shape))


def arr(shape, dtype=F32):
    return jax.ShapeDtypeStruct(shape, dtype)


def end_kernel(x_ref, wq_ref, wk_ref, wv_ref, o_ref, tail_ref, wqk_ref):
    wqk_ref[0:64] = wq_ref[...]
    wqk_ref[64:128] = wk_ref[...]
    x = x_ref[...]
    o_ref[:, :128] = nt(x, wqk_ref[...])
    o_ref[:, 128:] = nn(x, wv_ref[...])
    tail_ref[...] = o_ref[CHUNK - 8 :]


def project_end(x, wq_t, wk_t, wv):
    depth = x.shape[1]
    return call(
        end_kernel,
        (1,),
        [pl.BlockSpec((CHUNK, depth), lambda c: (CHUNKS - 1, 0)), full(64, depth), full(64, depth), full(depth, 512)],
        [full(CHUNK, 640), full(8, 640), full(128, depth)],
        [arr((CHUNK, 640)), arr((8, 640)), arr((128, depth), BF16)],
        (x, wq_t, wk_t, wv),
        flops=2 * CHUNK * depth * 640,
        moved=8e6,
    )


def project_kernel(x_ref, wqk_ref, wv_ref, o_ref):
    x = x_ref[...]
    o_ref[:, :128] = nt(x, wqk_ref[...])
    o_ref[:, 128:] = nn(x, wv_ref[...])


def project(x, wqk_t, wv):
    depth = x.shape[1]
    rows = lambda c: (c, 0)
    return call(
        project_kernel,
        (CHUNKS - 1,),
        [pl.BlockSpec((CHUNK, depth), rows), full(128, depth), full(depth, 512)],
        pl.BlockSpec((CHUNK, 640), rows),
        arr((LEN - CHUNK, 640)),
        (x, wqk_t, wv),
        flops=2 * (LEN - CHUNK) * depth * 640,
        moved=12e6,
    )


def conv(x, tail, taps):
    row = lax.broadcasted_iota(jnp.int32, (8, 1), 0)
    once, twice = pltpu.roll(x, 1, 0), pltpu.roll(x, 2, 0)
    top1 = jnp.where(row == 0, tail[7:8], once[0:8])
    top2 = jnp.where(row == 0, tail[6:7], jnp.where(row == 1, tail[7:8], twice[0:8]))
    once = jnp.concatenate([top1, once[8:]], axis=0)
    twice = jnp.concatenate([top2, twice[8:]], axis=0)
    return taps[0:1] * x + taps[1:2] * once + taps[2:3] * twice


def state_kernel(
    a_ref, b_ref, before_ref, tail_ref, taps_ref, pick_ref, biast_ref,
    ql_ref, kr_ref, vh_ref, vl_ref, sp_ref, st_ref,
):
    c = pl.program_id(0)

    @pl.when(c == 0)
    def _():
        st_ref[...] = jnp.zeros_like(st_ref)

    x = jnp.where(c < CHUNKS - 1, a_ref[...], b_ref[...])
    both = conv(x, jnp.where(c > 0, before_ref[...], tail_ref[...]), taps_ref[...])
    qk, v = both[:, :128] * 0.5, both[:, 128:]
    lane = lax.broadcasted_iota(jnp.int32, (1, 128), 1)
    low = lane < 64
    turned = pltpu.roll(qk, 64, 1)
    hi = qk.astype(BF16).astype(F32)
    lo = qk - hi
    turned_hi = turned.astype(BF16).astype(F32)
    turned_lo = turned - turned_hi
    zero = jnp.zeros_like(qk)
    ql = side(jnp.where(low, hi, turned_lo), jnp.where(low, hi, zero)).astype(BF16)
    kr = side(jnp.where(low, turned_hi, hi), jnp.where(low, turned_lo, zero)).astype(BF16)
    ql_ref[...] = ql
    kr_ref[...] = kr
    v_hi, v_lo = halves(v)
    vh_ref[...] = v_hi
    vl_ref[...] = v_lo
    for head in range(HEADS):
        ab = nt(pick_ref[head], kr) + biast_ref[...]
        p_hi, p_lo = halves(ab[:NF] * ab[WIDE : WIDE + NF])
        own = nn3(p_hi, p_lo, v_hi[:, cols(head)], v_lo[:, cols(head)])
        sp_ref[0, head] = st_ref[head]
        st_ref[head] += own


def shard_state(proj, end, tail, taps, pick_kt, bias_t):
    rows = lambda c: (c, 0)
    before = lambda c: (jnp.maximum(c * (CHUNK // 8) - 1, 0), 0)
    return call(
        state_kernel,
        (CHUNKS,),
        [
            pl.BlockSpec((CHUNK, 640), lambda c: (jnp.minimum(c, CHUNKS - 2), 0)),
            full(CHUNK, 640),
            pl.BlockSpec((8, 640), before),
            full(8, 640),
            full(3, 640),
            full(HEADS, 2 * WIDE, WIDE),
            full(2 * WIDE, 1),
        ],
        [
            pl.BlockSpec((CHUNK, WIDE), rows),
            pl.BlockSpec((CHUNK, WIDE), rows),
            pl.BlockSpec((CHUNK, 512), rows),
            pl.BlockSpec((CHUNK, 512), rows),
            pl.BlockSpec((1, HEADS, NF, HDIM), lambda c: (c, 0, 0, 0)),
            full(HEADS, NF, HDIM),
        ],
        [
            arr((LEN, WIDE), BF16),
            arr((LEN, WIDE), BF16),
            arr((LEN, 512), BF16),
            arr((LEN, 512), BF16),
            arr((CHUNKS, HEADS, NF, HDIM)),
            arr((HEADS, NF, HDIM)),
        ],
        (proj, end, proj, tail, taps, pick_kt, bias_t),
        flops=4e9,
        moved=15e6,
    )


def running_kernel(backward, x_ref, o_ref):
    count = x_ref.shape[0]
    order = range(count - 1, -1, -1) if backward else range(count)
    total = jnp.zeros(x_ref.shape[1:], F32)
    for i in order:
        o_ref[i] = total
        total = total + x_ref[i]


def carried_in(state, backward):
    count = lax.axis_size("seq")
    rows = HEADS * NF // count
    pieces = lax.all_to_all(state.reshape(count, rows, HDIM), "seq", 0, 0)
    shape = (count, rows, HDIM)
    sums = call(
        functools.partial(running_kernel, backward), (1,), [full(*shape)], full(*shape), arr(shape), (pieces,), moved=6e5
    )
    return lax.all_to_all(sums, "seq", 0, 0).reshape(HEADS, NF, HDIM)


def lower():
    row = lax.broadcasted_iota(jnp.int32, (CHUNK, CHUNK), 0)
    col = lax.broadcasted_iota(jnp.int32, (CHUNK, CHUNK), 1)
    return row >= col


def inner_kernel(ql_ref, kr_ref, vh_ref, vl_ref, num_ref):
    ql, kr = ql_ref[...], kr_ref[...]
    causal = lower()
    for head in range(HEADS):
        mine = jnp.where(head_mask(WIDE, head), ql, jnp.zeros_like(ql))
        s = nt(mine, kr)
        w_hi, w_lo = halves(jnp.where(causal, 1.0 + s + 0.5 * s * s, 0.0))
        num_ref[:, cols(head)] = nn3(w_hi, w_lo, vh_ref[:, cols(head)], vl_ref[:, cols(head)])


def inner(ql, kr, vh, vl):
    rows = lambda c: (c, 0)
    narrow, wide = pl.BlockSpec((CHUNK, WIDE), rows), pl.BlockSpec((CHUNK, 512), rows)
    return call(
        inner_kernel, (CHUNKS,), [narrow, narrow, wide, wide], wide, arr((LEN, 512)), (ql, kr, vh, vl), flops=6e9, moved=6e6
    )


def feature_kernel(ql_ref, pick_ref, pickt_ref, bias_ref, biast_ref, ph_ref, pl_ref, th_ref, tl_ref):
    ql = ql_ref[...]
    for head in range(HEADS):
        part = slice(head * WIDE, (head + 1) * WIDE)
        a, b = factors(ql, pick_ref[head], bias_ref[...])
        ph_ref[:, part], pl_ref[:, part] = halves(a * b)
        ab = nt(pickt_ref[head], ql) + biast_ref[...]
        th_ref[head], tl_ref[head] = halves(ab[:NF] * ab[WIDE : WIDE + NF])


def query_features(ql, pick, pick_t, bias, bias_t):
    rows = lambda c: (c, 0)
    wide, turned = pl.BlockSpec((CHUNK, HEADS * WIDE), rows), pl.BlockSpec((HEADS, NF, CHUNK), lambda c: (0, 0, c))
    return call(
        feature_kernel,
        (CHUNKS,),
        [
            pl.BlockSpec((CHUNK, WIDE), rows),
            full(HEADS, WIDE, 2 * WIDE), full(HEADS, 2 * WIDE, WIDE), full(1, 2 * WIDE), full(2 * WIDE, 1),
        ],
        [wide, wide, turned, turned],
        [arr((LEN, HEADS * WIDE), BF16)] * 2 + [arr((HEADS, NF, LEN), BF16)] * 2,
        (ql, pick, pick_t, bias, bias_t),
        flops=4e9,
        moved=10e6,
    )


def forward_kernel(ph_ref, pl_ref, th_ref, tl_ref, num_ref, sp_ref, se_ref, og_ref, gain_ref,
                   out_ref, dh_ref, dl_ref, gs_ref, gt_ref):
    @pl.when(pl.program_id(0) == 0)
    def _():
        gt_ref[...] = jnp.zeros_like(gt_ref)

    for head in range(HEADS):
        part = slice(head * WIDE, (head + 1) * WIDE)
        s_hi, s_lo = halves(padded(sp_ref[0, head] + se_ref[head]))
        num = num_ref[:, cols(head)] + nn3(ph_ref[:, part], pl_ref[:, part], s_hi, s_lo)
        r = lax.rsqrt(jnp.mean(num * num, axis=-1, keepdims=True) + EPS)
        gain = gain_ref[:, cols(head)]
        unit = num * r
        out_ref[:, cols(head)] = unit * gain
        g = og_ref[:, cols(head)] * gain
        d = r * (g - unit * jnp.mean(g * unit, axis=-1, keepdims=True))
        d_hi, d_lo = halves(d)
        dh_ref[:, cols(head)] = d_hi
        dl_ref[:, cols(head)] = d_lo
        own = nn3(th_ref[head], tl_ref[head], d_hi, d_lo)
        gs_ref[0, head] = own
        gt_ref[head] += own


def forward(features, num, sp, se, og, gain):
    rows = lambda c: (c, 0)
    packed, turned = pl.BlockSpec((CHUNK, HEADS * WIDE), rows), pl.BlockSpec((HEADS, NF, CHUNK), lambda c: (0, 0, c))
    wide = pl.BlockSpec((CHUNK, 512), rows)
    states = pl.BlockSpec((1, HEADS, NF, HDIM), lambda c: (c, 0, 0, 0))
    return call(
        forward_kernel,
        (CHUNKS,),
        [packed, packed, turned, turned, wide, states, full(HEADS, NF, HDIM), wide, full(1, 512)],
        [wide, wide, wide, states, full(HEADS, NF, HDIM)],
        [
            arr((LEN, 512)), arr((LEN, 512), BF16), arr((LEN, 512), BF16),
            arr((CHUNKS, HEADS, NF, HDIM)), arr((HEADS, NF, HDIM)),
        ],
        (*features, num, sp, se, og, gain),
        flops=5e9,
        moved=18e6,
    )


def query_kernel(ql_ref, kr_ref, vh_ref, vl_ref, dh_ref, dl_ref, sp_ref, se_ref, pick_ref, bias_ref, back_ref, gq_ref):
    ql, kr = ql_ref[...], kr_ref[...]
    causal = lower()
    gq = jnp.zeros((CHUNK, WIDE), F32)
    du = jnp.zeros((CHUNK, 128), F32)
    for head in range(HEADS):
        mask = head_mask(WIDE, head)
        q = jnp.where(mask, ql, jnp.zeros_like(ql))
        k = jnp.where(mask, kr, jnp.zeros_like(kr))
        v_hi, v_lo = vh_ref[:, cols(head)], vl_ref[:, cols(head)]
        d_hi, d_lo = dh_ref[:, cols(head)], dl_ref[:, cols(head)]
        slope = jnp.where(causal, 1.0 + nt(q, kr), 0.0)
        gq = gq + nn((nt3(d_hi, d_lo, v_hi, v_lo) * slope).astype(BF16), k)
        s_hi, s_lo = halves(padded(sp_ref[0, head] + se_ref[head]))
        dp = nt3(d_hi, d_lo, s_hi, s_lo)
        a, b = factors(ql, pick_ref[head], bias_ref[...])
        dab_hi, dab_lo = halves(side(dp * b, dp * a))
        du = du + nn(dab_hi, back_ref[head]) + nn(dab_lo, back_ref[head])
    gq_ref[...] = gq[:, :128] + gq[:, 128:] + du


def key_kernel(ql_ref, kr_ref, vh_ref, vl_ref, dh_ref, dl_ref, gk_ref, gv_ref):
    ql, kr = ql_ref[...], kr_ref[...]
    row = lax.broadcasted_iota(jnp.int32, (CHUNK, CHUNK), 0)
    col = lax.broadcasted_iota(jnp.int32, (CHUNK, CHUNK), 1)
    causal = col >= row
    gk = jnp.zeros((CHUNK, WIDE), F32)
    for head in range(HEADS):
        mask = head_mask(WIDE, head)
        q = jnp.where(mask, ql, jnp.zeros_like(ql))
        k = jnp.where(mask, kr, jnp.zeros_like(kr))
        v_hi, v_lo = vh_ref[:, cols(head)], vl_ref[:, cols(head)]
        d_hi, d_lo = dh_ref[:, cols(head)], dl_ref[:, cols(head)]
        s = nt(k, ql)
        ds_hi, ds_lo = halves(nt3(v_hi, v_lo, d_hi, d_lo) * jnp.where(causal, 1.0 + s, 0.0))
        gk = gk + nn(ds_hi, q) + nn(ds_lo, q)
        w_hi, w_lo = halves(jnp.where(causal, 1.0 + s + 0.5 * s * s, 0.0))
        gv_ref[:, cols(head)] = nn3(w_hi, w_lo, d_hi, d_lo)
    gk_ref[...] = gk[:, :128] + pltpu.roll(gk[:, :128], 64, 1)


def backward(ql, kr, vh, vl, dh, dl, sp, se, pick, bias, back):
    rows = lambda c: (c, 0)
    narrow, wide = pl.BlockSpec((CHUNK, WIDE), rows), pl.BlockSpec((CHUNK, 512), rows)
    half = pl.BlockSpec((CHUNK, 128), rows)
    states = pl.BlockSpec((1, HEADS, NF, HDIM), lambda c: (c, 0, 0, 0))
    gk, gv = call(
        key_kernel,
        (CHUNKS,),
        [narrow, narrow, wide, wide, wide, wide],
        [half, wide],
        [arr((LEN, 128)), arr((LEN, 512))],
        (ql, kr, vh, vl, dh, dl),
        flops=8e9,
        moved=8e6,
    )
    gq = call(
        query_kernel,
        (CHUNKS,),
        [
            narrow, narrow, wide, wide, wide, wide, states, full(HEADS, NF, HDIM),
            full(HEADS, WIDE, 2 * WIDE), full(1, 2 * WIDE), full(HEADS, 2 * WIDE, 128),
        ],
        half,
        arr((LEN, 128)),
        (ql, kr, vh, vl, dh, dl, sp, se, pick, bias, back),
        flops=8e9,
        moved=8e6,
    )
    return gq, gk, gv


def later_kernel(first, last, kr_ref, vh_ref, vl_ref, gs_ref, gl_ref, gq_ref, gk_ref, gv_ref, pick_ref, bias_ref,
                 back_ref, o_ref, head_ref, total):
    @pl.when(pl.program_id(0) == 0)
    def _():
        begin = gl_ref[...]
        for c in range(CHUNKS - 1, last - 1, -1):
            begin = begin + gs_ref[c]
        total[...] = begin

    kr = kr_ref[...]
    du = jnp.zeros((CHUNK, 128), F32)
    for head in range(HEADS):
        a, b = factors(kr, pick_ref[head], bias_ref[...])
        l_hi, l_lo = halves(padded(total[head]))
        gained = nn((a * b).astype(BF16), side(l_hi, l_lo))
        v_hi, v_lo = vh_ref[:, cols(head)], vl_ref[:, cols(head)]
        o_ref[:, 128 + head * HDIM : 256 + head * HDIM] = gv_ref[:, cols(head)] + gained[:, :HDIM] + gained[:, HDIM:]
        dp = nt(side(v_hi, v_lo), side(l_hi, l_hi))
        dab_hi, dab_lo = halves(side(dp * b, dp * a))
        du = du + nn(dab_hi, back_ref[head]) + nn(dab_lo, back_ref[head])
    low = lax.broadcasted_iota(jnp.int32, (1, 128), 1) < 64
    o_ref[:, :128] = 0.5 * jnp.where(low, gq_ref[...], pltpu.roll(gk_ref[...] + du, 64, 1))
    head_ref[...] = o_ref[:8]
    total[...] += gs_ref[last - 1 - pl.program_id(0)]


def later(first, last, kr, vh, vl, gs, gl, gq, gk, gv, pick, bias, back):
    count = last - first
    rows = lambda c: (last - 1 - c, 0)
    to = lambda c: (count - 1 - c, 0)
    narrow, wide = pl.BlockSpec((CHUNK, WIDE), rows), pl.BlockSpec((CHUNK, 512), rows)
    half = pl.BlockSpec((CHUNK, 128), rows)
    return call(
        functools.partial(later_kernel, first, last),
        (count,),
        [
            narrow, wide, wide, full(CHUNKS, HEADS, NF, HDIM), full(HEADS, NF, HDIM), half, half, wide,
            full(HEADS, WIDE, 2 * WIDE), full(1, 2 * WIDE), full(HEADS, 2 * WIDE, 128),
        ],
        [pl.BlockSpec((CHUNK, 640), to), full(8, 640)],
        [arr((count * CHUNK, 640)), arr((8, 640))],
        (kr, vh, vl, gs, gl, gq, gk, gv, pick, bias, back),
        [pltpu.VMEM((HEADS, NF, HDIM), F32)],
        flops=2e9 * count,
        moved=3e6 * count,
    )


def conv_back(x, tail, taps):
    n = x.shape[0]
    row = lax.broadcasted_iota(jnp.int32, (8, 1), 0)
    once, twice = pltpu.roll(x, n - 1, 0), pltpu.roll(x, n - 2, 0)
    end1 = jnp.where(row == 7, tail[0:1], once[n - 8 :])
    end2 = jnp.where(row == 7, tail[1:2], jnp.where(row == 6, tail[0:1], twice[n - 8 :]))
    once = jnp.concatenate([once[: n - 8], end1], axis=0)
    twice = jnp.concatenate([twice[: n - 8], end2], axis=0)
    return (taps[0:1] * x + taps[1:2] * once + taps[2:3] * twice).astype(BF16)


def f32(x):
    return x.astype(F32)


def flip(x, axis, bit):
    return lax.ppermute(x, axis, [(i, i ^ bit) for i in range(lax.axis_size(axis))])


def input_kernel(me_ref, a_ref, b_ref, h_ref, t_ref, wv_ref, wqk_ref, z_ref, keep_ref, send_ref, dt_ref, d_ref):
    @pl.when(pl.program_id(0) == 0)
    def _():
        n = a_ref.shape[0]
        for start in range(0, LEN, STEP):
            end = start + STEP
            src = a_ref[start:end] if start < n else b_ref[start - n : end - n]
            if end == LEN:
                tail = h_ref[...]
            else:
                tail = a_ref[end : end + 8] if end < n else b_ref[end - n : end - n + 8]
            got = conv_back(src, tail, t_ref[...])
            d_ref[start:end] = got
            dt_ref[:, start:end] = got.T

    d = d_ref[...]
    half = LEN // 2
    bottom = []
    for i in range(2):
        part = slice(512 * i, 512 * (i + 1))
        got = nt(d[:, 128:], wv_ref[part]) + nn(d[:, :128], wqk_ref[:, part])
        z_ref[0, i] = got[:half].astype(BF16)
        bottom.append(got[half:])
    first = me_ref[0] == 0
    keep_ref[0] = jnp.where(first, bottom[0], bottom[1])
    send_ref[0] = jnp.where(first, bottom[1], bottom[0]).astype(BF16)


def input_products(side_y, a, b, halo, taps, wv, wqk):
    n, m, half = a.shape[0], b.shape[0], LEN // 2
    const = lambda *shape: pl.BlockSpec(shape, lambda i, me: (0,) * len(shape))
    block = pl.BlockSpec((1, half, 512), lambda i, me: (i, 0, 0))
    return call(
        input_kernel,
        (4,),
        [
            const(n, 640), const(m, 640), const(8, 640), const(3, 640),
            pl.BlockSpec((1024, 512), lambda i, me: (i, 0)), pl.BlockSpec((128, 1024), lambda i, me: (0, i)),
        ],
        [pl.BlockSpec((1, 2, half, 512), lambda i, me: (i, 0, 0, 0)), block, block, const(640, LEN)],
        [arr((4, 2, half, 512), BF16), arr((4, half, 512)), arr((4, half, 512), BF16), arr((640, LEN), BF16)],
        (side_y, a, b, halo, taps, wv, wqk),
        [pltpu.VMEM((LEN, 640), BF16)],
        prefetch=1,
        flops=2 * LEN * 640 * 4096,
        moved=20e6,
    )


def pair_kernel(keep_ref, came_ref, o_ref):
    o_ref[...] = (keep_ref[...] + f32(came_ref[...])).astype(BF16)


def top_kernel(me_ref, p_ref, keep_ref, send_ref):
    total = f32(p_ref[0])
    for i in range(1, 4):
        total = total + f32(p_ref[i])
    first = me_ref[0] == 0
    keep_ref[...] = jnp.where(first, total[0], total[1])
    send_ref[...] = jnp.where(first, total[1], total[0]).astype(BF16)


def last_kernel(keep_ref, came_ref, p_ref, o_ref):
    @pl.when(pl.program_id(0) < 2)
    def _():
        o_ref[...] = (keep_ref[...] + f32(came_ref[...])).astype(BF16)

    @pl.when(pl.program_id(0) >= 2)
    def _():
        total = f32(p_ref[0])
        for i in range(1, 4):
            total = total + f32(p_ref[i])
        o_ref[...] = total.astype(BF16)


def along_z(x):
    return lax.all_to_all(x, "tp", 0, 0, axis_index_groups=[[0, 2, 4, 6], [1, 3, 5, 7]])


def reduce_input_grad(side_y, by_z, keep, send, first, second):
    half, tile = LEN // 2, LEN // 4
    came = flip(send, "tp", 1)
    tops = along_z(by_z)
    block = pl.BlockSpec((1, half, 512), lambda i: (i, 0, 0))
    pairs = call(pair_kernel, (4,), [block, block], block, arr((4, half, 512), BF16), (keep, came), moved=8e6, after=first)
    rows = pl.BlockSpec((tile // 2, 512), lambda i, me: (i, 0))
    keep, send = call(
        top_kernel,
        (4,),
        [pl.BlockSpec((4, 2, tile // 2, 512), lambda i, me: (0, 0, i, 0))],
        [rows, rows],
        [arr((half, 512)), arr((half, 512), BF16)],
        (side_y, tops),
        prefetch=1,
        after=second,
        moved=6e6,
    )
    pairs = along_z(pairs)
    came = flip(send, "tp", 1)
    top = pl.BlockSpec((tile, 512), lambda i: (jnp.minimum(i, 1), 0))
    return call(
        last_kernel,
        (4,),
        [top, top, pl.BlockSpec((4, tile, 512), lambda i: (0, jnp.maximum(i - 2, 0), 0))],
        pl.BlockSpec((tile, 512), lambda i: (i, 0)),
        arr((LEN, 512), BF16),
        (keep, came, pairs),
        moved=5e6,
    )


def weight_kernel(dest_ref, d_ref, x_ref, y_ref, theirs_ref, ours_ref):
    first = dest_ref[8] == 0
    for r, ref in enumerate((x_ref, y_ref)):
        got = nn(d_ref[...], ref[...]).astype(BF16)
        half = got.shape[1] // 2
        low, high = got[:, :half], got[:, half:]
        theirs_ref[r] = jnp.where(first, high, low)
        ours_ref[r] = jnp.where(first, low, high)


def split_kernel(mine_ref, came_ref, *outs):
    step = pl.program_id(0)
    got = (f32(mine_ref[...]) + f32(came_ref[...])).astype(BF16)
    for j in range(4):

        @pl.when(step == j)
        def _(j=j):
            outs[j][...] = got


def row_sum_kernel(mine_ref, a_ref, b_ref, c_ref, keep_ref, send_ref):
    for r, out in enumerate((keep_ref, send_ref)):
        out[...] = (f32(mine_ref[r]) + f32(a_ref[r]) + f32(b_ref[r]) + f32(c_ref[r])).astype(out.dtype)


def finish_kernel(keep_ref, came_ref, q_ref, k_ref, v_ref):
    step = pl.program_id(0)
    total = keep_ref[...] + f32(came_ref[...])

    @pl.when(step == 0)
    def _():
        q_ref[...] = total[:64]
        k_ref[...] = total[64:]

    @pl.when(step > 0)
    def _():
        v_ref[...] = total.T


def to_x(x, by):
    return lax.ppermute(x, "seq", [(s, s // 8 * 8 + (s % 8 + 2 * by) % 8) for s in range(16)])


def weight_parts(dt, x):
    me = lax.axis_index("seq")
    y, px, core = me // 8, me // 2 % 4, me % 2
    width = x.shape[1] // 16
    chips = [(y ^ r) * 4 + (px + dx) % 4 for dx in range(4) for r in range(2)]
    dest = jnp.stack([*chips, core]).astype(jnp.int32)
    theirs, ours = call(
        weight_kernel,
        (4,),
        [pl.BlockSpec((640, LEN), lambda i, dest: (0, 0))]
        + [pl.BlockSpec((LEN, 2 * width), lambda i, dest, r=r: (0, dest[2 * i + r])) for r in range(2)],
        [pl.BlockSpec((2, 640, width), lambda i, dest: (i, 0, 0))] * 2,
        [arr((8, 640, width), BF16)] * 2,
        (dest, dt, x, x),
        prefetch=1,
        flops=2 * LEN * 640 * 4096,
        moved=15e6,
    )
    came = flip(theirs, "seq", 1)
    block = pl.BlockSpec((2, 640, width), lambda i: (i, 0, 0))
    return call(
        split_kernel,
        (4,),
        [block, block],
        [full(2, 640, width)] * 4,
        [arr((2, 640, width), BF16)] * 4,
        (ours, came),
        moved=8e6,
    )


def reduce_weight_grad(parts):
    mine, *rest = parts
    width = mine.shape[2]
    pair = pl.BlockSpec((2, 128, width), lambda i: (0, i, 0))
    one = pl.BlockSpec((128, width), lambda i: (i, 0))
    keep, send = call(
        row_sum_kernel,
        (5,),
        [pair] * 4,
        [one] * 2,
        [arr((640, width)), arr((640, width), BF16)],
        (mine, *rest),
        moved=4e6,
    )
    return keep, flip(send, "seq", 8)


def finish_weight_grad(keep, came):
    width = keep.shape[1]
    one = pl.BlockSpec((128, width), lambda i: (i, 0))
    return call(
        finish_kernel,
        (5,),
        [one, one],
        [full(64, width), full(64, width), pl.BlockSpec((width, 128), lambda i: (0, jnp.maximum(i - 1, 0)))],
        [arr((64, width)), arr((64, width)), arr((width, 512))],
        (keep, came),
        moved=2e6,
    )


def along(x, by):
    n = lax.axis_size("seq")
    return lax.ppermute(x, "seq", [(i, i + by) for i in range(n) if 0 <= i + by < n])


def local(inputs, w_query, w_key, w_value, taps_query, taps_key, taps_value, out_gain, out_grad):
    packed, bias, back = feature_matrices()
    pick_q, pick_k = (jnp.asarray(packed[i], BF16) for i in range(2))
    pick_qt, pick_kt = (jnp.asarray(packed[i].transpose(0, 2, 1), BF16) for i in range(2))
    back_q, back_k = (jnp.asarray(back[i], BF16) for i in range(2))
    bias, bias_t = jnp.asarray(bias), jnp.asarray(bias.T)
    wq_t, wk_t = w_query.T, w_key.T
    taps = jnp.concatenate([taps_query, taps_key, taps_value], axis=1)

    end, tail, wqk_t = project_end(inputs, wq_t, wk_t, w_value)
    tail = along(tail, 1)
    proj = project(inputs, wqk_t, w_value)
    ql, kr, vh, vl, before, own = shard_state(proj, end, tail, taps, pick_kt, bias_t)
    earlier = carried_in(own, False)
    num = inner(ql, kr, vh, vl)
    features = query_features(ql, pick_q, pick_qt, bias, bias_t)
    outputs, dh, dl, grads, own_grad = forward(features, num, before, earlier, out_grad, out_gain.reshape(1, 512))
    after = carried_in(own_grad, True)
    gq, gk, gv = backward(ql, kr, vh, vl, dh, dl, before, earlier, pick_q, bias, back_q)
    rest = (kr, vh, vl, grads, after, gq, gk, gv, pick_k, bias, back_k)
    ga, halo = later(0, 1, *rest)
    halo = along(halo, -1)
    gb, _ = later(1, CHUNKS, *rest)
    side_y = (lax.axis_index("tp") % 2).astype(jnp.int32).reshape(1)
    by_z, keep, send, dt = input_products(side_y, ga, gb, halo, taps, w_value, wqk_t)
    mine, *rest = weight_parts(dt, inputs)
    parts = [mine, *(to_x(part, dx) for dx, part in enumerate(rest, 1))]
    own, came = reduce_weight_grad(parts)
    input_grad = reduce_input_grad(side_y, by_z, keep, send, parts[1:], ())
    grad_query, grad_key, grad_value = finish_weight_grad(own, came)
    return (outputs, input_grad, grad_query.T, grad_key.T, grad_value)


def solution(mesh):
    return jax.shard_map(
        local,
        mesh=mesh,
        in_specs=(
            P("seq", None),
            P(None, "tp"),
            P(None, "tp"),
            P(None, "tp"),
            P(None, "tp"),
            P(None, "tp"),
            P(None, "tp"),
            P("tp"),
            P("seq", "tp"),
        ),
        out_specs=(P("seq", "tp"), P("seq", "tp"), P("seq", "tp"), P("seq", "tp"), P("seq", "tp")),
        check_vma=False,
    )
```

```python
import functools

import jax
import jax.numpy as jnp
import numpy as np
from jax import lax
from jax.experimental import pallas as pl
from jax.experimental.pallas import tpu as pltpu
from jax.sharding import PartitionSpec as P

FEAT = 16
HDIM = 128
HEADS = 4
CHUNK = 256
LEN = 1024
CHUNKS = LEN // CHUNK
NF = 160
WIDE = 256
EPS = 1e-05
STEP = 128
F32, BF16 = jnp.float32, jnp.bfloat16


def feature_matrices():
    pairs = [(i, j) for i in range(FEAT) for j in range(i, FEAT)]
    pick = np.zeros((2, HEADS, 64, 2 * WIDE), np.float32)
    bias = np.zeros((1, 2 * WIDE), np.float32)
    for head in range(HEADS):
        base = head * FEAT
        for f, (i, j) in enumerate(pairs):
            pick[:, head, base + i, f] = 1.0
            pick[0, head, base + j, WIDE + f] = 0.5 if i == j else 1.0
            pick[1, head, base + j, WIDE + f] = 1.0
        for i in range(FEAT):
            pick[:, head, base + i, len(pairs) + i] = 1.0
    ones = len(pairs) + FEAT
    bias[0, ones] = 1.0
    bias[0, WIDE + len(pairs) : WIDE + ones + 1] = 1.0
    packed = np.zeros((2, HEADS, WIDE, 2 * WIDE), np.float32)
    packed[0, :, 0:64] = pick[0]
    packed[0, :, 64:128] = pick[0]
    packed[1, :, 0:64] = pick[1]
    packed[1, :, 128:192] = pick[1]
    back = np.zeros((2, HEADS, 2 * WIDE, 128), np.float32)
    back[:, :, :, 0:64] = pick.transpose(0, 1, 3, 2)
    return packed, bias, back


def nn(a, b):
    return lax.dot_general(a, b, (((1,), (0,)), ((), ())), preferred_element_type=F32)


def nt(a, b):
    return lax.dot_general(a, b, (((1,), (1,)), ((), ())), preferred_element_type=F32)


def halves(x):
    hi = x.astype(BF16)
    return hi, (x - hi.astype(F32)).astype(BF16)


def side(*parts):
    return jnp.concatenate(parts, axis=1)


def nn3(a_hi, a_lo, b_hi, b_lo):
    both = nn(a_hi, side(b_hi, b_lo))
    n = b_hi.shape[1]
    return both[:, :n] + both[:, n:] + nn(a_lo, b_hi)


def nt3(a_hi, a_lo, b_hi, b_lo):
    return nt(side(a_hi, a_lo), side(b_hi, b_hi)) + nt(a_hi, b_lo)


def factors(packed, pick, bias):
    both = nn(packed, pick) + bias
    return both[:, :WIDE], both[:, WIDE:]


def padded(state):
    return jnp.concatenate([state, jnp.zeros((WIDE - NF, HDIM), F32)], axis=0)


def head_mask(width, head):
    lane = lax.broadcasted_iota(jnp.int32, (1, width), 1)
    return (lane % 64) // FEAT == head


def cols(head):
    return slice(head * HDIM, (head + 1) * HDIM)


def call(body, grid, ins, outs, shapes, args, scratch=(), prefetch=0, flops=0, moved=0, after=()):
    if after:
        kept, skip = body, len(after)
        at = prefetch + len(ins)
        body = lambda *refs: kept(*refs[:at], *refs[at + skip :])
        ins = [*ins] + [pl.BlockSpec(memory_space=pl.ANY)] * skip
        args = (*args, *after)
    return pl.pallas_call(
        body,
        grid_spec=pltpu.PrefetchScalarGridSpec(
            num_scalar_prefetch=prefetch, grid=grid, in_specs=ins, out_specs=outs, scratch_shapes=list(scratch)
        ),
        out_shape=shapes,
        compiler_params=pltpu.CompilerParams(vmem_limit_bytes=56 * 2**20),
        cost_estimate=pl.CostEstimate(flops=int(flops), bytes_accessed=int(moved), transcendentals=0),
    )(*args)


def full(*shape):
    return pl.BlockSpec(shape, lambda *_: (0,) * len(shape))


def arr(shape, dtype=F32):
    return jax.ShapeDtypeStruct(shape, dtype)


def end_kernel(x_ref, wq_ref, wk_ref, wv_ref, o_ref, tail_ref, wqk_ref):
    step = pl.program_id(0)
    wqk_ref[0:64] = wq_ref[...]
    wqk_ref[64:128] = wk_ref[...]
    x = x_ref[...]
    qk, v = nt(x, wqk_ref[...]), nn(x, wv_ref[...])

    @pl.when(step == 0)
    def _():
        o_ref[:, :128] = qk
        o_ref[:, 128:] = v

    @pl.when(step > 0)
    def _():
        o_ref[:, :128] += qk
        o_ref[:, 128:] += v

    tail_ref[...] = o_ref[CHUNK - 8 :]


def project_end(x, wq_t, wk_t, wv):
    depth = x.shape[1]
    part = depth // 4
    at = lambda k: (0, k)
    return call(
        end_kernel,
        (4,),
        [
            pl.BlockSpec((CHUNK, part), lambda k: (CHUNKS - 1, k)),
            pl.BlockSpec((64, part), at),
            pl.BlockSpec((64, part), at),
            pl.BlockSpec((part, 512), lambda k: (k, 0)),
        ],
        [full(CHUNK, 640), full(8, 640), pl.BlockSpec((128, part), at)],
        [arr((CHUNK, 640)), arr((8, 640)), arr((128, depth), BF16)],
        (x, wq_t, wk_t, wv),
        flops=2 * CHUNK * depth * 640,
        moved=8e6,
    )


def project_kernel(x_ref, wqk_ref, wv_ref, o_ref):
    x = x_ref[...]
    o_ref[:, :128] = nt(x, wqk_ref[...])
    o_ref[:, 128:] = nn(x, wv_ref[...])


def project(x, wqk_t, wv):
    depth = x.shape[1]
    rows = lambda c: (c, 0)
    return call(
        project_kernel,
        (CHUNKS - 1,),
        [pl.BlockSpec((CHUNK, depth), rows), full(128, depth), full(depth, 512)],
        pl.BlockSpec((CHUNK, 640), rows),
        arr((LEN - CHUNK, 640)),
        (x, wqk_t, wv),
        flops=2 * (LEN - CHUNK) * depth * 640,
        moved=12e6,
    )


def conv(x, tail, taps):
    row = lax.broadcasted_iota(jnp.int32, (8, 1), 0)
    once, twice = pltpu.roll(x, 1, 0), pltpu.roll(x, 2, 0)
    top1 = jnp.where(row == 0, tail[7:8], once[0:8])
    top2 = jnp.where(row == 0, tail[6:7], jnp.where(row == 1, tail[7:8], twice[0:8]))
    once = jnp.concatenate([top1, once[8:]], axis=0)
    twice = jnp.concatenate([top2, twice[8:]], axis=0)
    return taps[0:1] * x + taps[1:2] * once + taps[2:3] * twice


def state_kernel(
    a_ref, b_ref, before_ref, tail_ref, taps_ref, pick_ref, biast_ref,
    ql_ref, kr_ref, vh_ref, vl_ref, sp_ref, st_ref,
):
    c = pl.program_id(0)

    @pl.when(c == 0)
    def _():
        st_ref[...] = jnp.zeros_like(st_ref)

    x = jnp.where(c < CHUNKS - 1, a_ref[...], b_ref[...])
    both = conv(x, jnp.where(c > 0, before_ref[...], tail_ref[...]), taps_ref[...])
    qk, v = both[:, :128] * 0.5, both[:, 128:]
    lane = lax.broadcasted_iota(jnp.int32, (1, 128), 1)
    low = lane < 64
    turned = pltpu.roll(qk, 64, 1)
    hi = qk.astype(BF16).astype(F32)
    lo = qk - hi
    turned_hi = turned.astype(BF16).astype(F32)
    turned_lo = turned - turned_hi
    zero = jnp.zeros_like(qk)
    ql = side(jnp.where(low, hi, turned_lo), jnp.where(low, hi, zero)).astype(BF16)
    kr = side(jnp.where(low, turned_hi, hi), jnp.where(low, turned_lo, zero)).astype(BF16)
    ql_ref[...] = ql
    kr_ref[...] = kr
    v_hi, v_lo = halves(v)
    vh_ref[...] = v_hi
    vl_ref[...] = v_lo
    for head in range(HEADS):
        ab = nt(pick_ref[head], kr) + biast_ref[...]
        p_hi, p_lo = halves(ab[:NF] * ab[WIDE : WIDE + NF])
        own = nn3(p_hi, p_lo, v_hi[:, cols(head)], v_lo[:, cols(head)])
        sp_ref[0, head] = st_ref[head]
        st_ref[head] += own


def shard_state(proj, end, tail, taps, pick_kt, bias_t):
    rows = lambda c: (c, 0)
    before = lambda c: (jnp.maximum(c * (CHUNK // 8) - 1, 0), 0)
    return call(
        state_kernel,
        (CHUNKS,),
        [
            pl.BlockSpec((CHUNK, 640), lambda c: (jnp.minimum(c, CHUNKS - 2), 0)),
            full(CHUNK, 640),
            pl.BlockSpec((8, 640), before),
            full(8, 640),
            full(3, 640),
            full(HEADS, 2 * WIDE, WIDE),
            full(2 * WIDE, 1),
        ],
        [
            pl.BlockSpec((CHUNK, WIDE), rows),
            pl.BlockSpec((CHUNK, WIDE), rows),
            pl.BlockSpec((CHUNK, 512), rows),
            pl.BlockSpec((CHUNK, 512), rows),
            pl.BlockSpec((1, HEADS, NF, HDIM), lambda c: (c, 0, 0, 0)),
            full(HEADS, NF, HDIM),
        ],
        [
            arr((LEN, WIDE), BF16),
            arr((LEN, WIDE), BF16),
            arr((LEN, 512), BF16),
            arr((LEN, 512), BF16),
            arr((CHUNKS, HEADS, NF, HDIM)),
            arr((HEADS, NF, HDIM)),
        ],
        (proj, end, proj, tail, taps, pick_kt, bias_t),
        flops=4e9,
        moved=15e6,
    )


def running_kernel(backward, x_ref, o_ref):
    count = x_ref.shape[0]
    order = range(count - 1, -1, -1) if backward else range(count)
    total = jnp.zeros(x_ref.shape[1:], F32)
    for i in order:
        o_ref[i] = total
        total = total + x_ref[i]


def carried_in(state, backward):
    count = lax.axis_size("seq")
    rows = HEADS * NF // count
    pieces = lax.all_to_all(state.reshape(count, rows, HDIM), "seq", 0, 0)
    shape = (count, rows, HDIM)
    sums = call(
        functools.partial(running_kernel, backward), (1,), [full(*shape)], full(*shape), arr(shape), (pieces,), moved=6e5
    )
    return lax.all_to_all(sums, "seq", 0, 0).reshape(HEADS, NF, HDIM)


def lower():
    row = lax.broadcasted_iota(jnp.int32, (CHUNK, CHUNK), 0)
    col = lax.broadcasted_iota(jnp.int32, (CHUNK, CHUNK), 1)
    return row >= col


def inner_kernel(ql_ref, kr_ref, vh_ref, vl_ref, num_ref):
    ql, kr = ql_ref[...], kr_ref[...]
    causal = lower()
    for head in range(HEADS):
        mine = jnp.where(head_mask(WIDE, head), ql, jnp.zeros_like(ql))
        s = nt(mine, kr)
        w_hi, w_lo = halves(jnp.where(causal, 1.0 + s + 0.5 * s * s, 0.0))
        num_ref[:, cols(head)] = nn3(w_hi, w_lo, vh_ref[:, cols(head)], vl_ref[:, cols(head)])


def inner(ql, kr, vh, vl):
    rows = lambda c: (c, 0)
    narrow, wide = pl.BlockSpec((CHUNK, WIDE), rows), pl.BlockSpec((CHUNK, 512), rows)
    return call(
        inner_kernel, (CHUNKS,), [narrow, narrow, wide, wide], wide, arr((LEN, 512)), (ql, kr, vh, vl), flops=6e9, moved=6e6
    )


def feature_kernel(ql_ref, pick_ref, pickt_ref, bias_ref, biast_ref, ph_ref, pl_ref, th_ref, tl_ref):
    ql = ql_ref[...]
    for head in range(HEADS):
        part = slice(head * WIDE, (head + 1) * WIDE)
        a, b = factors(ql, pick_ref[head], bias_ref[...])
        ph_ref[:, part], pl_ref[:, part] = halves(a * b)
        ab = nt(pickt_ref[head], ql) + biast_ref[...]
        th_ref[head], tl_ref[head] = halves(ab[:NF] * ab[WIDE : WIDE + NF])


def query_features(ql, pick, pick_t, bias, bias_t):
    rows = lambda c: (c, 0)
    wide, turned = pl.BlockSpec((CHUNK, HEADS * WIDE), rows), pl.BlockSpec((HEADS, NF, CHUNK), lambda c: (0, 0, c))
    return call(
        feature_kernel,
        (CHUNKS,),
        [
            pl.BlockSpec((CHUNK, WIDE), rows),
            full(HEADS, WIDE, 2 * WIDE), full(HEADS, 2 * WIDE, WIDE), full(1, 2 * WIDE), full(2 * WIDE, 1),
        ],
        [wide, wide, turned, turned],
        [arr((LEN, HEADS * WIDE), BF16)] * 2 + [arr((HEADS, NF, LEN), BF16)] * 2,
        (ql, pick, pick_t, bias, bias_t),
        flops=4e9,
        moved=10e6,
    )


def forward_kernel(ph_ref, pl_ref, th_ref, tl_ref, num_ref, sp_ref, se_ref, og_ref, gain_ref,
                   out_ref, dh_ref, dl_ref, gs_ref, gt_ref):
    @pl.when(pl.program_id(0) == 0)
    def _():
        gt_ref[...] = jnp.zeros_like(gt_ref)

    for head in range(HEADS):
        part = slice(head * WIDE, (head + 1) * WIDE)
        s_hi, s_lo = halves(padded(sp_ref[0, head] + se_ref[head]))
        num = num_ref[:, cols(head)] + nn3(ph_ref[:, part], pl_ref[:, part], s_hi, s_lo)
        r = lax.rsqrt(jnp.mean(num * num, axis=-1, keepdims=True) + EPS)
        gain = gain_ref[:, cols(head)]
        unit = num * r
        out_ref[:, cols(head)] = unit * gain
        g = og_ref[:, cols(head)] * gain
        d = r * (g - unit * jnp.mean(g * unit, axis=-1, keepdims=True))
        d_hi, d_lo = halves(d)
        dh_ref[:, cols(head)] = d_hi
        dl_ref[:, cols(head)] = d_lo
        own = nn3(th_ref[head], tl_ref[head], d_hi, d_lo)
        gs_ref[0, head] = own
        gt_ref[head] += own


def forward(features, num, sp, se, og, gain):
    rows = lambda c: (c, 0)
    packed, turned = pl.BlockSpec((CHUNK, HEADS * WIDE), rows), pl.BlockSpec((HEADS, NF, CHUNK), lambda c: (0, 0, c))
    wide = pl.BlockSpec((CHUNK, 512), rows)
    states = pl.BlockSpec((1, HEADS, NF, HDIM), lambda c: (c, 0, 0, 0))
    return call(
        forward_kernel,
        (CHUNKS,),
        [packed, packed, turned, turned, wide, states, full(HEADS, NF, HDIM), wide, full(1, 512)],
        [wide, wide, wide, states, full(HEADS, NF, HDIM)],
        [
            arr((LEN, 512)), arr((LEN, 512), BF16), arr((LEN, 512), BF16),
            arr((CHUNKS, HEADS, NF, HDIM)), arr((HEADS, NF, HDIM)),
        ],
        (*features, num, sp, se, og, gain),
        flops=5e9,
        moved=18e6,
    )


def query_kernel(ql_ref, kr_ref, vh_ref, vl_ref, dh_ref, dl_ref, sp_ref, se_ref, pick_ref, bias_ref, back_ref, gq_ref):
    ql, kr = ql_ref[...], kr_ref[...]
    causal = lower()
    gq = jnp.zeros((CHUNK, WIDE), F32)
    du = jnp.zeros((CHUNK, 128), F32)
    for head in range(HEADS):
        mask = head_mask(WIDE, head)
        q = jnp.where(mask, ql, jnp.zeros_like(ql))
        k = jnp.where(mask, kr, jnp.zeros_like(kr))
        v_hi, v_lo = vh_ref[:, cols(head)], vl_ref[:, cols(head)]
        d_hi, d_lo = dh_ref[:, cols(head)], dl_ref[:, cols(head)]
        slope = jnp.where(causal, 1.0 + nt(q, kr), 0.0)
        gq = gq + nn((nt3(d_hi, d_lo, v_hi, v_lo) * slope).astype(BF16), k)
        s_hi, s_lo = halves(padded(sp_ref[0, head] + se_ref[head]))
        dp = nt3(d_hi, d_lo, s_hi, s_lo)
        a, b = factors(ql, pick_ref[head], bias_ref[...])
        dab_hi, dab_lo = halves(side(dp * b, dp * a))
        du = du + nn(dab_hi, back_ref[head]) + nn(dab_lo, back_ref[head])
    gq_ref[...] = gq[:, :128] + gq[:, 128:] + du


def key_kernel(ql_ref, kr_ref, vh_ref, vl_ref, dh_ref, dl_ref, gk_ref, gv_ref):
    ql, kr = ql_ref[...], kr_ref[...]
    row = lax.broadcasted_iota(jnp.int32, (CHUNK, CHUNK), 0)
    col = lax.broadcasted_iota(jnp.int32, (CHUNK, CHUNK), 1)
    causal = col >= row
    gk = jnp.zeros((CHUNK, WIDE), F32)
    for head in range(HEADS):
        mask = head_mask(WIDE, head)
        q = jnp.where(mask, ql, jnp.zeros_like(ql))
        k = jnp.where(mask, kr, jnp.zeros_like(kr))
        v_hi, v_lo = vh_ref[:, cols(head)], vl_ref[:, cols(head)]
        d_hi, d_lo = dh_ref[:, cols(head)], dl_ref[:, cols(head)]
        s = nt(k, ql)
        ds_hi, ds_lo = halves(nt3(v_hi, v_lo, d_hi, d_lo) * jnp.where(causal, 1.0 + s, 0.0))
        gk = gk + nn(ds_hi, q) + nn(ds_lo, q)
        w_hi, w_lo = halves(jnp.where(causal, 1.0 + s + 0.5 * s * s, 0.0))
        gv_ref[:, cols(head)] = nn3(w_hi, w_lo, d_hi, d_lo)
    gk_ref[...] = gk[:, :128] + pltpu.roll(gk[:, :128], 64, 1)


def backward(ql, kr, vh, vl, dh, dl, sp, se, pick, bias, back):
    rows = lambda c: (c, 0)
    narrow, wide = pl.BlockSpec((CHUNK, WIDE), rows), pl.BlockSpec((CHUNK, 512), rows)
    half = pl.BlockSpec((CHUNK, 128), rows)
    states = pl.BlockSpec((1, HEADS, NF, HDIM), lambda c: (c, 0, 0, 0))
    gk, gv = call(
        key_kernel,
        (CHUNKS,),
        [narrow, narrow, wide, wide, wide, wide],
        [half, wide],
        [arr((LEN, 128)), arr((LEN, 512))],
        (ql, kr, vh, vl, dh, dl),
        flops=8e9,
        moved=8e6,
    )
    gq = call(
        query_kernel,
        (CHUNKS,),
        [
            narrow, narrow, wide, wide, wide, wide, states, full(HEADS, NF, HDIM),
            full(HEADS, WIDE, 2 * WIDE), full(1, 2 * WIDE), full(HEADS, 2 * WIDE, 128),
        ],
        half,
        arr((LEN, 128)),
        (ql, kr, vh, vl, dh, dl, sp, se, pick, bias, back),
        flops=8e9,
        moved=8e6,
    )
    return gq, gk, gv


def later_kernel(first, last, kr_ref, vh_ref, vl_ref, gs_ref, gl_ref, gq_ref, gk_ref, gv_ref, pick_ref, bias_ref,
                 back_ref, o_ref, head_ref, total):
    @pl.when(pl.program_id(0) == 0)
    def _():
        begin = gl_ref[...]
        for c in range(CHUNKS - 1, last - 1, -1):
            begin = begin + gs_ref[c]
        total[...] = begin

    kr = kr_ref[...]
    du = jnp.zeros((CHUNK, 128), F32)
    for head in range(HEADS):
        a, b = factors(kr, pick_ref[head], bias_ref[...])
        l_hi, l_lo = halves(padded(total[head]))
        gained = nn((a * b).astype(BF16), side(l_hi, l_lo))
        v_hi, v_lo = vh_ref[:, cols(head)], vl_ref[:, cols(head)]
        o_ref[:, 128 + head * HDIM : 256 + head * HDIM] = gv_ref[:, cols(head)] + gained[:, :HDIM] + gained[:, HDIM:]
        dp = nt(side(v_hi, v_lo), side(l_hi, l_hi))
        dab_hi, dab_lo = halves(side(dp * b, dp * a))
        du = du + nn(dab_hi, back_ref[head]) + nn(dab_lo, back_ref[head])
    low = lax.broadcasted_iota(jnp.int32, (1, 128), 1) < 64
    o_ref[:, :128] = 0.5 * jnp.where(low, gq_ref[...], pltpu.roll(gk_ref[...] + du, 64, 1))
    head_ref[...] = o_ref[:8]
    total[...] += gs_ref[last - 1 - pl.program_id(0)]


def later(first, last, kr, vh, vl, gs, gl, gq, gk, gv, pick, bias, back):
    count = last - first
    rows = lambda c: (last - 1 - c, 0)
    to = lambda c: (count - 1 - c, 0)
    narrow, wide = pl.BlockSpec((CHUNK, WIDE), rows), pl.BlockSpec((CHUNK, 512), rows)
    half = pl.BlockSpec((CHUNK, 128), rows)
    return call(
        functools.partial(later_kernel, first, last),
        (count,),
        [
            narrow, wide, wide, full(CHUNKS, HEADS, NF, HDIM), full(HEADS, NF, HDIM), half, half, wide,
            full(HEADS, WIDE, 2 * WIDE), full(1, 2 * WIDE), full(HEADS, 2 * WIDE, 128),
        ],
        [pl.BlockSpec((CHUNK, 640), to), full(8, 640)],
        [arr((count * CHUNK, 640)), arr((8, 640))],
        (kr, vh, vl, gs, gl, gq, gk, gv, pick, bias, back),
        [pltpu.VMEM((HEADS, NF, HDIM), F32)],
        flops=2e9 * count,
        moved=3e6 * count,
    )


def conv_back(x, tail, taps):
    n = x.shape[0]
    row = lax.broadcasted_iota(jnp.int32, (8, 1), 0)
    once, twice = pltpu.roll(x, n - 1, 0), pltpu.roll(x, n - 2, 0)
    end1 = jnp.where(row == 7, tail[0:1], once[n - 8 :])
    end2 = jnp.where(row == 7, tail[1:2], jnp.where(row == 6, tail[0:1], twice[n - 8 :]))
    once = jnp.concatenate([once[: n - 8], end1], axis=0)
    twice = jnp.concatenate([twice[: n - 8], end2], axis=0)
    return (taps[0:1] * x + taps[1:2] * once + taps[2:3] * twice).astype(BF16)


def f32(x):
    return x.astype(F32)


def flip(x, axis, bit):
    return lax.ppermute(x, axis, [(i, i ^ bit) for i in range(lax.axis_size(axis))])


def input_kernel(me_ref, a_ref, b_ref, h_ref, t_ref, wv_ref, wqk_ref, z_ref, keep_ref, send_ref, dt_ref, d_ref):
    @pl.when(pl.program_id(0) == 0)
    def _():
        n = a_ref.shape[0]
        for start in range(0, LEN, STEP):
            end = start + STEP
            src = a_ref[start:end] if start < n else b_ref[start - n : end - n]
            if end == LEN:
                tail = h_ref[...]
            else:
                tail = a_ref[end : end + 8] if end < n else b_ref[end - n : end - n + 8]
            got = conv_back(src, tail, t_ref[...])
            d_ref[start:end] = got
            dt_ref[:, start:end] = got.T

    d = d_ref[...]
    half = LEN // 2
    bottom = []
    for i in range(2):
        part = slice(512 * i, 512 * (i + 1))
        got = nt(d[:, 128:], wv_ref[part]) + nn(d[:, :128], wqk_ref[:, part])
        z_ref[0, i] = got[:half].astype(BF16)
        bottom.append(got[half:])
    first = me_ref[0] == 0
    keep_ref[0] = jnp.where(first, bottom[0], bottom[1])
    send_ref[0] = jnp.where(first, bottom[1], bottom[0]).astype(BF16)


def input_products(side_y, a, b, halo, taps, wv, wqk):
    n, m, half = a.shape[0], b.shape[0], LEN // 2
    const = lambda *shape: pl.BlockSpec(shape, lambda i, me: (0,) * len(shape))
    block = pl.BlockSpec((1, half, 512), lambda i, me: (i, 0, 0))
    return call(
        input_kernel,
        (4,),
        [
            const(n, 640), const(m, 640), const(8, 640), const(3, 640),
            pl.BlockSpec((1024, 512), lambda i, me: (i, 0)), pl.BlockSpec((128, 1024), lambda i, me: (0, i)),
        ],
        [pl.BlockSpec((1, 2, half, 512), lambda i, me: (i, 0, 0, 0)), block, block, const(640, LEN)],
        [arr((4, 2, half, 512), BF16), arr((4, half, 512)), arr((4, half, 512), BF16), arr((640, LEN), BF16)],
        (side_y, a, b, halo, taps, wv, wqk),
        [pltpu.VMEM((LEN, 640), BF16)],
        prefetch=1,
        flops=2 * LEN * 640 * 4096,
        moved=20e6,
    )


def pair_kernel(keep_ref, came_ref, o_ref):
    o_ref[...] = (keep_ref[...] + f32(came_ref[...])).astype(BF16)


def top_kernel(me_ref, p_ref, keep_ref, send_ref):
    total = f32(p_ref[0])
    for i in range(1, 4):
        total = total + f32(p_ref[i])
    first = me_ref[0] == 0
    keep_ref[...] = jnp.where(first, total[0], total[1])
    send_ref[...] = jnp.where(first, total[1], total[0]).astype(BF16)


def last_kernel(keep_ref, came_ref, p_ref, o_ref):
    @pl.when(pl.program_id(0) < 2)
    def _():
        o_ref[...] = (keep_ref[...] + f32(came_ref[...])).astype(BF16)

    @pl.when(pl.program_id(0) >= 2)
    def _():
        total = f32(p_ref[0])
        for i in range(1, 4):
            total = total + f32(p_ref[i])
        o_ref[...] = total.astype(BF16)


def along_z(x):
    return lax.all_to_all(x, "tp", 0, 0, axis_index_groups=[[0, 2, 4, 6], [1, 3, 5, 7]])


def reduce_input_grad(side_y, by_z, keep, send, first, second):
    half, tile = LEN // 2, LEN // 4
    came = flip(send, "tp", 1)
    tops = along_z(by_z)
    block = pl.BlockSpec((1, half, 512), lambda i: (i, 0, 0))
    pairs = call(pair_kernel, (4,), [block, block], block, arr((4, half, 512), BF16), (keep, came), moved=8e6, after=first)
    rows = pl.BlockSpec((tile // 2, 512), lambda i, me: (i, 0))
    keep, send = call(
        top_kernel,
        (4,),
        [pl.BlockSpec((4, 2, tile // 2, 512), lambda i, me: (0, 0, i, 0))],
        [rows, rows],
        [arr((half, 512)), arr((half, 512), BF16)],
        (side_y, tops),
        prefetch=1,
        after=second,
        moved=6e6,
    )
    pairs = along_z(pairs)
    came = flip(send, "tp", 1)
    top = pl.BlockSpec((tile, 512), lambda i: (jnp.minimum(i, 1), 0))
    return call(
        last_kernel,
        (4,),
        [top, top, pl.BlockSpec((4, tile, 512), lambda i: (0, jnp.maximum(i - 2, 0), 0))],
        pl.BlockSpec((tile, 512), lambda i: (i, 0)),
        arr((LEN, 512), BF16),
        (keep, came, pairs),
        moved=5e6,
    )


def weight_kernel(dest_ref, d_ref, x_ref, y_ref, theirs_ref, ours_ref):
    first = dest_ref[8] == 0
    for r, ref in enumerate((x_ref, y_ref)):
        got = nn(d_ref[...], ref[...]).astype(BF16)
        half = got.shape[1] // 2
        low, high = got[:, :half], got[:, half:]
        theirs_ref[r] = jnp.where(first, high, low)
        ours_ref[r] = jnp.where(first, low, high)


def split_kernel(mine_ref, came_ref, *outs):
    step = pl.program_id(0)
    got = (f32(mine_ref[...]) + f32(came_ref[...])).astype(BF16)
    for j in range(4):

        @pl.when(step == j)
        def _(j=j):
            outs[j][...] = got


def row_sum_kernel(mine_ref, a_ref, b_ref, c_ref, keep_ref, send_ref):
    for r, out in enumerate((keep_ref, send_ref)):
        out[...] = (f32(mine_ref[r]) + f32(a_ref[r]) + f32(b_ref[r]) + f32(c_ref[r])).astype(out.dtype)


def finish_kernel(keep_ref, came_ref, q_ref, k_ref, v_ref):
    step = pl.program_id(0)
    total = keep_ref[...] + f32(came_ref[...])

    @pl.when(step == 0)
    def _():
        q_ref[...] = total[:64]
        k_ref[...] = total[64:]

    @pl.when(step > 0)
    def _():
        v_ref[...] = total.T


def to_x(x, by):
    return lax.ppermute(x, "seq", [(s, s // 8 * 8 + (s % 8 + 2 * by) % 8) for s in range(16)])


def weight_parts(dt, x):
    me = lax.axis_index("seq")
    y, px, core = me // 8, me // 2 % 4, me % 2
    width = x.shape[1] // 16
    chips = [(y ^ r) * 4 + (px + dx) % 4 for dx in range(4) for r in range(2)]
    dest = jnp.stack([*chips, core]).astype(jnp.int32)
    theirs, ours = call(
        weight_kernel,
        (4,),
        [pl.BlockSpec((640, LEN), lambda i, dest: (0, 0))]
        + [pl.BlockSpec((LEN, 2 * width), lambda i, dest, r=r: (0, dest[2 * i + r])) for r in range(2)],
        [pl.BlockSpec((2, 640, width), lambda i, dest: (i, 0, 0))] * 2,
        [arr((8, 640, width), BF16)] * 2,
        (dest, dt, x, x),
        prefetch=1,
        flops=2 * LEN * 640 * 4096,
        moved=15e6,
    )
    came = flip(theirs, "seq", 1)
    block = pl.BlockSpec((2, 640, width), lambda i: (i, 0, 0))
    return call(
        split_kernel,
        (4,),
        [block, block],
        [full(2, 640, width)] * 4,
        [arr((2, 640, width), BF16)] * 4,
        (ours, came),
        moved=8e6,
    )


def reduce_weight_grad(parts):
    mine, *rest = parts
    width = mine.shape[2]
    pair = pl.BlockSpec((2, 128, width), lambda i: (0, i, 0))
    one = pl.BlockSpec((128, width), lambda i: (i, 0))
    keep, send = call(
        row_sum_kernel,
        (5,),
        [pair] * 4,
        [one] * 2,
        [arr((640, width)), arr((640, width), BF16)],
        (mine, *rest),
        moved=4e6,
    )
    return keep, flip(send, "seq", 8)


def finish_weight_grad(keep, came, before):
    width = keep.shape[1]
    one = pl.BlockSpec((128, width), lambda i: (i, 0))
    return call(
        finish_kernel,
        (5,),
        [one, one],
        [full(64, width), full(64, width), pl.BlockSpec((width, 128), lambda i: (0, jnp.maximum(i - 1, 0)))],
        [arr((64, width)), arr((64, width)), arr((width, 512))],
        (keep, came),
        moved=2e6,
        after=(before,),
    )


def along(x, by):
    n = lax.axis_size("seq")
    return lax.ppermute(x, "seq", [(i, i + by) for i in range(n) if 0 <= i + by < n])


def local(inputs, w_query, w_key, w_value, taps_query, taps_key, taps_value, out_gain, out_grad):
    packed, bias, back = feature_matrices()
    pick_q, pick_k = (jnp.asarray(packed[i], BF16) for i in range(2))
    pick_qt, pick_kt = (jnp.asarray(packed[i].transpose(0, 2, 1), BF16) for i in range(2))
    back_q, back_k = (jnp.asarray(back[i], BF16) for i in range(2))
    bias, bias_t = jnp.asarray(bias), jnp.asarray(bias.T)
    wq_t, wk_t = w_query.T, w_key.T
    taps = jnp.concatenate([taps_query, taps_key, taps_value], axis=1)

    end, tail, wqk_t = project_end(inputs, wq_t, wk_t, w_value)
    tail = along(tail, 1)
    proj = project(inputs, wqk_t, w_value)
    ql, kr, vh, vl, before, own = shard_state(proj, end, tail, taps, pick_kt, bias_t)
    earlier = carried_in(own, False)
    num = inner(ql, kr, vh, vl)
    features = query_features(ql, pick_q, pick_qt, bias, bias_t)
    outputs, dh, dl, grads, own_grad = forward(features, num, before, earlier, out_grad, out_gain.reshape(1, 512))
    after = carried_in(own_grad, True)
    gq, gk, gv = backward(ql, kr, vh, vl, dh, dl, before, earlier, pick_q, bias, back_q)
    rest = (kr, vh, vl, grads, after, gq, gk, gv, pick_k, bias, back_k)
    ga, halo = later(0, 1, *rest)
    halo = along(halo, -1)
    gb, _ = later(1, CHUNKS, *rest)
    side_y = (lax.axis_index("tp") % 2).astype(jnp.int32).reshape(1)
    by_z, keep, send, dt = input_products(side_y, ga, gb, halo, taps, w_value, wqk_t)
    mine, *rest = weight_parts(dt, inputs)
    parts = [mine, *(to_x(part, dx) for dx, part in enumerate(rest, 1))]
    own, came = reduce_weight_grad(parts)
    input_grad = reduce_input_grad(side_y, by_z, keep, send, parts[1:], ())
    grad_query, grad_key, grad_value = finish_weight_grad(own, came, input_grad)
    return (outputs, input_grad, grad_query.T, grad_key.T, grad_value)


def solution(mesh):
    return jax.shard_map(
        local,
        mesh=mesh,
        in_specs=(
            P("seq", None),
            P(None, "tp"),
            P(None, "tp"),
            P(None, "tp"),
            P(None, "tp"),
            P(None, "tp"),
            P(None, "tp"),
            P("tp"),
            P("seq", "tp"),
        ),
        out_specs=(P("seq", "tp"), P("seq", "tp"), P("seq", "tp"), P("seq", "tp"), P("seq", "tp")),
        check_vma=False,
    )
```

```python
import functools

import jax
import jax.numpy as jnp
import numpy as np
from jax import lax
from jax.experimental import pallas as pl
from jax.experimental.pallas import tpu as pltpu
from jax.sharding import PartitionSpec as P

FEAT = 16
HDIM = 128
HEADS = 4
CHUNK = 256
LEN = 1024
CHUNKS = LEN // CHUNK
NF = 160
WIDE = 256
EPS = 1e-05
STEP = 128
F32, BF16 = jnp.float32, jnp.bfloat16


def feature_matrices():
    pairs = [(i, j) for i in range(FEAT) for j in range(i, FEAT)]
    pick = np.zeros((2, HEADS, 64, 2 * WIDE), np.float32)
    bias = np.zeros((1, 2 * WIDE), np.float32)
    for head in range(HEADS):
        base = head * FEAT
        for f, (i, j) in enumerate(pairs):
            pick[:, head, base + i, f] = 1.0
            pick[0, head, base + j, WIDE + f] = 0.5 if i == j else 1.0
            pick[1, head, base + j, WIDE + f] = 1.0
        for i in range(FEAT):
            pick[:, head, base + i, len(pairs) + i] = 1.0
    ones = len(pairs) + FEAT
    bias[0, ones] = 1.0
    bias[0, WIDE + len(pairs) : WIDE + ones + 1] = 1.0
    packed = np.zeros((2, HEADS, WIDE, 2 * WIDE), np.float32)
    packed[0, :, 0:64] = pick[0]
    packed[0, :, 64:128] = pick[0]
    packed[1, :, 0:64] = pick[1]
    packed[1, :, 128:192] = pick[1]
    back = np.zeros((2, HEADS, 2 * WIDE, 128), np.float32)
    back[:, :, :, 0:64] = pick.transpose(0, 1, 3, 2)
    return packed, bias, back


def nn(a, b):
    return lax.dot_general(a, b, (((1,), (0,)), ((), ())), preferred_element_type=F32)


def nt(a, b):
    return lax.dot_general(a, b, (((1,), (1,)), ((), ())), preferred_element_type=F32)


def halves(x):
    hi = x.astype(BF16)
    return hi, (x - hi.astype(F32)).astype(BF16)


def side(*parts):
    return jnp.concatenate(parts, axis=1)


def nn3(a_hi, a_lo, b_hi, b_lo):
    both = nn(a_hi, side(b_hi, b_lo))
    n = b_hi.shape[1]
    return both[:, :n] + both[:, n:] + nn(a_lo, b_hi)


def nt3(a_hi, a_lo, b_hi, b_lo):
    return nt(side(a_hi, a_lo), side(b_hi, b_hi)) + nt(a_hi, b_lo)


def factors(packed, pick, bias):
    both = nn(packed, pick) + bias
    return both[:, :WIDE], both[:, WIDE:]


def padded(state):
    return jnp.concatenate([state, jnp.zeros((WIDE - NF, HDIM), F32)], axis=0)


def head_mask(width, head):
    lane = lax.broadcasted_iota(jnp.int32, (1, width), 1)
    return (lane % 64) // FEAT == head


def cols(head):
    return slice(head * HDIM, (head + 1) * HDIM)


def call(body, grid, ins, outs, shapes, args, scratch=(), prefetch=0, flops=0, moved=0, after=()):
    if after:
        kept, skip = body, len(after)
        at = prefetch + len(ins)
        body = lambda *refs: kept(*refs[:at], *refs[at + skip :])
        ins = [*ins] + [pl.BlockSpec(memory_space=pl.ANY)] * skip
        args = (*args, *after)
    return pl.pallas_call(
        body,
        grid_spec=pltpu.PrefetchScalarGridSpec(
            num_scalar_prefetch=prefetch, grid=grid, in_specs=ins, out_specs=outs, scratch_shapes=list(scratch)
        ),
        out_shape=shapes,
        compiler_params=pltpu.CompilerParams(vmem_limit_bytes=56 * 2**20),
        cost_estimate=pl.CostEstimate(flops=int(flops), bytes_accessed=int(moved), transcendentals=0),
    )(*args)


def full(*shape):
    return pl.BlockSpec(shape, lambda *_: (0,) * len(shape))


def arr(shape, dtype=F32):
    return jax.ShapeDtypeStruct(shape, dtype)


def end_kernel(x_ref, wq_ref, wk_ref, wv_ref, o_ref, tail_ref, wqk_ref):
    step = pl.program_id(0)
    wqk_ref[0:64] = wq_ref[...]
    wqk_ref[64:128] = wk_ref[...]
    x = x_ref[...]
    qk, v = nt(x, wqk_ref[...]), nn(x, wv_ref[...])

    @pl.when(step == 0)
    def _():
        o_ref[:, :128] = qk
        o_ref[:, 128:] = v

    @pl.when(step > 0)
    def _():
        o_ref[:, :128] += qk
        o_ref[:, 128:] += v

    tail_ref[...] = o_ref[CHUNK - 8 :]


def project_end(x, wq_t, wk_t, wv):
    depth = x.shape[1]
    part = depth // 4
    at = lambda k: (0, k)
    return call(
        end_kernel,
        (4,),
        [
            pl.BlockSpec((CHUNK, part), lambda k: (CHUNKS - 1, k)),
            pl.BlockSpec((64, part), at),
            pl.BlockSpec((64, part), at),
            pl.BlockSpec((part, 512), lambda k: (k, 0)),
        ],
        [full(CHUNK, 640), full(8, 640), pl.BlockSpec((128, part), at)],
        [arr((CHUNK, 640)), arr((8, 640)), arr((128, depth), BF16)],
        (x, wq_t, wk_t, wv),
        flops=2 * CHUNK * depth * 640,
        moved=8e6,
    )


def project_kernel(x_ref, wqk_ref, wv_ref, o_ref):
    x = x_ref[...]
    o_ref[:, :128] = nt(x, wqk_ref[...])
    o_ref[:, 128:] = nn(x, wv_ref[...])


def project(x, wqk_t, wv):
    depth = x.shape[1]
    rows = lambda c: (c, 0)
    return call(
        project_kernel,
        (CHUNKS - 1,),
        [pl.BlockSpec((CHUNK, depth), rows), full(128, depth), full(depth, 512)],
        pl.BlockSpec((CHUNK, 640), rows),
        arr((LEN - CHUNK, 640)),
        (x, wqk_t, wv),
        flops=2 * (LEN - CHUNK) * depth * 640,
        moved=12e6,
    )


def conv(x, tail, taps):
    row = lax.broadcasted_iota(jnp.int32, (8, 1), 0)
    once, twice = pltpu.roll(x, 1, 0), pltpu.roll(x, 2, 0)
    top1 = jnp.where(row == 0, tail[7:8], once[0:8])
    top2 = jnp.where(row == 0, tail[6:7], jnp.where(row == 1, tail[7:8], twice[0:8]))
    once = jnp.concatenate([top1, once[8:]], axis=0)
    twice = jnp.concatenate([top2, twice[8:]], axis=0)
    return taps[0:1] * x + taps[1:2] * once + taps[2:3] * twice


def state_kernel(
    a_ref, b_ref, before_ref, tail_ref, taps_ref, pick_ref, biast_ref,
    ql_ref, kr_ref, vh_ref, vl_ref, sp_ref, st_ref,
):
    c = pl.program_id(0)

    @pl.when(c == 0)
    def _():
        st_ref[...] = jnp.zeros_like(st_ref)

    x = jnp.where(c < CHUNKS - 1, a_ref[...], b_ref[...])
    both = conv(x, jnp.where(c > 0, before_ref[...], tail_ref[...]), taps_ref[...])
    qk, v = both[:, :128] * 0.5, both[:, 128:]
    lane = lax.broadcasted_iota(jnp.int32, (1, 128), 1)
    low = lane < 64
    turned = pltpu.roll(qk, 64, 1)
    hi = qk.astype(BF16).astype(F32)
    lo = qk - hi
    turned_hi = turned.astype(BF16).astype(F32)
    turned_lo = turned - turned_hi
    zero = jnp.zeros_like(qk)
    ql = side(jnp.where(low, hi, turned_lo), jnp.where(low, hi, zero)).astype(BF16)
    kr = side(jnp.where(low, turned_hi, hi), jnp.where(low, turned_lo, zero)).astype(BF16)
    ql_ref[...] = ql
    kr_ref[...] = kr
    v_hi, v_lo = halves(v)
    vh_ref[...] = v_hi
    vl_ref[...] = v_lo
    for head in range(HEADS):
        ab = nt(pick_ref[head], kr) + biast_ref[...]
        p_hi, p_lo = halves(ab[:NF] * ab[WIDE : WIDE + NF])
        own = nn3(p_hi, p_lo, v_hi[:, cols(head)], v_lo[:, cols(head)])
        sp_ref[0, head] = st_ref[head]
        st_ref[head] += own


def shard_state(proj, end, tail, taps, pick_kt, bias_t):
    rows = lambda c: (c, 0)
    before = lambda c: (jnp.maximum(c * (CHUNK // 8) - 1, 0), 0)
    return call(
        state_kernel,
        (CHUNKS,),
        [
            pl.BlockSpec((CHUNK, 640), lambda c: (jnp.minimum(c, CHUNKS - 2), 0)),
            full(CHUNK, 640),
            pl.BlockSpec((8, 640), before),
            full(8, 640),
            full(3, 640),
            full(HEADS, 2 * WIDE, WIDE),
            full(2 * WIDE, 1),
        ],
        [
            pl.BlockSpec((CHUNK, WIDE), rows),
            pl.BlockSpec((CHUNK, WIDE), rows),
            pl.BlockSpec((CHUNK, 512), rows),
            pl.BlockSpec((CHUNK, 512), rows),
            pl.BlockSpec((1, HEADS, NF, HDIM), lambda c: (c, 0, 0, 0)),
            full(HEADS, NF, HDIM),
        ],
        [
            arr((LEN, WIDE), BF16),
            arr((LEN, WIDE), BF16),
            arr((LEN, 512), BF16),
            arr((LEN, 512), BF16),
            arr((CHUNKS, HEADS, NF, HDIM)),
            arr((HEADS, NF, HDIM)),
        ],
        (proj, end, proj, tail, taps, pick_kt, bias_t),
        flops=4e9,
        moved=15e6,
    )


def running_kernel(backward, x_ref, o_ref):
    count = x_ref.shape[0]
    order = range(count - 1, -1, -1) if backward else range(count)
    total = jnp.zeros(x_ref.shape[1:], F32)
    for i in order:
        o_ref[i] = total
        total = total + x_ref[i]


def carried_in(state, backward):
    count = lax.axis_size("seq")
    rows = HEADS * NF // count
    pieces = lax.all_to_all(state.reshape(count, rows, HDIM), "seq", 0, 0)
    shape = (count, rows, HDIM)
    sums = call(
        functools.partial(running_kernel, backward), (1,), [full(*shape)], full(*shape), arr(shape), (pieces,), moved=6e5
    )
    return lax.all_to_all(sums, "seq", 0, 0).reshape(HEADS, NF, HDIM)


def lower():
    row = lax.broadcasted_iota(jnp.int32, (CHUNK, CHUNK), 0)
    col = lax.broadcasted_iota(jnp.int32, (CHUNK, CHUNK), 1)
    return row >= col


def inner_kernel(ql_ref, kr_ref, vh_ref, vl_ref, num_ref):
    ql, kr = ql_ref[...], kr_ref[...]
    causal = lower()
    for head in range(HEADS):
        mine = jnp.where(head_mask(WIDE, head), ql, jnp.zeros_like(ql))
        s = nt(mine, kr)
        w_hi, w_lo = halves(jnp.where(causal, 1.0 + s + 0.5 * s * s, 0.0))
        num_ref[:, cols(head)] = nn3(w_hi, w_lo, vh_ref[:, cols(head)], vl_ref[:, cols(head)])


def inner(ql, kr, vh, vl):
    rows = lambda c: (c, 0)
    narrow, wide = pl.BlockSpec((CHUNK, WIDE), rows), pl.BlockSpec((CHUNK, 512), rows)
    return call(
        inner_kernel, (CHUNKS,), [narrow, narrow, wide, wide], wide, arr((LEN, 512)), (ql, kr, vh, vl), flops=6e9, moved=6e6
    )


def feature_kernel(ql_ref, pick_ref, pickt_ref, bias_ref, biast_ref, ph_ref, pl_ref, th_ref, tl_ref):
    ql = ql_ref[...]
    for head in range(HEADS):
        part = slice(head * WIDE, (head + 1) * WIDE)
        a, b = factors(ql, pick_ref[head], bias_ref[...])
        ph_ref[:, part], pl_ref[:, part] = halves(a * b)
        ab = nt(pickt_ref[head], ql) + biast_ref[...]
        th_ref[head], tl_ref[head] = halves(ab[:NF] * ab[WIDE : WIDE + NF])


def query_features(ql, pick, pick_t, bias, bias_t):
    rows = lambda c: (c, 0)
    wide, turned = pl.BlockSpec((CHUNK, HEADS * WIDE), rows), pl.BlockSpec((HEADS, NF, CHUNK), lambda c: (0, 0, c))
    return call(
        feature_kernel,
        (CHUNKS,),
        [
            pl.BlockSpec((CHUNK, WIDE), rows),
            full(HEADS, WIDE, 2 * WIDE), full(HEADS, 2 * WIDE, WIDE), full(1, 2 * WIDE), full(2 * WIDE, 1),
        ],
        [wide, wide, turned, turned],
        [arr((LEN, HEADS * WIDE), BF16)] * 2 + [arr((HEADS, NF, LEN), BF16)] * 2,
        (ql, pick, pick_t, bias, bias_t),
        flops=4e9,
        moved=10e6,
    )


def forward_kernel(ph_ref, pl_ref, th_ref, tl_ref, num_ref, sp_ref, se_ref, og_ref, gain_ref,
                   out_ref, dh_ref, dl_ref, gs_ref, gt_ref):
    @pl.when(pl.program_id(0) == 0)
    def _():
        gt_ref[...] = jnp.zeros_like(gt_ref)

    for head in range(HEADS):
        part = slice(head * WIDE, (head + 1) * WIDE)
        s_hi, s_lo = halves(padded(sp_ref[0, head] + se_ref[head]))
        num = num_ref[:, cols(head)] + nn3(ph_ref[:, part], pl_ref[:, part], s_hi, s_lo)
        r = lax.rsqrt(jnp.mean(num * num, axis=-1, keepdims=True) + EPS)
        gain = gain_ref[:, cols(head)]
        unit = num * r
        out_ref[:, cols(head)] = unit * gain
        g = og_ref[:, cols(head)] * gain
        d = r * (g - unit * jnp.mean(g * unit, axis=-1, keepdims=True))
        d_hi, d_lo = halves(d)
        dh_ref[:, cols(head)] = d_hi
        dl_ref[:, cols(head)] = d_lo
        own = nn3(th_ref[head], tl_ref[head], d_hi, d_lo)
        gs_ref[0, head] = own
        gt_ref[head] += own


def forward(features, num, sp, se, og, gain):
    rows = lambda c: (c, 0)
    packed, turned = pl.BlockSpec((CHUNK, HEADS * WIDE), rows), pl.BlockSpec((HEADS, NF, CHUNK), lambda c: (0, 0, c))
    wide = pl.BlockSpec((CHUNK, 512), rows)
    states = pl.BlockSpec((1, HEADS, NF, HDIM), lambda c: (c, 0, 0, 0))
    return call(
        forward_kernel,
        (CHUNKS,),
        [packed, packed, turned, turned, wide, states, full(HEADS, NF, HDIM), wide, full(1, 512)],
        [wide, wide, wide, states, full(HEADS, NF, HDIM)],
        [
            arr((LEN, 512)), arr((LEN, 512), BF16), arr((LEN, 512), BF16),
            arr((CHUNKS, HEADS, NF, HDIM)), arr((HEADS, NF, HDIM)),
        ],
        (*features, num, sp, se, og, gain),
        flops=5e9,
        moved=18e6,
    )


def query_kernel(ql_ref, kr_ref, vh_ref, vl_ref, dh_ref, dl_ref, sp_ref, se_ref, pick_ref, bias_ref, back_ref, gq_ref):
    ql, kr = ql_ref[...], kr_ref[...]
    causal = lower()
    gq = jnp.zeros((CHUNK, WIDE), F32)
    du = jnp.zeros((CHUNK, 128), F32)
    for head in range(HEADS):
        mask = head_mask(WIDE, head)
        q = jnp.where(mask, ql, jnp.zeros_like(ql))
        k = jnp.where(mask, kr, jnp.zeros_like(kr))
        v_hi, v_lo = vh_ref[:, cols(head)], vl_ref[:, cols(head)]
        d_hi, d_lo = dh_ref[:, cols(head)], dl_ref[:, cols(head)]
        slope = jnp.where(causal, 1.0 + nt(q, kr), 0.0)
        gq = gq + nn((nt3(d_hi, d_lo, v_hi, v_lo) * slope).astype(BF16), k)
        s_hi, s_lo = halves(padded(sp_ref[0, head] + se_ref[head]))
        dp = nt3(d_hi, d_lo, s_hi, s_lo)
        a, b = factors(ql, pick_ref[head], bias_ref[...])
        dab_hi, dab_lo = halves(side(dp * b, dp * a))
        du = du + nn(dab_hi, back_ref[head]) + nn(dab_lo, back_ref[head])
    gq_ref[...] = gq[:, :128] + gq[:, 128:] + du


def key_kernel(ql_ref, kr_ref, vh_ref, vl_ref, dh_ref, dl_ref, gk_ref, gv_ref):
    ql, kr = ql_ref[...], kr_ref[...]
    row = lax.broadcasted_iota(jnp.int32, (CHUNK, CHUNK), 0)
    col = lax.broadcasted_iota(jnp.int32, (CHUNK, CHUNK), 1)
    causal = col >= row
    gk = jnp.zeros((CHUNK, WIDE), F32)
    for head in range(HEADS):
        mask = head_mask(WIDE, head)
        q = jnp.where(mask, ql, jnp.zeros_like(ql))
        k = jnp.where(mask, kr, jnp.zeros_like(kr))
        v_hi, v_lo = vh_ref[:, cols(head)], vl_ref[:, cols(head)]
        d_hi, d_lo = dh_ref[:, cols(head)], dl_ref[:, cols(head)]
        s = nt(k, ql)
        ds_hi, ds_lo = halves(nt3(v_hi, v_lo, d_hi, d_lo) * jnp.where(causal, 1.0 + s, 0.0))
        gk = gk + nn(ds_hi, q) + nn(ds_lo, q)
        w_hi, w_lo = halves(jnp.where(causal, 1.0 + s + 0.5 * s * s, 0.0))
        gv_ref[:, cols(head)] = nn3(w_hi, w_lo, d_hi, d_lo)
    gk_ref[...] = gk[:, :128] + pltpu.roll(gk[:, :128], 64, 1)


def backward(ql, kr, vh, vl, dh, dl, sp, se, pick, bias, back):
    rows = lambda c: (c, 0)
    narrow, wide = pl.BlockSpec((CHUNK, WIDE), rows), pl.BlockSpec((CHUNK, 512), rows)
    half = pl.BlockSpec((CHUNK, 128), rows)
    states = pl.BlockSpec((1, HEADS, NF, HDIM), lambda c: (c, 0, 0, 0))
    gk, gv = call(
        key_kernel,
        (CHUNKS,),
        [narrow, narrow, wide, wide, wide, wide],
        [half, wide],
        [arr((LEN, 128)), arr((LEN, 512))],
        (ql, kr, vh, vl, dh, dl),
        flops=8e9,
        moved=8e6,
    )
    gq = call(
        query_kernel,
        (CHUNKS,),
        [
            narrow, narrow, wide, wide, wide, wide, states, full(HEADS, NF, HDIM),
            full(HEADS, WIDE, 2 * WIDE), full(1, 2 * WIDE), full(HEADS, 2 * WIDE, 128),
        ],
        half,
        arr((LEN, 128)),
        (ql, kr, vh, vl, dh, dl, sp, se, pick, bias, back),
        flops=8e9,
        moved=8e6,
    )
    return gq, gk, gv


def later_kernel(first, last, kr_ref, vh_ref, vl_ref, gs_ref, gl_ref, gq_ref, gk_ref, gv_ref, pick_ref, bias_ref,
                 back_ref, o_ref, head_ref, total):
    @pl.when(pl.program_id(0) == 0)
    def _():
        begin = gl_ref[...]
        for c in range(CHUNKS - 1, last - 1, -1):
            begin = begin + gs_ref[c]
        total[...] = begin

    kr = kr_ref[...]
    du = jnp.zeros((CHUNK, 128), F32)
    for head in range(HEADS):
        a, b = factors(kr, pick_ref[head], bias_ref[...])
        l_hi, l_lo = halves(padded(total[head]))
        gained = nn((a * b).astype(BF16), side(l_hi, l_lo))
        v_hi, v_lo = vh_ref[:, cols(head)], vl_ref[:, cols(head)]
        o_ref[:, 128 + head * HDIM : 256 + head * HDIM] = gv_ref[:, cols(head)] + gained[:, :HDIM] + gained[:, HDIM:]
        dp = nt(side(v_hi, v_lo), side(l_hi, l_hi))
        dab_hi, dab_lo = halves(side(dp * b, dp * a))
        du = du + nn(dab_hi, back_ref[head]) + nn(dab_lo, back_ref[head])
    low = lax.broadcasted_iota(jnp.int32, (1, 128), 1) < 64
    o_ref[:, :128] = 0.5 * jnp.where(low, gq_ref[...], pltpu.roll(gk_ref[...] + du, 64, 1))
    head_ref[...] = o_ref[:8]
    total[...] += gs_ref[last - 1 - pl.program_id(0)]


def later(first, last, kr, vh, vl, gs, gl, gq, gk, gv, pick, bias, back):
    count = last - first
    rows = lambda c: (last - 1 - c, 0)
    to = lambda c: (count - 1 - c, 0)
    narrow, wide = pl.BlockSpec((CHUNK, WIDE), rows), pl.BlockSpec((CHUNK, 512), rows)
    half = pl.BlockSpec((CHUNK, 128), rows)
    return call(
        functools.partial(later_kernel, first, last),
        (count,),
        [
            narrow, wide, wide, full(CHUNKS, HEADS, NF, HDIM), full(HEADS, NF, HDIM), half, half, wide,
            full(HEADS, WIDE, 2 * WIDE), full(1, 2 * WIDE), full(HEADS, 2 * WIDE, 128),
        ],
        [pl.BlockSpec((CHUNK, 640), to), full(8, 640)],
        [arr((count * CHUNK, 640)), arr((8, 640))],
        (kr, vh, vl, gs, gl, gq, gk, gv, pick, bias, back),
        [pltpu.VMEM((HEADS, NF, HDIM), F32)],
        flops=2e9 * count,
        moved=3e6 * count,
    )


def conv_back(x, tail, taps):
    n = x.shape[0]
    row = lax.broadcasted_iota(jnp.int32, (8, 1), 0)
    once, twice = pltpu.roll(x, n - 1, 0), pltpu.roll(x, n - 2, 0)
    end1 = jnp.where(row == 7, tail[0:1], once[n - 8 :])
    end2 = jnp.where(row == 7, tail[1:2], jnp.where(row == 6, tail[0:1], twice[n - 8 :]))
    once = jnp.concatenate([once[: n - 8], end1], axis=0)
    twice = jnp.concatenate([twice[: n - 8], end2], axis=0)
    return (taps[0:1] * x + taps[1:2] * once + taps[2:3] * twice).astype(BF16)


def f32(x):
    return x.astype(F32)


def flip(x, axis, bit):
    return lax.ppermute(x, axis, [(i, i ^ bit) for i in range(lax.axis_size(axis))])


def input_kernel(me_ref, a_ref, b_ref, h_ref, t_ref, wv_ref, wqk_ref, z_ref, keep_ref, send_ref, dt_ref, d_ref):
    @pl.when(pl.program_id(0) == 0)
    def _():
        n = a_ref.shape[0]
        for start in range(0, LEN, STEP):
            end = start + STEP
            src = a_ref[start:end] if start < n else b_ref[start - n : end - n]
            if end == LEN:
                tail = h_ref[...]
            else:
                tail = a_ref[end : end + 8] if end < n else b_ref[end - n : end - n + 8]
            got = conv_back(src, tail, t_ref[...])
            d_ref[start:end] = got
            dt_ref[:, start:end] = got.T

    d = d_ref[...]
    half = LEN // 2
    bottom = []
    for i in range(2):
        part = slice(512 * i, 512 * (i + 1))
        got = nt(d[:, 128:], wv_ref[part]) + nn(d[:, :128], wqk_ref[:, part])
        z_ref[0, i] = got[:half].astype(BF16)
        bottom.append(got[half:])
    first = me_ref[0] == 0
    keep_ref[0] = jnp.where(first, bottom[0], bottom[1])
    send_ref[0] = jnp.where(first, bottom[1], bottom[0]).astype(BF16)


def input_products(side_y, a, b, halo, taps, wv, wqk):
    n, m, half = a.shape[0], b.shape[0], LEN // 2
    const = lambda *shape: pl.BlockSpec(shape, lambda i, me: (0,) * len(shape))
    block = pl.BlockSpec((1, half, 512), lambda i, me: (i, 0, 0))
    return call(
        input_kernel,
        (4,),
        [
            const(n, 640), const(m, 640), const(8, 640), const(3, 640),
            pl.BlockSpec((1024, 512), lambda i, me: (i, 0)), pl.BlockSpec((128, 1024), lambda i, me: (0, i)),
        ],
        [pl.BlockSpec((1, 2, half, 512), lambda i, me: (i, 0, 0, 0)), block, block, const(640, LEN)],
        [arr((4, 2, half, 512), BF16), arr((4, half, 512)), arr((4, half, 512), BF16), arr((640, LEN), BF16)],
        (side_y, a, b, halo, taps, wv, wqk),
        [pltpu.VMEM((LEN, 640), BF16)],
        prefetch=1,
        flops=2 * LEN * 640 * 4096,
        moved=20e6,
    )


def pair_kernel(keep_ref, came_ref, o_ref):
    o_ref[...] = (keep_ref[...] + f32(came_ref[...])).astype(BF16)


def top_kernel(me_ref, p_ref, keep_ref, send_ref):
    total = f32(p_ref[0])
    for i in range(1, 4):
        total = total + f32(p_ref[i])
    first = me_ref[0] == 0
    keep_ref[...] = jnp.where(first, total[0], total[1])
    send_ref[...] = jnp.where(first, total[1], total[0]).astype(BF16)


def last_kernel(keep_ref, came_ref, p_ref, o_ref):
    @pl.when(pl.program_id(0) < 2)
    def _():
        o_ref[...] = (keep_ref[...] + f32(came_ref[...])).astype(BF16)

    @pl.when(pl.program_id(0) >= 2)
    def _():
        total = f32(p_ref[0])
        for i in range(1, 4):
            total = total + f32(p_ref[i])
        o_ref[...] = total.astype(BF16)


def along_z(x):
    return lax.all_to_all(x, "tp", 0, 0, axis_index_groups=[[0, 2, 4, 6], [1, 3, 5, 7]])


def reduce_input_grad(side_y, by_z, keep, send, first, last):
    half, tile = LEN // 2, LEN // 4
    came = flip(send, "tp", 1)
    tops = along_z(by_z)
    block = pl.BlockSpec((1, half, 512), lambda i: (i, 0, 0))
    mine = keep
    rows = pl.BlockSpec((tile // 2, 512), lambda i, me: (i, 0))
    keep, send = call(
        top_kernel,
        (4,),
        [pl.BlockSpec((4, 2, tile // 2, 512), lambda i, me: (0, 0, i, 0))],
        [rows, rows],
        [arr((half, 512)), arr((half, 512), BF16)],
        (side_y, tops),
        prefetch=1,
        moved=6e6,
    )
    pairs = call(
        pair_kernel,
        (4,),
        [block, block],
        block,
        arr((4, half, 512), BF16),
        (mine, came),
        moved=8e6,
        after=(*first, send),
    )
    pairs = along_z(pairs)
    came = flip(send, "tp", 1)
    top = pl.BlockSpec((tile, 512), lambda i: (jnp.minimum(i, 1), 0))
    return call(
        last_kernel,
        (4,),
        [top, top, pl.BlockSpec((4, tile, 512), lambda i: (0, jnp.maximum(i - 2, 0), 0))],
        pl.BlockSpec((tile, 512), lambda i: (i, 0)),
        arr((LEN, 512), BF16),
        (keep, came, pairs),
        moved=5e6,
        after=last,
    )


def weight_kernel(dest_ref, d_ref, x_ref, y_ref, theirs_ref, ours_ref):
    first = dest_ref[8] == 0
    for r, ref in enumerate((x_ref, y_ref)):
        got = nn(d_ref[...], ref[...]).astype(BF16)
        half = got.shape[1] // 2
        low, high = got[:, :half], got[:, half:]
        theirs_ref[r] = jnp.where(first, high, low)
        ours_ref[r] = jnp.where(first, low, high)


def split_kernel(mine_ref, came_ref, *outs):
    step = pl.program_id(0)
    got = (f32(mine_ref[...]) + f32(came_ref[...])).astype(BF16)
    for j in range(4):

        @pl.when(step == j)
        def _(j=j):
            outs[j][...] = got


def row_sum_kernel(mine_ref, a_ref, b_ref, c_ref, keep_ref, send_ref):
    for r, out in enumerate((keep_ref, send_ref)):
        out[...] = (f32(mine_ref[r]) + f32(a_ref[r]) + f32(b_ref[r]) + f32(c_ref[r])).astype(out.dtype)


def finish_kernel(keep_ref, came_ref, q_ref, k_ref, v_ref):
    step = pl.program_id(0)
    total = keep_ref[...] + f32(came_ref[...])

    @pl.when(step == 0)
    def _():
        q_ref[...] = total[:64]
        k_ref[...] = total[64:]

    @pl.when(step > 0)
    def _():
        v_ref[...] = total.T


def to_x(x, by):
    return lax.ppermute(x, "seq", [(s, s // 8 * 8 + (s % 8 + 2 * by) % 8) for s in range(16)])


def weight_parts(dt, x):
    me = lax.axis_index("seq")
    y, px, core = me // 8, me // 2 % 4, me % 2
    width = x.shape[1] // 16
    chips = [(y ^ r) * 4 + (px + dx) % 4 for dx in range(4) for r in range(2)]
    dest = jnp.stack([*chips, core]).astype(jnp.int32)
    theirs, ours = call(
        weight_kernel,
        (4,),
        [pl.BlockSpec((640, LEN), lambda i, dest: (0, 0))]
        + [pl.BlockSpec((LEN, 2 * width), lambda i, dest, r=r: (0, dest[2 * i + r])) for r in range(2)],
        [pl.BlockSpec((2, 640, width), lambda i, dest: (i, 0, 0))] * 2,
        [arr((8, 640, width), BF16)] * 2,
        (dest, dt, x, x),
        prefetch=1,
        flops=2 * LEN * 640 * 4096,
        moved=15e6,
    )
    came = flip(theirs, "seq", 1)
    block = pl.BlockSpec((2, 640, width), lambda i: (i, 0, 0))
    return call(
        split_kernel,
        (4,),
        [block, block],
        [full(2, 640, width)] * 4,
        [arr((2, 640, width), BF16)] * 4,
        (ours, came),
        moved=8e6,
    )


def reduce_weight_grad(parts):
    mine, *rest = parts
    width = mine.shape[2]
    pair = pl.BlockSpec((2, 128, width), lambda i: (0, i, 0))
    one = pl.BlockSpec((128, width), lambda i: (i, 0))
    keep, send = call(
        row_sum_kernel,
        (5,),
        [pair] * 4,
        [one] * 2,
        [arr((640, width)), arr((640, width), BF16)],
        (mine, *rest),
        moved=4e6,
    )
    return keep, flip(send, "seq", 8)


def finish_weight_grad(keep, came):
    width = keep.shape[1]
    one = pl.BlockSpec((128, width), lambda i: (i, 0))
    return call(
        finish_kernel,
        (5,),
        [one, one],
        [full(64, width), full(64, width), pl.BlockSpec((width, 128), lambda i: (0, jnp.maximum(i - 1, 0)))],
        [arr((64, width)), arr((64, width)), arr((width, 512))],
        (keep, came),
        moved=2e6,
    )


def along(x, by):
    n = lax.axis_size("seq")
    return lax.ppermute(x, "seq", [(i, i + by) for i in range(n) if 0 <= i + by < n])


def local(inputs, w_query, w_key, w_value, taps_query, taps_key, taps_value, out_gain, out_grad):
    packed, bias, back = feature_matrices()
    pick_q, pick_k = (jnp.asarray(packed[i], BF16) for i in range(2))
    pick_qt, pick_kt = (jnp.asarray(packed[i].transpose(0, 2, 1), BF16) for i in range(2))
    back_q, back_k = (jnp.asarray(back[i], BF16) for i in range(2))
    bias, bias_t = jnp.asarray(bias), jnp.asarray(bias.T)
    wq_t, wk_t = w_query.T, w_key.T
    taps = jnp.concatenate([taps_query, taps_key, taps_value], axis=1)

    end, tail, wqk_t = project_end(inputs, wq_t, wk_t, w_value)
    tail = along(tail, 1)
    proj = project(inputs, wqk_t, w_value)
    ql, kr, vh, vl, before, own = shard_state(proj, end, tail, taps, pick_kt, bias_t)
    earlier = carried_in(own, False)
    num = inner(ql, kr, vh, vl)
    features = query_features(ql, pick_q, pick_qt, bias, bias_t)
    outputs, dh, dl, grads, own_grad = forward(features, num, before, earlier, out_grad, out_gain.reshape(1, 512))
    after = carried_in(own_grad, True)
    gq, gk, gv = backward(ql, kr, vh, vl, dh, dl, before, earlier, pick_q, bias, back_q)
    rest = (kr, vh, vl, grads, after, gq, gk, gv, pick_k, bias, back_k)
    ga, halo = later(0, 1, *rest)
    halo = along(halo, -1)
    gb, _ = later(1, CHUNKS, *rest)
    side_y = (lax.axis_index("tp") % 2).astype(jnp.int32).reshape(1)
    by_z, keep, send, dt = input_products(side_y, ga, gb, halo, taps, w_value, wqk_t)
    mine, *rest = weight_parts(dt, inputs)
    parts = [mine, *(to_x(part, dx) for dx, part in enumerate(rest, 1))]
    own, came = reduce_weight_grad(parts)
    grad_query, grad_key, grad_value = finish_weight_grad(own, came)
    input_grad = reduce_input_grad(side_y, by_z, keep, send, parts[1:], (grad_query,))
    return (outputs, input_grad, grad_query.T, grad_key.T, grad_value)


def solution(mesh):
    return jax.shard_map(
        local,
        mesh=mesh,
        in_specs=(
            P("seq", None),
            P(None, "tp"),
            P(None, "tp"),
            P(None, "tp"),
            P(None, "tp"),
            P(None, "tp"),
            P(None, "tp"),
            P("tp"),
            P("seq", "tp"),
        ),
        out_specs=(P("seq", "tp"), P("seq", "tp"), P("seq", "tp"), P("seq", "tp"), P("seq", "tp")),
        check_vma=False,
    )
```
